32 devices in a mesh: az: 2 (over y), ax: 16 (over z, x, core).
Axes of the slice: x: 2, y: 2, z: 4, core: 2. Of those that a mesh axis runs over, the one named last changes fastest.
Arguments:
- density: float32 [128, 32, 512], P('ax', 'az'), may hold values from 0.1 to 2
- courant_r: bfloat16 [128, 32, 512], P('ax', 'az'), may hold values from -0.19921875 to 0.19921875
- courant_t: bfloat16 [128, 32, 512], P('ax', 'az'), may hold values from -0.19921875 to 0.19921875
- courant_z: bfloat16 [128, 32, 512], P('ax', 'az'), may hold values from -0.19921875 to 0.19921875
- ionization: bfloat16 [128, 32, 512], P('ax', 'az'), may hold values from 0.0099487305 to 0.19921875
- send_block: int32 [2, 256, 2], P('az', 'ax'), may hold values from 0 to 16, as said below
- recv_slot: int32 [2, 384], P('az', 'ax'), may hold values from 0 to 31, as said below
Outputs:
- evolved: float32 [128, 32, 512], P('ax', 'az')
- fine_patches: float32 [2, 384, 8, 16, 256], P('az', 'ax')
The draws below stay inside these ranges and needn't reach their ends.
Inputs may be any that keep to these rules, and one draw needn't show every extreme that they name: `send_block`: an entry is the local id (block_z * 8 + block_t * 4 + block_r) of a coarse block of the source device, with block_r 0 or 1, or 16 for an empty slot. Each (source, destination) pair carries 0 or exactly 2 blocks; the sources of one sector lie within 12 cyclically consecutive slabs. `recv_slot`: each owner's 24 patches name distinct non-empty slots of the blocks sent to that owner, as source * 2 + slot; every non-empty slot is named once.
All inputs are finite; a program needn't handle non-finite values.
Results may differ from the reference program's by a relative error of at most 0.0015.
Values may be sent and summed in bfloat16 or wider, within the bound.
No kernel may reach another device: no remote copies, remote signals or barrier semaphores. Data moves between devices by JAX's collectives and lax.ppermute only.
A program may use at most 128 MiB of HBM per device.

```python
import math
import jax
import jax.numpy as jnp
from jax import lax

NR = 512
TL = 16
ZL = 8
BZ = 4
BT = 8
BR = 128
PD = 24
CAP = 2
HEAD_SLABS = 12
NZ = 128
NTH = 32
N_AZ = 2
N_AX = 16


def patch_plan(key):
    folded = jax.random.fold_in(key, 11)
    subkeys = jax.random.split(folded, 4)
    head_slab = jax.random.randint(subkeys[0], (N_AZ,), 0, N_AX)
    head_slab = head_slab.at[0].set(N_AX - 1)
    plan_shape = (N_AZ, N_AX, PD)
    blocks_t = TL // BT
    blocks_r = NR // BR
    block_z = jax.random.randint(subkeys[1], plan_shape, 0, ZL // BZ)
    block_t = jax.random.randint(subkeys[2], plan_shape, 0, blocks_t)
    block_r = jax.random.randint(subkeys[3], plan_shape, 0, 2)
    block_id = block_z * (blocks_t * blocks_r) + block_t * blocks_r + block_r
    block_id = block_id.at[0, 0, 0].set(0)
    owner_slab = jnp.arange(N_AX, dtype=jnp.int32)[None, :, None]
    patch_index = jnp.arange(PD, dtype=jnp.int32)[None, None, :]
    source_slab = (head_slab[:, None, None] + (owner_slab + patch_index // CAP) % HEAD_SLABS) % N_AX
    slot_index = patch_index % CAP
    return (block_id, source_slab, slot_index)


def draw_send_block(key, part):
    block_id, source_slab, slot_index = patch_plan(key)
    plan_shape = (N_AZ, N_AX, PD)
    block_total = ZL // BZ * (TL // BT) * (NR // BR)
    sector_index = jnp.broadcast_to(jnp.arange(N_AZ, dtype=jnp.int32)[:, None, None], plan_shape)
    owner_slab = jnp.broadcast_to(jnp.arange(N_AX, dtype=jnp.int32)[None, :, None], plan_shape)
    source_full = jnp.broadcast_to(source_slab, plan_shape)
    slot_full = jnp.broadcast_to(slot_index, plan_shape)
    send_table = jnp.full((N_AZ, N_AX, N_AX, CAP), block_total, jnp.int32)
    send_table = send_table.at[sector_index, source_full, owner_slab, slot_full].set(block_id.astype(jnp.int32))
    return send_table.reshape(N_AZ, N_AX * N_AX, CAP)


def draw_recv_slot(key, part):
    block_id, source_slab, slot_index = patch_plan(key)
    plan_shape = (N_AZ, N_AX, PD)
    codes = jnp.broadcast_to(source_slab * CAP + slot_index, plan_shape)
    return codes.reshape(N_AZ, N_AX * PD).astype(jnp.int32)


def levels(own_key, shape, cuts, smallest, largest):
    def one(position, blocks):
        draws = jax.random.uniform(jax.random.fold_in(jax.random.fold_in(own_key, 6), position), (blocks,), jnp.float32, smallest / len(cuts), largest / len(cuts))
        return jnp.repeat(jnp.exp(draws), shape[position] // blocks).reshape((-1,) + (1,) * (len(shape) - position - 1))

    gain = one(*cuts[0])
    for cut in cuts[1:]:
        gain = gain * one(*cut)
    return gain


def setup_inputs(seed: int = 0) -> dict:
    key_list = jax.random.split(jax.random.key(seed), 8)
    return {
        "density": jnp.clip(jnp.exp(math.log(2.0) - 2.9957323 * jax.random.uniform(key_list[0], (NZ, NTH, NR), jnp.float32) ** levels(key_list[0], (NZ, NTH, NR), ((0, 16), (1, 2)), -0.2, 0.2)), 0.1, 2.0),
        "courant_r": jnp.clip(jax.random.uniform(key_list[1], (NZ, NTH, NR), jnp.float32, -0.19921875, 0.19921875) * levels(key_list[1], (NZ, NTH, NR), ((0, 16), (1, 2)), -0.4, 0.0), -0.19921875, 0.19921875).astype(jnp.bfloat16),
        "courant_t": jnp.clip(jax.random.uniform(key_list[2], (NZ, NTH, NR), jnp.float32, -0.19921875, 0.19921875) * levels(key_list[2], (NZ, NTH, NR), ((0, 16), (1, 2)), -0.4, 0.0), -0.19921875, 0.19921875).astype(jnp.bfloat16),
        "courant_z": jnp.clip(jax.random.uniform(key_list[3], (NZ, NTH, NR), jnp.float32, -0.19921875, 0.19921875) * levels(key_list[3], (NZ, NTH, NR), ((0, 16), (1, 2)), -0.4, 0.0), -0.19921875, 0.19921875).astype(jnp.bfloat16),
        "ionization": jnp.clip(jnp.exp(math.log(0.19921875) - 2.9969585 * jax.random.uniform(key_list[4], (NZ, NTH, NR), jnp.float32) ** levels(key_list[4], (NZ, NTH, NR), ((0, 16), (1, 2)), -0.2, 0.2)), 0.0099487305, 0.19921875).astype(jnp.bfloat16),
        "send_block": draw_send_block(jax.random.fold_in(key_list[7], 71), 0),
        "recv_slot": draw_recv_slot(jax.random.fold_in(key_list[7], 71), 0),
    }


diffusion_number = 0.05


def upwind_change(values, courant, axis_dim):
    length = values.shape[axis_dim]
    slopes = 0.5 * (lax.slice_in_dim(values, 2, length, axis=axis_dim) - lax.slice_in_dim(values, 0, length - 2, axis=axis_dim))
    centre = lax.slice_in_dim(values, 1, length - 1, axis=axis_dim)
    face_count = length - 3
    upwind_left = lax.slice_in_dim(centre, 0, face_count, axis=axis_dim) + 0.5 * lax.slice_in_dim(slopes, 0, face_count, axis=axis_dim)
    upwind_right = lax.slice_in_dim(centre, 1, face_count + 1, axis=axis_dim) - 0.5 * lax.slice_in_dim(slopes, 1, face_count + 1, axis=axis_dim)
    courant_f = courant.astype(jnp.float32)
    face_flux = jnp.maximum(courant_f, 0.0) * upwind_left + jnp.minimum(courant_f, 0.0) * upwind_right
    return lax.slice_in_dim(face_flux, 1, face_count, axis=axis_dim) - lax.slice_in_dim(face_flux, 0, face_count - 1, axis=axis_dim)


def section_rate(padded, across, radial_c, azim_c, axial_c, source):
    cells = padded[2:-2, 2:-2, :]
    azimuthal = upwind_change(padded[2:-2, :, :], azim_c, 1)
    axial_change = upwind_change(padded[:, 2:-2, :], axial_c, 0)
    axial_lap = padded[3:-1, 2:-2, :] + padded[1:-3, 2:-2, :] - 2.0 * cells
    radial_n = cells.shape[2]
    zero_col = jnp.zeros(cells.shape[:2] + (1,), jnp.float32)
    extended = jnp.concatenate([across[:, :, None], cells, zero_col, zero_col], axis=2)
    slopes = 0.5 * (extended[:, :, 2:] - extended[:, :, :-2])
    upwind_left = cells + 0.5 * slopes[:, :, :-1]
    upwind_right = extended[:, :, 2:radial_n + 2] - 0.5 * slopes[:, :, 1:]
    courant_f = radial_c.astype(jnp.float32)
    face_flux = jnp.maximum(courant_f, 0.0) * upwind_left + jnp.minimum(courant_f, 0.0) * upwind_right
    radial_index = jnp.arange(radial_n, dtype=jnp.float32)
    face_area = jnp.where(radial_index < radial_n - 1, radial_index + 1.0, 0.0)
    radius = radial_index + 0.5
    carried = face_area * (diffusion_number * (extended[:, :, 2:radial_n + 2] - cells) - face_flux)
    before = jnp.concatenate([zero_col, carried[:, :, :-1]], axis=2)
    radial = (carried - before) / radius
    return radial - azimuthal - axial_change + diffusion_number * axial_lap + source.astype(jnp.float32) * cells


def interp_matrix(coarse_count):
    fine_index = jnp.arange(2 * coarse_count, dtype=jnp.int32)
    parent = fine_index // 2
    neighbour = jnp.where(fine_index % 2 == 0, jnp.maximum(parent - 1, 0), jnp.minimum(parent + 1, coarse_count - 1))
    columns = jnp.arange(coarse_count, dtype=jnp.int32)
    matrix = 0.75 * (parent[:, None] == columns[None, :]).astype(jnp.float32)
    return matrix + 0.25 * (neighbour[:, None] == columns[None, :]).astype(jnp.float32)


def prolong(blocks):
    spread = jnp.einsum('pztr,Rr->pztR', blocks, interp_matrix(blocks.shape[3]), precision=lax.Precision.HIGHEST)
    spread = jnp.einsum('pztR,Tt->pzTR', spread, interp_matrix(blocks.shape[2]), precision=lax.Precision.HIGHEST)
    return jnp.einsum('pzTR,Zz->pZTR', spread, interp_matrix(blocks.shape[1]), precision=lax.Precision.HIGHEST)


def reference(density, courant_r, courant_t, courant_z, ionization, send_block, recv_slot):
    rows_z, cells_t, cells_r = density.shape
    azim_pad = jnp.concatenate([courant_t[:, -1:], courant_t], axis=1)
    axial_pad = jnp.concatenate([jnp.zeros_like(courant_z[:1]), courant_z], axis=0)

    def full_rate(values):
        wrapped = jnp.concatenate([values[:, -2:], values, values[:, :2]], axis=1)
        padded = jnp.pad(wrapped, ((2, 2), (0, 0), (0, 0)))
        across = jnp.roll(values[:, :, 0], -(cells_t // 2), axis=1)

        def slab_rate(first_row):
            return section_rate(
                lax.dynamic_slice_in_dim(padded, first_row, ZL + 4, 0),
                lax.dynamic_slice_in_dim(across, first_row, ZL, 0),
                lax.dynamic_slice_in_dim(courant_r, first_row, ZL, 0),
                lax.dynamic_slice_in_dim(azim_pad, first_row, ZL, 0),
                lax.dynamic_slice_in_dim(axial_pad, first_row, ZL + 1, 0),
                lax.dynamic_slice_in_dim(ionization, first_row, ZL, 0))

        starts = jnp.arange(N_AX, dtype=jnp.int32) * ZL
        return lax.map(slab_rate, starts).reshape(rows_z, cells_t, cells_r)

    section_one = density + full_rate(density)
    evolved = 0.5 * (density + section_one + full_rate(section_one))
    blocks_z = ZL // BZ
    blocks_t = TL // BT
    blocks_r = NR // BR
    block_total = blocks_z * blocks_t * blocks_r

    def locate(flat_index):
        sector = flat_index // (N_AX * PD)
        within = flat_index % (N_AX * PD)
        owner_slab = within // PD
        slot_code = recv_slot[sector, within]
        source_slab = slot_code // CAP
        slot_index = slot_code % CAP
        block_id = send_block[sector, source_slab * N_AX + owner_slab, slot_index]
        is_valid = (block_id < block_total).astype(jnp.float32)
        clipped = jnp.minimum(block_id, block_total - 1)
        start_z = (source_slab * ZL + (clipped // (blocks_t * blocks_r)) * BZ).astype(jnp.int32)
        start_t = (sector * TL + ((clipped // blocks_r) % blocks_t) * BT).astype(jnp.int32)
        start_r = ((clipped % blocks_r) * BR).astype(jnp.int32)
        return lax.dynamic_slice(evolved, (start_z, start_t, start_r), (BZ, BT, BR)) * is_valid

    flat_all = jnp.arange(N_AZ * N_AX * PD, dtype=jnp.int32)
    blocks = jax.vmap(locate)(flat_all)
    fine_patches = prolong(blocks).reshape(N_AZ, N_AX * PD, 2 * BZ, 2 * BT, 2 * BR)
    return evolved, fine_patches
```

```python
import functools

import jax
import jax.numpy as jnp
import numpy as np
from jax import lax
from jax.experimental import pallas as pl
from jax.experimental.pallas import tpu as pltpu
from jax.sharding import PartitionSpec as P

BZ = 4
BT = 8
BR = 128
CAP = 2
F32 = jnp.float32
BF16 = jnp.bfloat16
DIFFUSION = 0.05
VMEM_LIMIT = 24 * 1024 * 1024

BLOCK_ROWS = BZ * BT
MEAN_ROW = CAP * BLOCK_ROWS
CHUNK_ROWS = MEAN_ROW + 8


def pack_sector(values, courant_t, out_ref):
    rows_z, cells_t, cells_r = values.shape
    row = lax.broadcasted_iota(jnp.int32, (8, cells_r), 0)
    lane = lax.broadcasted_iota(jnp.int32, (cells_t, 128), 1)
    inner = jnp.zeros((cells_t, 128), F32)
    tiles = []
    for k in range(rows_z):
        tile = jnp.where(row < 2, values[k, 0:8, :], values[k, cells_t - 8 :, :])
        if courant_t is not None:
            face = courant_t[k].astype(F32)[cells_t - 8 :, :]
            tile = jnp.where(row == 5, pltpu.roll(face, 6, 0), tile)
        tiles.append(tile)
        inner = jnp.where(lane == k, values[k, :, 0:1], inner)
    for pair in range(rows_z // 2):
        out_ref[pair] = jnp.concatenate(tiles[2 * pair : 2 * pair + 2], axis=0).astype(BF16)
    rounded = inner.astype(BF16)
    out_ref[rows_z // 2, :, 0:128] = rounded
    out_ref[rows_z // 2, :, 128:256] = (inner - rounded.astype(F32)).astype(BF16)
    out_ref[rows_z // 2, :, 256:] = jnp.zeros((cells_t, cells_r - 256), BF16)


def pack_slab(values, courant_z, even_ref, odd_ref):
    rows_z = values.shape[0]
    parity = lax.rem(lax.axis_index("ax"), 2)
    first_even = jnp.where(parity == 0, rows_z - 2, 0)
    first_odd = jnp.where(parity == 0, 0, rows_z - 2)
    for out_ref, first in ((even_ref, first_even), (odd_ref, first_odd)):
        for r in range(2):
            out_ref[r] = values[first + r].astype(BF16)
        if courant_z is not None:
            out_ref[2] = courant_z[rows_z - 1]


def first_messages(density, courant_t, courant_z, sector_ref, even_ref, odd_ref):
    pack_sector(density, courant_t, sector_ref)
    pack_slab(density, courant_z, even_ref, odd_ref)


def rates(values, sector, slab, faces_below, courants, ionization):
    rows_z, cells_t, cells_r = values.shape
    left, right, across = sector
    even_msg, odd_msg = slab
    left_faces, even_faces, odd_faces = faces_below
    courant_r, courant_t, courant_z = courants
    me = lax.axis_index("ax")
    is_even = lax.rem(me, 2) == 0
    has_below = me > 0
    has_above = me < lax.axis_size("ax") - 1
    zero = jnp.zeros((cells_t, cells_r), F32)

    def below(even, odd):
        return jnp.where(has_below, jnp.where(is_even, odd, even).astype(F32), zero)

    def above(even, odd):
        return jnp.where(has_above, jnp.where(is_even, even, odd).astype(F32), zero)

    def row_at(k):
        if k < 0:
            return below(even_msg[k + 2], odd_msg[k + 2])
        if k >= rows_z:
            return above(even_msg[k - rows_z], odd_msg[k - rows_z])
        return values[k]

    lane = lax.broadcasted_iota(jnp.int32, (cells_t, cells_r), 1)
    index = lane.astype(F32)
    area = jnp.where(lane < cells_r - 1, index + 1.0, 0.0)
    inverse_radius = 1.0 / (index + 0.5)
    inner = across[rows_z // 2, :, 0:128].astype(F32) + across[rows_z // 2, :, 128:256].astype(F32)
    halo_row = lax.broadcasted_iota(jnp.int32, (8, cells_r), 0)

    def tile_of(msg, k):
        return msg[k // 2].astype(F32)[(k % 2) * 8 : (k % 2) * 8 + 8, :]

    def axial_flux(courant, back, here, up, up_two):
        low = here + 0.25 * (up - back)
        high = up - 0.25 * (up_two - here)
        return courant * jnp.where(courant > 0.0, low, high)

    flux_z = axial_flux(
        below(even_faces[2], odd_faces[2]), row_at(-2), row_at(-1), row_at(0), row_at(1)
    )
    for k in range(rows_z):
        here, back, up = row_at(k), row_at(k - 1), row_at(k + 1)
        next_flux = axial_flux(courant_z[k].astype(F32), back, here, up, row_at(k + 2))
        rate = (
            DIFFUSION * (up - 2.0 * here + back)
            + ionization[k].astype(F32) * here
            - (next_flux - flux_z)
        )
        flux_z = next_flux
        halo = tile_of(left, k)
        if right is not left:
            halo = jnp.where(halo_row < 4, tile_of(right, k), halo)
        face_halo = pltpu.roll(tile_of(left_faces, k), 2, 0)
        ring = jnp.concatenate([halo, here], axis=0)
        rows = cells_t + 8
        courant = jnp.concatenate([face_halo, courant_t[k].astype(F32)], axis=0)
        quarter = 0.25 * (pltpu.roll(ring, rows - 1, 0) - pltpu.roll(ring, 1, 0))
        flux = courant * jnp.where(courant > 0.0, ring + quarter, pltpu.roll(ring - quarter, rows - 1, 0))
        rate = rate - (flux - pltpu.roll(flux, 1, 0))[8:, :]
        inward = jnp.where(lane == 0, inner[:, k : k + 1], pltpu.roll(here, 1, 1))
        outward = jnp.where(lane == cells_r - 1, 0.0, pltpu.roll(here, cells_r - 1, 1))
        quarter = 0.25 * (outward - inward)
        courant = courant_r[k].astype(F32)
        flux = courant * jnp.where(
            courant > 0.0, here + quarter, pltpu.roll(here - quarter, cells_r - 1, 1)
        )
        carried = area * (DIFFUSION * (outward - here) - flux)
        yield rate + (carried - pltpu.roll(carried, 1, 1)) * inverse_radius


def first_stage(count, *refs):
    density, courant_r, courant_t, courant_z, ionization, even, odd = refs[:7]
    sector = refs[7 : 7 + count]
    section, sector_out, even_out, odd_out = refs[7 + count :]
    left, right, across = sector if count == 3 else sector * 3
    steps = rates(
        density, (left, right, across), (even, odd), (left, even, odd), (courant_r, courant_t, courant_z), ionization
    )
    for k, rate in enumerate(steps):
        section[k] = density[k] + rate
    pack_sector(section, None, sector_out)
    pack_slab(section, None, even_out, odd_out)


def second_stage(count, *refs):
    wanted, density, section, courant_r, courant_t, courant_z, ionization = refs[:7]
    left_faces, even_faces, odd_faces, even, odd = refs[7:12]
    sector = refs[12 : 12 + count]
    evolved, outgoing, table, means = refs[12 + count :]
    left, right, across = sector if count == 3 else sector * 3
    steps = rates(
        section,
        (left, right, across),
        (even, odd),
        (left_faces, even_faces, odd_faces),
        (courant_r, courant_t, courant_z),
        ionization,
    )
    for k, rate in enumerate(steps):
        evolved[k] = 0.5 * (density[k] + section[k] + rate)
    rows_z, cells_t, cells_r = evolved.shape
    blocks_t, blocks_r = cells_t // BT, cells_r // BR
    total = rows_z // BZ * blocks_t * blocks_r
    for block in range(total):
        z = block // (blocks_t * blocks_r) * BZ
        t = block // blocks_r % blocks_t * BT
        r = block % blocks_r * BR
        tiles = [evolved[z + i, t : t + BT, r : r + BR] for i in range(BZ)]
        mean = jnp.mean(sum(tiles), axis=0, keepdims=True) * (1.0 / BZ)
        mean = jnp.broadcast_to(mean.astype(BF16).astype(F32), (BT, BR))
        means[block] = mean
        table[block] = jnp.concatenate([tile - mean for tile in tiles], axis=0).astype(BF16)
    means[total] = jnp.zeros((BT, BR), F32)
    table[total] = jnp.zeros((BLOCK_ROWS, BR), BF16)
    row = lax.broadcasted_iota(jnp.int32, (8, BR), 0)
    for owner in range(outgoing.shape[0]):
        mean_rows = jnp.zeros((8, BR), F32)
        for slot in range(CAP):
            block = wanted[0, owner, slot]
            outgoing[owner, slot * BLOCK_ROWS : (slot + 1) * BLOCK_ROWS, :] = table[block]
            mean_rows = jnp.where(row == slot, means[block], mean_rows)
        outgoing[owner, MEAN_ROW:, :] = mean_rows.astype(BF16)


def prolong_patches(slots, arrived, radial_matrix, tile_matrix, patches, spread, fine, sems):
    sources = arrived.shape[0]
    for source in range(sources):
        spread[source] = jnp.dot(arrived[source], radial_matrix[...], preferred_element_type=F32)
    copies = []
    for p in range(fine.shape[0]):
        code = slots[0, p]
        source, slot = lax.shift_right_logical(code, 1), lax.bitwise_and(code, 1)
        first = pl.multiple_of(slot * BLOCK_ROWS, BLOCK_ROWS)
        coarse = spread[source, pl.ds(first, BLOCK_ROWS), :] + spread[source, pl.ds(MEAN_ROW + slot, 1), :]
        high = coarse.astype(BF16)
        low = (coarse - high.astype(F32)).astype(BF16)
        fine[p] = jnp.dot(
            tile_matrix[...], jnp.concatenate([high, low], axis=0), preferred_element_type=F32
        )
        copy = pltpu.make_async_copy(fine.at[p], patches.at[p], sems.at[p])
        copy.start()
        copies.append(copy)
    for copy in copies:
        copy.wait()


def interp_matrix(coarse_count):
    matrix = np.zeros((2 * coarse_count, coarse_count), np.float32)
    for m in range(coarse_count):
        matrix[2 * m, m] += 0.75
        matrix[2 * m, max(m - 1, 0)] += 0.25
        matrix[2 * m + 1, m] += 0.75
        matrix[2 * m + 1, min(m + 1, coarse_count - 1)] += 0.25
    return matrix


def in_vmem(count):
    return [pl.BlockSpec(memory_space=pltpu.VMEM)] * count


def in_smem(count):
    return [pl.BlockSpec(memory_space=pltpu.SMEM)] * count


PARAMS = pltpu.CompilerParams(vmem_limit_bytes=VMEM_LIMIT)


def local(density, courant_r, courant_t, courant_z, ionization, send_block, recv_slot):
    rows_z, cells_t, cells_r = density.shape
    ax_count = lax.axis_size("ax")
    az_count = lax.axis_size("az")
    owned = recv_slot.shape[1]

    def flat(a, i):
        return a * ax_count + i

    even_pairs = [(i, i ^ 1) for i in range(ax_count)]
    odd_pairs = []
    for a in range(az_count):
        odd_pairs += [(flat(a, i), flat(a, ((i - 1) ^ 1) + 1)) for i in range(1, ax_count - 1)]
        odd_pairs += [(flat(a, i), flat(a ^ 1, i)) for i in (0, ax_count - 1)]

    def by(steps):
        return [(a, (a + steps) % az_count) for a in range(az_count)]

    def exchange(sector, even, odd):
        if az_count == 2:
            sectors = [lax.ppermute(sector, "az", by(1))]
        else:
            sectors = [lax.ppermute(sector, "az", by(s)) for s in (1, az_count - 1, az_count // 2)]
        return sectors, lax.ppermute(even, "ax", even_pairs), lax.ppermute(odd, ("az", "ax"), odd_pairs)

    sector_shape = jax.ShapeDtypeStruct((rows_z // 2 + 1, cells_t, cells_r), BF16)
    slab_three = jax.ShapeDtypeStruct((3, cells_t, cells_r), BF16)
    slab_two = jax.ShapeDtypeStruct((2, cells_t, cells_r), BF16)
    field = jax.ShapeDtypeStruct(density.shape, F32)

    sector, even, odd = pl.pallas_call(
        first_messages,
        out_shape=(sector_shape, slab_three, slab_three),
        in_specs=in_vmem(3),
        out_specs=tuple(in_vmem(3)),
        compiler_params=PARAMS,
        name="first_messages",
    )(density, courant_t, courant_z)
    sectors, even, odd = exchange(sector, even, odd)
    count = len(sectors)

    section, sector, even_two, odd_two = pl.pallas_call(
        functools.partial(first_stage, count),
        out_shape=(field, sector_shape, slab_two, slab_two),
        in_specs=in_vmem(7 + count),
        out_specs=tuple(in_vmem(4)),
        compiler_params=PARAMS,
        name="first_stage",
    )(density, courant_r, courant_t, courant_z, ionization, even, odd, *sectors)
    sectors_two, even_two, odd_two = exchange(sector, even_two, odd_two)

    blocks = rows_z // BZ * (cells_t // BT) * (cells_r // BR)
    evolved, outgoing = pl.pallas_call(
        functools.partial(second_stage, count),
        out_shape=(field, jax.ShapeDtypeStruct((ax_count, CHUNK_ROWS, BR), BF16)),
        in_specs=in_smem(1) + in_vmem(11 + count),
        out_specs=tuple(in_vmem(2)),
        scratch_shapes=[
            pltpu.VMEM((blocks + 1, BLOCK_ROWS, BR), BF16),
            pltpu.VMEM((blocks + 1, BT, BR), F32),
        ],
        compiler_params=PARAMS,
        name="second_stage",
    )(
        send_block, density, section, courant_r, courant_t, courant_z, ionization,
        sectors[0], even, odd, even_two, odd_two, *sectors_two,
    )

    arrived = lax.all_to_all(outgoing, "ax", split_axis=0, concat_axis=0, tiled=True)

    tile_matrix = np.kron(interp_matrix(BZ), interp_matrix(BT))
    tile_matrix = jnp.asarray(np.concatenate([tile_matrix, tile_matrix], axis=1), BF16)
    radial_matrix = jnp.asarray(interp_matrix(BR).T, BF16)
    fine_rows = 4 * BZ * BT
    patches = pl.pallas_call(
        prolong_patches,
        out_shape=jax.ShapeDtypeStruct((owned, fine_rows, 2 * BR), F32),
        in_specs=in_smem(1) + in_vmem(3),
        out_specs=pl.BlockSpec(memory_space=pl.ANY),
        scratch_shapes=[
            pltpu.VMEM((ax_count, CHUNK_ROWS, 2 * BR), F32),
            pltpu.VMEM((owned, fine_rows, 2 * BR), F32),
            pltpu.SemaphoreType.DMA((owned,)),
        ],
        compiler_params=PARAMS,
        name="prolong_patches",
    )(recv_slot, arrived, radial_matrix, tile_matrix)
    return (evolved, patches.reshape(1, owned, 2 * BZ, 2 * BT, 2 * BR))


def solution(mesh):
    in_specs = (
        P("ax", "az", None),
        P("ax", "az", None),
        P("ax", "az", None),
        P("ax", "az", None),
        P("ax", "az", None),
        P("az", "ax", None),
        P("az", "ax"),
    )
    out_specs = (P("ax", "az", None), P("az", "ax", None, None, None))
    return jax.shard_map(local, mesh=mesh, in_specs=in_specs, out_specs=out_specs, check_vma=False)
```

```python
import functools

import jax
import jax.numpy as jnp
import numpy as np
from jax import lax
from jax.experimental import pallas as pl
from jax.experimental.pallas import tpu as pltpu
from jax.sharding import PartitionSpec as P

BZ = 4
BT = 8
BR = 128
CAP = 2
HEAD_R = 2
GROUP = 4
F32 = jnp.float32
BF16 = jnp.bfloat16
DIFFUSION = 0.05
VMEM_LIMIT = 24 * 1024 * 1024

BLOCK_ROWS = BZ * BT
MEAN_ROW = CAP * BLOCK_ROWS
CHUNK_ROWS = MEAN_ROW + 8


def pack_sector(values, courant_t, out_ref):
    rows_z, cells_t, cells_r = values.shape
    row = lax.broadcasted_iota(jnp.int32, (8, cells_r), 0)
    lane = lax.broadcasted_iota(jnp.int32, (cells_t, 128), 1)
    inner = jnp.zeros((cells_t, 128), F32)
    tiles = []
    for k in range(rows_z):
        tile = jnp.where(row < 2, values[k, 0:8, :], values[k, cells_t - 8 :, :])
        if courant_t is not None:
            face = courant_t[k].astype(F32)[cells_t - 8 :, :]
            tile = jnp.where(row == 5, pltpu.roll(face, 6, 0), tile)
        tiles.append(tile)
        inner = jnp.where(lane == k, values[k, :, 0:1], inner)
    for pair in range(rows_z // 2):
        out_ref[pair] = jnp.concatenate(tiles[2 * pair : 2 * pair + 2], axis=0).astype(BF16)
    rounded = inner.astype(BF16)
    out_ref[rows_z // 2, :, 0:128] = rounded
    out_ref[rows_z // 2, :, 128:256] = (inner - rounded.astype(F32)).astype(BF16)
    out_ref[rows_z // 2, :, 256:] = jnp.zeros((cells_t, cells_r - 256), BF16)


def pack_slab(values, courant_z, even_ref, odd_ref):
    rows_z = values.shape[0]
    parity = lax.rem(lax.axis_index("ax"), 2)
    first_even = jnp.where(parity == 0, rows_z - 2, 0)
    first_odd = jnp.where(parity == 0, 0, rows_z - 2)
    for out_ref, first in ((even_ref, first_even), (odd_ref, first_odd)):
        for r in range(2):
            out_ref[r] = values[first + r].astype(BF16)
        if courant_z is not None:
            out_ref[2] = courant_z[rows_z - 1]


def first_messages(count, *refs):
    given, held = refs[:count], refs[count : 2 * count]
    sector_out, even_out, odd_out, sems = refs[2 * count :]
    copies = [pltpu.make_async_copy(given[i], held[i], sems.at[i]) for i in range(count)]
    for copy in copies:
        copy.start()
    density, courant_t, courant_z = held[:3]
    for copy in copies[:3]:
        copy.wait()
    pack_slab(density, courant_z, even_out, odd_out)
    pack_sector(density, courant_t, sector_out)
    for copy in copies[3:]:
        copy.wait()


def rates(values, sector, slab, faces_below, courants, ionization):
    rows_z, cells_t, cells_r = values.shape
    left, right, across = sector
    even_msg, odd_msg = slab
    left_faces, even_faces, odd_faces = faces_below
    courant_r, courant_t, courant_z = courants
    me = lax.axis_index("ax")
    is_even = lax.rem(me, 2) == 0
    has_below = me > 0
    has_above = me < lax.axis_size("ax") - 1
    zero = jnp.zeros((cells_t, cells_r), F32)

    def below(even, odd):
        return jnp.where(has_below, jnp.where(is_even, odd, even).astype(F32), zero)

    def above(even, odd):
        return jnp.where(has_above, jnp.where(is_even, even, odd).astype(F32), zero)

    def row_at(k):
        if k < 0:
            return below(even_msg[k + 2], odd_msg[k + 2])
        if k >= rows_z:
            return above(even_msg[k - rows_z], odd_msg[k - rows_z])
        return values[k]

    lane = lax.broadcasted_iota(jnp.int32, (cells_t, cells_r), 1)
    index = lane.astype(F32)
    area = jnp.where(lane < cells_r - 1, index + 1.0, 0.0)
    inverse_radius = 1.0 / (index + 0.5)
    inner = across[rows_z // 2, :, 0:128].astype(F32) + across[rows_z // 2, :, 128:256].astype(F32)
    halo_row = lax.broadcasted_iota(jnp.int32, (8, cells_r), 0)

    def tile_of(msg, k):
        return msg[k // 2].astype(F32)[(k % 2) * 8 : (k % 2) * 8 + 8, :]

    def axial_flux(courant, back, here, up, up_two):
        low = here + 0.25 * (up - back)
        high = up - 0.25 * (up_two - here)
        return courant * jnp.where(courant > 0.0, low, high)

    flux_z = axial_flux(
        below(even_faces[2], odd_faces[2]), row_at(-2), row_at(-1), row_at(0), row_at(1)
    )
    for k in range(rows_z):
        here, back, up = row_at(k), row_at(k - 1), row_at(k + 1)
        next_flux = axial_flux(courant_z[k].astype(F32), back, here, up, row_at(k + 2))
        rate = (
            DIFFUSION * (up - 2.0 * here + back)
            + ionization[k].astype(F32) * here
            - (next_flux - flux_z)
        )
        flux_z = next_flux
        halo = tile_of(left, k)
        if right is not left:
            halo = jnp.where(halo_row < 4, tile_of(right, k), halo)
        face_halo = pltpu.roll(tile_of(left_faces, k), 2, 0)
        ring = jnp.concatenate([halo, here], axis=0)
        rows = cells_t + 8
        courant = jnp.concatenate([face_halo, courant_t[k].astype(F32)], axis=0)
        quarter = 0.25 * (pltpu.roll(ring, rows - 1, 0) - pltpu.roll(ring, 1, 0))
        flux = courant * jnp.where(courant > 0.0, ring + quarter, pltpu.roll(ring - quarter, rows - 1, 0))
        rate = rate - (flux - pltpu.roll(flux, 1, 0))[8:, :]
        inward = jnp.where(lane == 0, inner[:, k : k + 1], pltpu.roll(here, 1, 1))
        outward = jnp.where(lane == cells_r - 1, 0.0, pltpu.roll(here, cells_r - 1, 1))
        quarter = 0.25 * (outward - inward)
        courant = courant_r[k].astype(F32)
        flux = courant * jnp.where(
            courant > 0.0, here + quarter, pltpu.roll(here - quarter, cells_r - 1, 1)
        )
        carried = area * (DIFFUSION * (outward - here) - flux)
        yield rate + (carried - pltpu.roll(carried, 1, 1)) * inverse_radius


def first_stage(count, *refs):
    density, courant_r, courant_t, courant_z, ionization, even, odd = refs[:7]
    sector = refs[7 : 7 + count]
    section, sector_out, even_out, odd_out = refs[7 + count :]
    left, right, across = sector if count == 3 else sector * 3
    steps = rates(
        density, (left, right, across), (even, odd), (left, even, odd), (courant_r, courant_t, courant_z), ionization
    )
    for k, rate in enumerate(steps):
        section[k] = density[k] + rate
    pack_sector(section, None, sector_out)
    pack_slab(section, None, even_out, odd_out)


def second_stage(count, *refs):
    wanted_held, density, section, courant_r, courant_t, courant_z, ionization = refs[:7]
    left_faces, even_faces, odd_faces, even, odd = refs[7:12]
    sector = refs[12 : 12 + count]
    evolved, outgoing, table, means, wanted, sem = refs[12 + count :]
    copy = pltpu.make_async_copy(wanted_held, wanted, sem)
    copy.start()
    left, right, across = sector if count == 3 else sector * 3
    steps = rates(
        section,
        (left, right, across),
        (even, odd),
        (left_faces, even_faces, odd_faces),
        (courant_r, courant_t, courant_z),
        ionization,
    )
    for k, rate in enumerate(steps):
        evolved[k] = 0.5 * (density[k] + section[k] + rate)
    rows_z, cells_t, cells_r = evolved.shape
    blocks_t, blocks_r = cells_t // BT, cells_r // BR
    total = rows_z // BZ * blocks_t * blocks_r
    for block in range(total):
        z = block // (blocks_t * blocks_r) * BZ
        t = block // blocks_r % blocks_t * BT
        r = block % blocks_r * BR
        if r >= HEAD_R * BR:
            continue
        tiles = [evolved[z + i, t : t + BT, r : r + BR] for i in range(BZ)]
        mean = jnp.mean(sum(tiles), axis=0, keepdims=True) * (1.0 / BZ)
        mean = jnp.broadcast_to(mean.astype(BF16).astype(F32), (BT, BR))
        means[block] = mean
        table[block] = jnp.concatenate([tile - mean for tile in tiles], axis=0).astype(BF16)
    means[total] = jnp.zeros((BT, BR), F32)
    table[total] = jnp.zeros((BLOCK_ROWS, BR), BF16)
    row = lax.broadcasted_iota(jnp.int32, (8, BR), 0)
    copy.wait()
    for owner in range(outgoing.shape[0]):
        mean_rows = jnp.zeros((8, BR), F32)
        for slot in range(CAP):
            block = wanted[0, slot, owner]
            outgoing[owner, slot * BLOCK_ROWS : (slot + 1) * BLOCK_ROWS, :] = table[block]
            mean_rows = jnp.where(row == slot, means[block], mean_rows)
        outgoing[owner, MEAN_ROW:, :] = mean_rows.astype(BF16)


def prolong_patches(
    slots_held, evolved, arrived, radial_matrix, tile_matrix, evolved_out, patches, spread, fine, slots, sems
):
    codes = pltpu.make_async_copy(slots_held, slots, sems.at[0])
    codes.start()
    copies = [pltpu.make_async_copy(evolved, evolved_out, sems.at[1])]
    copies[0].start()
    for source in range(arrived.shape[0]):
        spread[source] = jnp.dot(arrived[source], radial_matrix[...], preferred_element_type=F32)
    codes.wait()
    owned = fine.shape[0]
    for first in range(0, owned, GROUP):
        size = min(GROUP, owned - first)
        for p in range(first, first + size):
            code = slots[0, p]
            source, slot = lax.shift_right_logical(code, 1), lax.bitwise_and(code, 1)
            row = pl.multiple_of(slot * BLOCK_ROWS, BLOCK_ROWS)
            coarse = spread[source, pl.ds(row, BLOCK_ROWS), :] + spread[source, pl.ds(MEAN_ROW + slot, 1), :]
            high = coarse.astype(BF16)
            low = (coarse - high.astype(F32)).astype(BF16)
            fine[p] = jnp.dot(
                tile_matrix[...], jnp.concatenate([high, low], axis=0), preferred_element_type=F32
            )
        part = pl.ds(first, size)
        copies.append(pltpu.make_async_copy(fine.at[part], patches.at[part], sems.at[len(copies) + 1]))
        copies[-1].start()
    for copy in copies:
        copy.wait()


def interp_matrix(coarse_count):
    matrix = np.zeros((2 * coarse_count, coarse_count), np.float32)
    for m in range(coarse_count):
        matrix[2 * m, m] += 0.75
        matrix[2 * m, max(m - 1, 0)] += 0.25
        matrix[2 * m + 1, m] += 0.75
        matrix[2 * m + 1, min(m + 1, coarse_count - 1)] += 0.25
    return matrix


def in_vmem(count):
    return [pl.BlockSpec(memory_space=pltpu.VMEM)] * count


PARAMS = pltpu.CompilerParams(vmem_limit_bytes=VMEM_LIMIT)


def local(density, courant_r, courant_t, courant_z, ionization, send_block, recv_slot):
    rows_z, cells_t, cells_r = density.shape
    ax_count = lax.axis_size("ax")
    az_count = lax.axis_size("az")
    owned = recv_slot.shape[1]

    def flat(a, i):
        return a * ax_count + i

    even_pairs = [(i, i ^ 1) for i in range(ax_count)]
    odd_pairs = []
    for a in range(az_count):
        odd_pairs += [(flat(a, i), flat(a, ((i - 1) ^ 1) + 1)) for i in range(1, ax_count - 1)]
        odd_pairs += [(flat(a, i), flat(a ^ 1, i)) for i in (0, ax_count - 1)]

    def by(steps):
        return [(a, (a + steps) % az_count) for a in range(az_count)]

    def exchange(sector, even, odd):
        if az_count == 2:
            sectors = [lax.ppermute(sector, "az", by(1))]
        else:
            sectors = [lax.ppermute(sector, "az", by(s)) for s in (1, az_count - 1, az_count // 2)]
        return sectors, lax.ppermute(even, "ax", even_pairs), lax.ppermute(odd, ("az", "ax"), odd_pairs)

    sector_shape = jax.ShapeDtypeStruct((rows_z // 2 + 1, cells_t, cells_r), BF16)
    slab_three = jax.ShapeDtypeStruct((3, cells_t, cells_r), BF16)
    slab_two = jax.ShapeDtypeStruct((2, cells_t, cells_r), BF16)
    field = jax.ShapeDtypeStruct(density.shape, F32)

    given = (
        density, courant_t, courant_z, courant_r, ionization, jnp.transpose(send_block, (0, 2, 1)), recv_slot
    )
    given = tuple(pltpu.with_memory_space_constraint(x, pltpu.HBM) for x in given)
    *held, sector, even, odd = pl.pallas_call(
        functools.partial(first_messages, len(given)),
        out_shape=tuple(jax.ShapeDtypeStruct(x.shape, x.dtype) for x in given)
        + (sector_shape, slab_three, slab_three),
        in_specs=[pl.BlockSpec(memory_space=pltpu.HBM)] * len(given),
        out_specs=tuple(in_vmem(len(given) + 3)),
        scratch_shapes=[pltpu.SemaphoreType.DMA((len(given),))],
        compiler_params=PARAMS,
        name="first_messages",
    )(*given)
    density, courant_t, courant_z, courant_r, ionization, wanted, slots = held
    sectors, even, odd = exchange(sector, even, odd)
    count = len(sectors)

    section, sector, even_two, odd_two = pl.pallas_call(
        functools.partial(first_stage, count),
        out_shape=(field, sector_shape, slab_two, slab_two),
        in_specs=in_vmem(7 + count),
        out_specs=tuple(in_vmem(4)),
        compiler_params=PARAMS,
        name="first_stage",
    )(density, courant_r, courant_t, courant_z, ionization, even, odd, *sectors)
    sectors_two, even_two, odd_two = exchange(sector, even_two, odd_two)

    blocks = rows_z // BZ * (cells_t // BT) * (cells_r // BR)
    evolved, outgoing = pl.pallas_call(
        functools.partial(second_stage, count),
        out_shape=(field, jax.ShapeDtypeStruct((ax_count, CHUNK_ROWS, BR), BF16)),
        in_specs=in_vmem(12 + count),
        out_specs=tuple(in_vmem(2)),
        scratch_shapes=[
            pltpu.VMEM((blocks + 1, BLOCK_ROWS, BR), BF16),
            pltpu.VMEM((blocks + 1, BT, BR), F32),
            pltpu.SMEM(wanted.shape, jnp.int32),
            pltpu.SemaphoreType.DMA,
        ],
        compiler_params=PARAMS,
        name="second_stage",
    )(
        wanted, density, section, courant_r, courant_t, courant_z, ionization,
        sectors[0], even, odd, even_two, odd_two, *sectors_two,
    )

    arrived = lax.all_to_all(outgoing, "ax", split_axis=0, concat_axis=0, tiled=True)

    tile_matrix = np.kron(interp_matrix(BZ), interp_matrix(BT))
    tile_matrix = jnp.asarray(np.concatenate([tile_matrix, tile_matrix], axis=1), BF16)
    radial_matrix = jnp.asarray(interp_matrix(BR).T, BF16)
    fine_rows = 4 * BZ * BT
    evolved, patches = pl.pallas_call(
        prolong_patches,
        out_shape=(field, jax.ShapeDtypeStruct((owned, fine_rows, 2 * BR), F32)),
        in_specs=in_vmem(5),
        out_specs=(pl.BlockSpec(memory_space=pltpu.HBM),) * 2,
        scratch_shapes=[
            pltpu.VMEM((ax_count, CHUNK_ROWS, 2 * BR), F32),
            pltpu.VMEM((owned, fine_rows, 2 * BR), F32),
            pltpu.SMEM(slots.shape, jnp.int32),
            pltpu.SemaphoreType.DMA((-(-owned // GROUP) + 2,)),
        ],
        compiler_params=PARAMS,
        name="prolong_patches",
    )(slots, evolved, arrived, radial_matrix, tile_matrix)
    return (evolved, patches.reshape(1, owned, 2 * BZ, 2 * BT, 2 * BR))


def solution(mesh):
    in_specs = (
        P("ax", "az", None),
        P("ax", "az", None),
        P("ax", "az", None),
        P("ax", "az", None),
        P("ax", "az", None),
        P("az", "ax", None),
        P("az", "ax"),
    )
    out_specs = (P("ax", "az", None), P("az", "ax", None, None, None))
    return jax.shard_map(local, mesh=mesh, in_specs=in_specs, out_specs=out_specs, check_vma=False)
```

```python
import functools

import jax
import jax.numpy as jnp
import numpy as np
from jax import lax
from jax.experimental import pallas as pl
from jax.experimental.pallas import tpu as pltpu
from jax.sharding import PartitionSpec as P

BZ = 4
BT = 8
BR = 128
CAP = 2
HEAD_R = 2
GROUP = 4
F32 = jnp.float32
BF16 = jnp.bfloat16
DIFFUSION = 0.05
VMEM_LIMIT = 24 * 1024 * 1024

BLOCK_ROWS = BZ * BT
MEAN_ROW = CAP * BLOCK_ROWS
CHUNK_ROWS = MEAN_ROW + 8


def pack_sector(values, courant_t, out_ref):
    rows_z, cells_t, cells_r = values.shape
    row = lax.broadcasted_iota(jnp.int32, (8, cells_r), 0)
    lane = lax.broadcasted_iota(jnp.int32, (cells_t, 128), 1)
    inner = jnp.zeros((cells_t, 128), F32)
    ends = []
    for k in range(rows_z):
        ends.append(jnp.where(row < 2, values[k, 0:8, :], values[k, cells_t - 8 :, :]))
        inner = jnp.where(lane == k, values[k, :, 0:1], inner)
    outer = (row < 2) | (row > 5)
    tiles = [
        jnp.where(outer, ends[k], pltpu.roll(ends[k + 1], 4, 0)) for k in range(0, rows_z, 2)
    ]
    faces = jnp.zeros((8, cells_r), F32)
    if courant_t is not None:
        for k in range(rows_z):
            face = courant_t[k].astype(F32)[cells_t - 8 :, :]
            faces = jnp.where(row == k, pltpu.roll(face, (k + 1) % 8, 0), faces)
    tiles.append(faces)
    rounded = inner.astype(BF16).astype(F32)
    rest = inner - rounded
    tiles.append(jnp.concatenate([rounded[:8], rounded[8:], rest[:8], rest[8:]], axis=1))
    for pair in range(len(tiles) // 2):
        out_ref[pair] = jnp.concatenate(tiles[2 * pair : 2 * pair + 2], axis=0).astype(BF16)


def tile_of(msg, index):
    return msg[index // 2].astype(F32)[(index % 2) * 8 : (index % 2) * 8 + 8, :]


def pack_slab(values, courant_z, even_ref, odd_ref):
    rows_z = values.shape[0]
    parity = lax.rem(lax.axis_index("ax"), 2)
    first_even = jnp.where(parity == 0, rows_z - 2, 0)
    first_odd = jnp.where(parity == 0, 0, rows_z - 2)
    for out_ref, first in ((even_ref, first_even), (odd_ref, first_odd)):
        for r in range(2):
            out_ref[r] = values[first + r].astype(BF16)
        if courant_z is not None:
            out_ref[2] = courant_z[rows_z - 1]


def first_messages(count, *refs):
    given, held = refs[:count], refs[count : 2 * count]
    sector_out, even_out, odd_out, sems = refs[2 * count :]
    copies = [pltpu.make_async_copy(given[i], held[i], sems.at[i]) for i in range(count)]
    for copy in copies:
        copy.start()
    density, courant_t, courant_z = held[:3]
    for copy in copies[:3]:
        copy.wait()
    pack_slab(density, courant_z, even_out, odd_out)
    pack_sector(density, courant_t, sector_out)
    for copy in copies[3:]:
        copy.wait()


def axial_flux(courant, back, here, up, up_two):
    low = here + 0.25 * (up - back)
    high = up - 0.25 * (up_two - here)
    return courant * jnp.where(courant > 0.0, low, high)


def inner_rates(values, courant_r, courant_z, ionization):
    rows_z, cells_t, cells_r = values.shape
    zero = jnp.zeros((cells_t, cells_r), F32)

    def row_at(k):
        return values[k] if 0 <= k < rows_z else zero

    lane = lax.broadcasted_iota(jnp.int32, (cells_t, cells_r), 1)
    index = lane.astype(F32)
    area = jnp.where(lane < cells_r - 1, index + 1.0, 0.0)
    inverse_radius = 1.0 / (index + 0.5)
    flux_z = zero
    for k in range(rows_z):
        here, back, up = row_at(k), row_at(k - 1), row_at(k + 1)
        next_flux = zero
        if k < rows_z - 1:
            next_flux = axial_flux(courant_z[k].astype(F32), back, here, up, row_at(k + 2))
        rate = (
            DIFFUSION * (up - 2.0 * here + back)
            + ionization[k].astype(F32) * here
            - (next_flux - flux_z)
        )
        flux_z = next_flux
        inward = jnp.where(lane == 0, 0.0, pltpu.roll(here, 1, 1))
        outward = jnp.where(lane == cells_r - 1, 0.0, pltpu.roll(here, cells_r - 1, 1))
        quarter = 0.25 * (outward - inward)
        courant = courant_r[k].astype(F32)
        flux = courant * jnp.where(
            courant > 0.0, here + quarter, pltpu.roll(here - quarter, cells_r - 1, 1)
        )
        carried = area * (DIFFUSION * (outward - here) - flux)
        yield rate + (carried - pltpu.roll(carried, 1, 1)) * inverse_radius


def outer_rates(values, sector, slab, faces_below, courants):
    rows_z, cells_t, cells_r = values.shape
    left, right, across = sector
    even_msg, odd_msg = slab
    left_faces, even_faces, odd_faces = faces_below
    courant_r, courant_t, courant_z = courants
    me = lax.axis_index("ax")
    is_even = lax.rem(me, 2) == 0
    has_below = me > 0
    has_above = me < lax.axis_size("ax") - 1
    zero = jnp.zeros((cells_t, cells_r), F32)

    def below(even, odd):
        return jnp.where(has_below, jnp.where(is_even, odd, even).astype(F32), zero)

    def above(even, odd):
        return jnp.where(has_above, jnp.where(is_even, even, odd).astype(F32), zero)

    top = rows_z - 1
    below_one, below_two = below(even_msg[1], odd_msg[1]), below(even_msg[0], odd_msg[0])
    above_one, above_two = above(even_msg[0], odd_msg[0]), above(even_msg[1], odd_msg[1])
    first_flux = axial_flux(
        below(even_faces[2], odd_faces[2]), below_two, below_one, values[0], values[1]
    )
    last_flux = axial_flux(
        courant_z[top].astype(F32), values[top - 1], values[top], above_one, above_two
    )
    low_change = -0.25 * jnp.maximum(courant_z[0].astype(F32), 0.0) * below_one
    high_change = -0.25 * jnp.minimum(courant_z[top - 1].astype(F32), 0.0) * above_one
    axial = {
        0: first_flux - low_change + DIFFUSION * below_one,
        1: low_change,
        top - 1: -high_change,
        top: high_change - last_flux + DIFFUSION * above_one,
    }
    halo_row = lax.broadcasted_iota(jnp.int32, (8, cells_r), 0)
    lane = lax.broadcasted_iota(jnp.int32, (cells_t, 128), 1)
    packed = tile_of(across, rows_z // 2 + 1)
    packed = packed[:, 0:256] + packed[:, 256:512]
    inner = jnp.concatenate([packed[:, 0:128], packed[:, 128:256]], axis=0)
    faces = tile_of(left_faces, rows_z // 2)
    rows = cells_t + 8
    for k in range(rows_z):
        here = values[k]
        halo = tile_of(left, k // 2)
        if right is not left:
            beyond = (halo_row < 2) | (halo_row == 4) | (halo_row == 5)
            halo = jnp.where(beyond, tile_of(right, k // 2), halo)
        if k % 2:
            halo = pltpu.roll(halo, 4, 0)
        ring = jnp.concatenate([halo, here], axis=0)
        face_halo = pltpu.roll(faces, 7 - k, 0)
        courant = jnp.concatenate([face_halo, courant_t[k].astype(F32)], axis=0)
        quarter = 0.25 * (pltpu.roll(ring, rows - 1, 0) - pltpu.roll(ring, 1, 0))
        flux = courant * jnp.where(courant > 0.0, ring + quarter, pltpu.roll(ring - quarter, rows - 1, 0))
        rate = (pltpu.roll(flux, 1, 0) - flux)[8:, :]
        if k in axial:
            rate = rate + axial[k]
        change = 0.25 * jnp.maximum(courant_r[k, :, 0:128].astype(F32), 0.0)
        change = change * (pltpu.roll(inner, 128 - k, 1) if k else inner)
        change = jnp.where(lane == 0, change, 0.0)
        change = 2.0 * change - (1.0 / 1.5) * pltpu.roll(change, 1, 1)
        yield jnp.concatenate([rate[:, 0:128] + change, rate[:, 128:]], axis=1)


def first_inner(density, courant_r, courant_z, ionization, partial):
    for k, rate in enumerate(inner_rates(density, courant_r, courant_z, ionization)):
        partial[k] = density[k] + rate


def second_inner(density, section, courant_r, courant_z, ionization, partial):
    for k, rate in enumerate(inner_rates(section, courant_r, courant_z, ionization)):
        partial[k] = 0.5 * (density[k] + section[k] + rate)


def first_stage(count, *refs):
    odd, sector, refs = refs[0], refs[1 : 1 + count], refs[1:]
    even, partial, density, courant_r, courant_t, courant_z = refs[count : count + 6]
    section, sector_out, even_out, odd_out = refs[count + 6 :]
    left, right, across = sector if count == 3 else sector * 3
    steps = outer_rates(
        density, (left, right, across), (even, odd), (left, even, odd), (courant_r, courant_t, courant_z)
    )
    for k, rate in enumerate(steps):
        section[k] = partial[k] + rate
    pack_sector(section, None, sector_out)
    pack_slab(section, None, even_out, odd_out)


def second_stage(count, *refs):
    odd, sector, refs = refs[0], refs[1 : 1 + count], refs[1:]
    even, partial, wanted_held, section, courant_r, courant_t, courant_z = refs[count : count + 7]
    left_faces, even_faces, odd_faces = refs[count + 7 : count + 10]
    evolved, outgoing, table, means, wanted, sem = refs[count + 10 :]
    copy = pltpu.make_async_copy(wanted_held, wanted, sem)
    copy.start()
    left, right, across = sector if count == 3 else sector * 3
    steps = outer_rates(
        section,
        (left, right, across),
        (even, odd),
        (left_faces, even_faces, odd_faces),
        (courant_r, courant_t, courant_z),
    )
    for k, rate in enumerate(steps):
        evolved[k] = partial[k] + 0.5 * rate
    rows_z, cells_t, cells_r = evolved.shape
    blocks_t, blocks_r = cells_t // BT, cells_r // BR
    total = rows_z // BZ * blocks_t * blocks_r
    for block in range(total):
        z = block // (blocks_t * blocks_r) * BZ
        t = block // blocks_r % blocks_t * BT
        r = block % blocks_r * BR
        if r >= HEAD_R * BR:
            continue
        tiles = [evolved[z + i, t : t + BT, r : r + BR] for i in range(BZ)]
        mean = jnp.mean(sum(tiles), axis=0, keepdims=True) * (1.0 / BZ)
        mean = jnp.broadcast_to(mean.astype(BF16).astype(F32), (BT, BR))
        means[block] = mean
        table[block] = jnp.concatenate([tile - mean for tile in tiles], axis=0).astype(BF16)
    means[total] = jnp.zeros((BT, BR), F32)
    table[total] = jnp.zeros((BLOCK_ROWS, BR), BF16)
    row = lax.broadcasted_iota(jnp.int32, (8, BR), 0)
    copy.wait()
    for owner in range(outgoing.shape[0]):
        mean_rows = jnp.zeros((8, BR), F32)
        for slot in range(CAP):
            block = wanted[0, slot, owner]
            outgoing[owner, slot * BLOCK_ROWS : (slot + 1) * BLOCK_ROWS, :] = table[block]
            mean_rows = jnp.where(row == slot, means[block], mean_rows)
        outgoing[owner, MEAN_ROW:, :] = mean_rows.astype(BF16)


def prolong_patches(
    slots_held, evolved, arrived, radial_matrix, tile_matrix, evolved_out, patches, spread, fine, slots, sems
):
    codes = pltpu.make_async_copy(slots_held, slots, sems.at[0])
    codes.start()
    copies = [pltpu.make_async_copy(evolved, evolved_out, sems.at[1])]
    copies[0].start()
    for source in range(arrived.shape[0]):
        spread[source] = jnp.dot(arrived[source], radial_matrix[...], preferred_element_type=F32)
    codes.wait()
    owned = fine.shape[0]
    for first in range(0, owned, GROUP):
        size = min(GROUP, owned - first)
        for p in range(first, first + size):
            code = slots[0, p]
            source, slot = lax.shift_right_logical(code, 1), lax.bitwise_and(code, 1)
            row = pl.multiple_of(slot * BLOCK_ROWS, BLOCK_ROWS)
            coarse = spread[source, pl.ds(row, BLOCK_ROWS), :] + spread[source, pl.ds(MEAN_ROW + slot, 1), :]
            high = coarse.astype(BF16)
            low = (coarse - high.astype(F32)).astype(BF16)
            fine[p] = jnp.dot(
                tile_matrix[...], jnp.concatenate([high, low], axis=0), preferred_element_type=F32
            )
        part = pl.ds(first, size)
        copies.append(pltpu.make_async_copy(fine.at[part], patches.at[part], sems.at[len(copies) + 1]))
        copies[-1].start()
    for copy in copies:
        copy.wait()


def interp_matrix(coarse_count):
    matrix = np.zeros((2 * coarse_count, coarse_count), np.float32)
    for m in range(coarse_count):
        matrix[2 * m, m] += 0.75
        matrix[2 * m, max(m - 1, 0)] += 0.25
        matrix[2 * m + 1, m] += 0.75
        matrix[2 * m + 1, min(m + 1, coarse_count - 1)] += 0.25
    return matrix


def in_vmem(count):
    return [pl.BlockSpec(memory_space=pltpu.VMEM)] * count


PARAMS = pltpu.CompilerParams(vmem_limit_bytes=VMEM_LIMIT)


def local(density, courant_r, courant_t, courant_z, ionization, send_block, recv_slot):
    rows_z, cells_t, cells_r = density.shape
    ax_count = lax.axis_size("ax")
    az_count = lax.axis_size("az")
    owned = recv_slot.shape[1]

    def flat(a, i):
        return a * ax_count + i

    even_pairs = [(i, i ^ 1) for i in range(ax_count)]
    odd_pairs = []
    for a in range(az_count):
        odd_pairs += [(flat(a, i), flat(a, ((i - 1) ^ 1) + 1)) for i in range(1, ax_count - 1)]
        odd_pairs += [(flat(a, i), flat(a ^ 1, i)) for i in (0, ax_count - 1)]

    def by(steps):
        return [(a, (a + steps) % az_count) for a in range(az_count)]

    def exchange(sector, even, odd):
        if az_count == 2:
            sectors = [lax.ppermute(sector, "az", by(1))]
        else:
            sectors = [lax.ppermute(sector, "az", by(s)) for s in (1, az_count - 1, az_count // 2)]
        return sectors, lax.ppermute(even, "ax", even_pairs), lax.ppermute(odd, ("az", "ax"), odd_pairs)

    sector_shape = jax.ShapeDtypeStruct((rows_z // 4 + 1, cells_t, cells_r), BF16)
    slab_three = jax.ShapeDtypeStruct((3, cells_t, cells_r), BF16)
    slab_two = jax.ShapeDtypeStruct((3, cells_t, cells_r), BF16)
    field = jax.ShapeDtypeStruct(density.shape, F32)

    given = (
        density, courant_t, courant_z, courant_r, ionization, jnp.transpose(send_block, (0, 2, 1)), recv_slot
    )
    given = tuple(pltpu.with_memory_space_constraint(x, pltpu.HBM) for x in given)
    *held, sector, even, odd = pl.pallas_call(
        functools.partial(first_messages, len(given)),
        out_shape=tuple(jax.ShapeDtypeStruct(x.shape, x.dtype) for x in given)
        + (sector_shape, slab_three, slab_three),
        in_specs=[pl.BlockSpec(memory_space=pltpu.HBM)] * len(given),
        out_specs=tuple(in_vmem(len(given) + 3)),
        scratch_shapes=[pltpu.SemaphoreType.DMA((len(given),))],
        compiler_params=PARAMS,
        name="first_messages",
    )(*given)
    density, courant_t, courant_z, courant_r, ionization, wanted, slots = held
    sectors, even, odd = exchange(sector, even, odd)
    count = len(sectors)

    inner_cost = pl.CostEstimate(flops=40 * density.size, bytes_accessed=16 * density.size, transcendentals=0)
    partial = pl.pallas_call(
        first_inner,
        out_shape=field,
        in_specs=in_vmem(4),
        out_specs=in_vmem(1)[0],
        compiler_params=PARAMS,
        cost_estimate=inner_cost,
        name="first_inner",
    )(density, courant_r, courant_z, ionization)
    section, sector, even_two, odd_two = pl.pallas_call(
        functools.partial(first_stage, count),
        out_shape=(field, sector_shape, slab_two, slab_two),
        in_specs=in_vmem(7 + count),
        out_specs=tuple(in_vmem(4)),
        compiler_params=PARAMS,
        name="first_stage",
    )(odd, *sectors, even, partial, density, courant_r, courant_t, courant_z)
    sectors_two, even_two, odd_two = exchange(sector, even_two, odd_two)

    partial = pl.pallas_call(
        second_inner,
        out_shape=field,
        in_specs=in_vmem(5),
        out_specs=in_vmem(1)[0],
        compiler_params=PARAMS,
        cost_estimate=inner_cost,
        name="second_inner",
    )(density, section, courant_r, courant_z, ionization)
    blocks = rows_z // BZ * (cells_t // BT) * (cells_r // BR)
    evolved, outgoing = pl.pallas_call(
        functools.partial(second_stage, count),
        out_shape=(field, jax.ShapeDtypeStruct((ax_count, CHUNK_ROWS, BR), BF16)),
        in_specs=in_vmem(11 + count),
        out_specs=tuple(in_vmem(2)),
        scratch_shapes=[
            pltpu.VMEM((blocks + 1, BLOCK_ROWS, BR), BF16),
            pltpu.VMEM((blocks + 1, BT, BR), F32),
            pltpu.SMEM(wanted.shape, jnp.int32),
            pltpu.SemaphoreType.DMA,
        ],
        compiler_params=PARAMS,
        name="second_stage",
    )(
        odd_two, *sectors_two, even_two, partial, wanted, section, courant_r, courant_t, courant_z,
        sectors[0], even, odd,
    )

    arrived = lax.all_to_all(outgoing, "ax", split_axis=0, concat_axis=0, tiled=True)

    tile_matrix = np.kron(interp_matrix(BZ), interp_matrix(BT))
    tile_matrix = jnp.asarray(np.concatenate([tile_matrix, tile_matrix], axis=1), BF16)
    radial_matrix = jnp.asarray(interp_matrix(BR).T, BF16)
    fine_rows = 4 * BZ * BT
    evolved, patches = pl.pallas_call(
        prolong_patches,
        out_shape=(field, jax.ShapeDtypeStruct((owned, fine_rows, 2 * BR), F32)),
        in_specs=in_vmem(5),
        out_specs=(pl.BlockSpec(memory_space=pltpu.HBM),) * 2,
        scratch_shapes=[
            pltpu.VMEM((ax_count, CHUNK_ROWS, 2 * BR), F32),
            pltpu.VMEM((owned, fine_rows, 2 * BR), F32),
            pltpu.SMEM(slots.shape, jnp.int32),
            pltpu.SemaphoreType.DMA((-(-owned // GROUP) + 2,)),
        ],
        compiler_params=PARAMS,
        name="prolong_patches",
    )(slots, evolved, arrived, radial_matrix, tile_matrix)
    return (evolved, patches.reshape(1, owned, 2 * BZ, 2 * BT, 2 * BR))


def solution(mesh):
    in_specs = (
        P("ax", "az", None),
        P("ax", "az", None),
        P("ax", "az", None),
        P("ax", "az", None),
        P("ax", "az", None),
        P("az", "ax", None),
        P("az", "ax"),
    )
    out_specs = (P("ax", "az", None), P("az", "ax", None, None, None))
    return jax.shard_map(local, mesh=mesh, in_specs=in_specs, out_specs=out_specs, check_vma=False)
```

```python
import functools

import jax
import jax.numpy as jnp
import numpy as np
from jax import lax
from jax.experimental import pallas as pl
from jax.experimental.pallas import tpu as pltpu
from jax.sharding import PartitionSpec as P

BZ = 4
BT = 8
BR = 128
CAP = 2
HEAD_R = 2
GROUP = 4
F32 = jnp.float32
BF16 = jnp.bfloat16
DIFFUSION = 0.05
VMEM_LIMIT = 24 * 1024 * 1024

BLOCK_ROWS = BZ * BT
MEAN_ROW = CAP * BLOCK_ROWS
CHUNK_ROWS = MEAN_ROW + 8


def pack_sector(values, courant_t, out_ref):
    rows_z, cells_t, cells_r = values.shape
    row = lax.broadcasted_iota(jnp.int32, (8, cells_r), 0)
    lane = lax.broadcasted_iota(jnp.int32, (cells_t, 128), 1)
    inner = jnp.zeros((cells_t, 128), F32)
    ends = []
    for k in range(rows_z):
        ends.append(jnp.where(row < 2, values[k, 0:8, :], values[k, cells_t - 8 :, :]))
        inner = jnp.where(lane == k, values[k, :, 0:1], inner)
    outer = (row < 2) | (row > 5)
    tiles = [
        jnp.where(outer, ends[k], pltpu.roll(ends[k + 1], 4, 0)) for k in range(0, rows_z, 2)
    ]
    faces = jnp.zeros((8, cells_r), F32)
    if courant_t is not None:
        for k in range(rows_z):
            face = courant_t[k].astype(F32)[cells_t - 8 :, :]
            faces = jnp.where(row == k, pltpu.roll(face, (k + 1) % 8, 0), faces)
    tiles.append(faces)
    rounded = inner.astype(BF16).astype(F32)
    rest = inner - rounded
    tiles.append(jnp.concatenate([rounded[:8], rounded[8:], rest[:8], rest[8:]], axis=1))
    for pair in range(len(tiles) // 2):
        out_ref[pair] = jnp.concatenate(tiles[2 * pair : 2 * pair + 2], axis=0).astype(BF16)


def tile_of(msg, index):
    return msg[index // 2].astype(F32)[(index % 2) * 8 : (index % 2) * 8 + 8, :]


def pack_slab(values, courant_z, even_ref, odd_ref):
    rows_z = values.shape[0]
    parity = lax.rem(lax.axis_index("ax"), 2)
    first_even = jnp.where(parity == 0, rows_z - 2, 0)
    first_odd = jnp.where(parity == 0, 0, rows_z - 2)
    for out_ref, first in ((even_ref, first_even), (odd_ref, first_odd)):
        for r in range(2):
            out_ref[r] = values[first + r].astype(BF16)
        if courant_z is not None:
            out_ref[2] = courant_z[rows_z - 1]


def first_messages(count, *refs):
    given, held = refs[:count], refs[count : 2 * count]
    sector_out, even_out, odd_out, sems = refs[2 * count :]
    copies = [pltpu.make_async_copy(given[i], held[i], sems.at[i]) for i in range(count)]
    for copy in copies:
        copy.start()
    density, courant_t, courant_z = held[:3]
    for copy in copies[:3]:
        copy.wait()
    pack_slab(density, courant_z, even_out, odd_out)
    pack_sector(density, courant_t, sector_out)
    for copy in copies[3:]:
        copy.wait()


def axial_flux(courant, back, here, up, up_two):
    low = here + 0.25 * (up - back)
    high = up - 0.25 * (up_two - here)
    return courant * jnp.where(courant > 0.0, low, high)


def inner_rates(values, courant_r, courant_z, ionization):
    rows_z, cells_t, cells_r = values.shape
    zero = jnp.zeros((cells_t, cells_r), F32)

    def row_at(k):
        return values[k] if 0 <= k < rows_z else zero

    lane = lax.broadcasted_iota(jnp.int32, (cells_t, cells_r), 1)
    index = lane.astype(F32)
    area = jnp.where(lane < cells_r - 1, index + 1.0, 0.0)
    inverse_radius = 1.0 / (index + 0.5)
    flux_z = zero
    for k in range(rows_z):
        here, back, up = row_at(k), row_at(k - 1), row_at(k + 1)
        next_flux = zero
        if k < rows_z - 1:
            next_flux = axial_flux(courant_z[k].astype(F32), back, here, up, row_at(k + 2))
        rate = (
            DIFFUSION * (up - 2.0 * here + back)
            + ionization[k].astype(F32) * here
            - (next_flux - flux_z)
        )
        flux_z = next_flux
        inward = jnp.where(lane == 0, 0.0, pltpu.roll(here, 1, 1))
        outward = jnp.where(lane == cells_r - 1, 0.0, pltpu.roll(here, cells_r - 1, 1))
        quarter = 0.25 * (outward - inward)
        courant = courant_r[k].astype(F32)
        flux = courant * jnp.where(
            courant > 0.0, here + quarter, pltpu.roll(here - quarter, cells_r - 1, 1)
        )
        carried = area * (DIFFUSION * (outward - here) - flux)
        yield rate + (carried - pltpu.roll(carried, 1, 1)) * inverse_radius


def outer_rates(values, sector, slab, faces_below, courants):
    rows_z, cells_t, cells_r = values.shape
    left, right, across = sector
    even_msg, odd_msg = slab
    left_faces, even_faces, odd_faces = faces_below
    courant_r, courant_t, courant_z = courants
    me = lax.axis_index("ax")
    is_even = lax.rem(me, 2) == 0
    has_below = me > 0
    has_above = me < lax.axis_size("ax") - 1
    zero = jnp.zeros((cells_t, cells_r), F32)

    def below(even, odd):
        return jnp.where(has_below, jnp.where(is_even, odd, even).astype(F32), zero)

    def above(even, odd):
        return jnp.where(has_above, jnp.where(is_even, even, odd).astype(F32), zero)

    top = rows_z - 1
    below_one, below_two = below(even_msg[1], odd_msg[1]), below(even_msg[0], odd_msg[0])
    above_one, above_two = above(even_msg[0], odd_msg[0]), above(even_msg[1], odd_msg[1])
    first_flux = axial_flux(
        below(even_faces[2], odd_faces[2]), below_two, below_one, values[0], values[1]
    )
    last_flux = axial_flux(
        courant_z[top].astype(F32), values[top - 1], values[top], above_one, above_two
    )
    low_change = -0.25 * jnp.maximum(courant_z[0].astype(F32), 0.0) * below_one
    high_change = -0.25 * jnp.minimum(courant_z[top - 1].astype(F32), 0.0) * above_one
    axial = {
        0: first_flux - low_change + DIFFUSION * below_one,
        1: low_change,
        top - 1: -high_change,
        top: high_change - last_flux + DIFFUSION * above_one,
    }
    halo_row = lax.broadcasted_iota(jnp.int32, (8, cells_r), 0)
    lane = lax.broadcasted_iota(jnp.int32, (cells_t, 128), 1)
    packed = tile_of(across, rows_z // 2 + 1)
    packed = packed[:, 0:256] + packed[:, 256:512]
    inner = jnp.concatenate([packed[:, 0:128], packed[:, 128:256]], axis=0)
    faces = tile_of(left_faces, rows_z // 2)
    rows = cells_t + 8
    for k in range(rows_z):
        here = values[k]
        halo = tile_of(left, k // 2)
        if right is not left:
            beyond = (halo_row < 2) | (halo_row == 4) | (halo_row == 5)
            halo = jnp.where(beyond, tile_of(right, k // 2), halo)
        if k % 2:
            halo = pltpu.roll(halo, 4, 0)
        ring = jnp.concatenate([halo, here], axis=0)
        face_halo = pltpu.roll(faces, 7 - k, 0)
        courant = jnp.concatenate([face_halo, courant_t[k].astype(F32)], axis=0)
        quarter = 0.25 * (pltpu.roll(ring, rows - 1, 0) - pltpu.roll(ring, 1, 0))
        flux = courant * jnp.where(courant > 0.0, ring + quarter, pltpu.roll(ring - quarter, rows - 1, 0))
        rate = (pltpu.roll(flux, 1, 0) - flux)[8:, :]
        if k in axial:
            rate = rate + axial[k]
        change = 0.25 * jnp.maximum(courant_r[k, :, 0:128].astype(F32), 0.0)
        change = change * (pltpu.roll(inner, 128 - k, 1) if k else inner)
        change = jnp.where(lane == 0, change, 0.0)
        change = 2.0 * change - (1.0 / 1.5) * pltpu.roll(change, 1, 1)
        yield jnp.concatenate([rate[:, 0:128] + change, rate[:, 128:]], axis=1)


def first_inner(density, courant_r, courant_z, ionization, partial):
    for k, rate in enumerate(inner_rates(density, courant_r, courant_z, ionization)):
        partial[k] = density[k] + rate


def second_inner(density, section, courant_r, courant_z, ionization, partial):
    for k, rate in enumerate(inner_rates(section, courant_r, courant_z, ionization)):
        partial[k] = 0.5 * (density[k] + section[k] + rate)


def first_stage(count, *refs):
    odd, sector, refs = refs[0], refs[1 : 1 + count], refs[1:]
    even, partial, density, courant_r, courant_t, courant_z = refs[count : count + 6]
    section, sector_out, even_out, odd_out = refs[count + 6 :]
    left, right, across = sector if count == 3 else sector * 3
    steps = outer_rates(
        density, (left, right, across), (even, odd), (left, even, odd), (courant_r, courant_t, courant_z)
    )
    for k, rate in enumerate(steps):
        section[k] = partial[k] + rate
    pack_sector(section, None, sector_out)
    pack_slab(section, None, even_out, odd_out)


def second_stage(count, *refs):
    wanted, odd, sector, refs = refs[0], refs[1], refs[2 : 2 + count], refs[2:]
    even, partial, section, courant_r, courant_t, courant_z = refs[count : count + 6]
    left_faces, even_faces, odd_faces = refs[count + 6 : count + 9]
    evolved, outgoing, table, means = refs[count + 9 :]
    left, right, across = sector if count == 3 else sector * 3
    steps = outer_rates(
        section,
        (left, right, across),
        (even, odd),
        (left_faces, even_faces, odd_faces),
        (courant_r, courant_t, courant_z),
    )
    for k, rate in enumerate(steps):
        evolved[k] = partial[k] + 0.5 * rate
    rows_z, cells_t, cells_r = evolved.shape
    blocks_t, blocks_r = cells_t // BT, cells_r // BR
    total = rows_z // BZ * blocks_t * blocks_r
    for block in range(total):
        z = block // (blocks_t * blocks_r) * BZ
        t = block // blocks_r % blocks_t * BT
        r = block % blocks_r * BR
        if r >= HEAD_R * BR:
            continue
        tiles = [evolved[z + i, t : t + BT, r : r + BR] for i in range(BZ)]
        mean = jnp.mean(sum(tiles), axis=0, keepdims=True) * (1.0 / BZ)
        mean = jnp.broadcast_to(mean.astype(BF16).astype(F32), (BT, BR))
        means[block] = mean
        table[block] = jnp.concatenate([tile - mean for tile in tiles], axis=0).astype(BF16)
    means[total] = jnp.zeros((BT, BR), F32)
    table[total] = jnp.zeros((BLOCK_ROWS, BR), BF16)
    row = lax.broadcasted_iota(jnp.int32, (8, BR), 0)
    for owner in range(outgoing.shape[0]):
        mean_rows = jnp.zeros((8, BR), F32)
        for slot in range(CAP):
            block = wanted[0, slot, owner]
            outgoing[owner, slot * BLOCK_ROWS : (slot + 1) * BLOCK_ROWS, :] = table[block]
            mean_rows = jnp.where(row == slot, means[block], mean_rows)
        outgoing[owner, MEAN_ROW:, :] = mean_rows.astype(BF16)


def prolong_patches(slots, evolved, arrived, radial_matrix, tile_matrix, evolved_out, patches, fine, sems):
    copies = [pltpu.make_async_copy(evolved, evolved_out, sems.at[0])]
    copies[0].start()
    owned = fine.shape[0]

    def radial(group):
        blocks, chosen = [], []
        for p in group:
            source = lax.shift_right_logical(slots[0, p], 1)
            slot = lax.bitwise_and(slots[0, p], 1)
            row = pl.multiple_of(slot * BLOCK_ROWS, BLOCK_ROWS)
            blocks += [arrived[source, pl.ds(row, BLOCK_ROWS), :], arrived[source, MEAN_ROW:, :]]
            chosen.append(slot)
        spread = jnp.dot(jnp.concatenate(blocks, axis=0), radial_matrix[...], preferred_element_type=F32)
        pairs = []
        for i, slot in enumerate(chosen):
            first = i * (BLOCK_ROWS + 8)
            after = first + BLOCK_ROWS
            mean = jnp.where(slot == 0, spread[after : after + 1], spread[after + 1 : after + 2])
            coarse = spread[first:after] + mean
            high = coarse.astype(BF16)
            low = (coarse - high.astype(F32)).astype(BF16)
            pairs.append(jnp.concatenate([high, low], axis=0))
        return pairs

    groups = [range(p, min(p + GROUP, owned)) for p in range(0, owned, GROUP)]
    following = radial(groups[0])
    for g, group in enumerate(groups):
        pairs = following
        if g + 1 < len(groups):
            following = radial(groups[g + 1])
        for p, pair in zip(group, pairs):
            fine[p] = jnp.dot(tile_matrix[...], pair, preferred_element_type=F32)
        part = pl.ds(group[0], len(group))
        copies.append(pltpu.make_async_copy(fine.at[part], patches.at[part], sems.at[g + 1]))
        copies[-1].start()
    for copy in copies:
        copy.wait()


def interp_matrix(coarse_count):
    matrix = np.zeros((2 * coarse_count, coarse_count), np.float32)
    for m in range(coarse_count):
        matrix[2 * m, m] += 0.75
        matrix[2 * m, max(m - 1, 0)] += 0.25
        matrix[2 * m + 1, m] += 0.75
        matrix[2 * m + 1, min(m + 1, coarse_count - 1)] += 0.25
    return matrix


def in_vmem(count):
    return [pl.BlockSpec(memory_space=pltpu.VMEM)] * count


def in_smem(count):
    return [pl.BlockSpec(memory_space=pltpu.SMEM)] * count


PARAMS = pltpu.CompilerParams(vmem_limit_bytes=VMEM_LIMIT)


def local(density, courant_r, courant_t, courant_z, ionization, send_block, recv_slot):
    rows_z, cells_t, cells_r = density.shape
    ax_count = lax.axis_size("ax")
    az_count = lax.axis_size("az")
    owned = recv_slot.shape[1]

    def flat(a, i):
        return a * ax_count + i

    even_pairs = [(i, i ^ 1) for i in range(ax_count)]
    odd_pairs = []
    for a in range(az_count):
        odd_pairs += [(flat(a, i), flat(a, ((i - 1) ^ 1) + 1)) for i in range(1, ax_count - 1)]
        odd_pairs += [(flat(a, i), flat(a ^ 1, i)) for i in (0, ax_count - 1)]

    def by(steps):
        return [(a, (a + steps) % az_count) for a in range(az_count)]

    def exchange(sector, even, odd):
        if az_count == 2:
            sectors = [lax.ppermute(sector, "az", by(1))]
        else:
            sectors = [lax.ppermute(sector, "az", by(s)) for s in (1, az_count - 1, az_count // 2)]
        return sectors, lax.ppermute(even, "ax", even_pairs), lax.ppermute(odd, ("az", "ax"), odd_pairs)

    sector_shape = jax.ShapeDtypeStruct((rows_z // 4 + 1, cells_t, cells_r), BF16)
    slab_three = jax.ShapeDtypeStruct((3, cells_t, cells_r), BF16)
    slab_two = jax.ShapeDtypeStruct((3, cells_t, cells_r), BF16)
    field = jax.ShapeDtypeStruct(density.shape, F32)

    given = (
        density, courant_t, courant_z, courant_r, ionization, jnp.transpose(send_block, (0, 2, 1)), recv_slot
    )
    given = tuple(pltpu.with_memory_space_constraint(x, pltpu.HBM) for x in given)
    *held, sector, even, odd = pl.pallas_call(
        functools.partial(first_messages, len(given)),
        out_shape=tuple(
            pltpu.SMEM(x.shape, x.dtype) if x.dtype == jnp.int32 else jax.ShapeDtypeStruct(x.shape, x.dtype)
            for x in given
        )
        + (sector_shape, slab_three, slab_three),
        in_specs=[pl.BlockSpec(memory_space=pltpu.HBM)] * len(given),
        out_specs=tuple(in_vmem(len(given) - 2) + in_smem(2) + in_vmem(3)),
        scratch_shapes=[pltpu.SemaphoreType.DMA((len(given),))],
        compiler_params=PARAMS,
        name="first_messages",
    )(*given)
    density, courant_t, courant_z, courant_r, ionization, wanted, slots = held
    sectors, even, odd = exchange(sector, even, odd)
    count = len(sectors)

    inner_cost = pl.CostEstimate(flops=40 * density.size, bytes_accessed=16 * density.size, transcendentals=0)
    partial = pl.pallas_call(
        first_inner,
        out_shape=field,
        in_specs=in_vmem(4),
        out_specs=in_vmem(1)[0],
        compiler_params=PARAMS,
        cost_estimate=inner_cost,
        name="first_inner",
    )(density, courant_r, courant_z, ionization)
    section, sector, even_two, odd_two = pl.pallas_call(
        functools.partial(first_stage, count),
        out_shape=(field, sector_shape, slab_two, slab_two),
        in_specs=in_vmem(7 + count),
        out_specs=tuple(in_vmem(4)),
        compiler_params=PARAMS,
        name="first_stage",
    )(odd, *sectors, even, partial, density, courant_r, courant_t, courant_z)
    sectors_two, even_two, odd_two = exchange(sector, even_two, odd_two)

    partial = pl.pallas_call(
        second_inner,
        out_shape=field,
        in_specs=in_vmem(5),
        out_specs=in_vmem(1)[0],
        compiler_params=PARAMS,
        cost_estimate=inner_cost,
        name="second_inner",
    )(density, section, courant_r, courant_z, ionization)
    blocks = rows_z // BZ * (cells_t // BT) * (cells_r // BR)
    evolved, outgoing = pl.pallas_call(
        functools.partial(second_stage, count),
        out_shape=(field, jax.ShapeDtypeStruct((ax_count, CHUNK_ROWS, BR), BF16)),
        in_specs=in_smem(1) + in_vmem(10 + count),
        out_specs=tuple(in_vmem(2)),
        scratch_shapes=[
            pltpu.VMEM((blocks + 1, BLOCK_ROWS, BR), BF16),
            pltpu.VMEM((blocks + 1, BT, BR), F32),
        ],
        compiler_params=PARAMS,
        name="second_stage",
    )(
        wanted, odd_two, *sectors_two, even_two, partial, section, courant_r, courant_t, courant_z,
        sectors[0], even, odd,
    )

    arrived = lax.all_to_all(outgoing, "ax", split_axis=0, concat_axis=0, tiled=True)

    tile_matrix = np.kron(interp_matrix(BZ), interp_matrix(BT))
    tile_matrix = jnp.asarray(np.concatenate([tile_matrix, tile_matrix], axis=1), BF16)
    radial_matrix = jnp.asarray(interp_matrix(BR).T, BF16)
    fine_rows = 4 * BZ * BT
    evolved, patches = pl.pallas_call(
        prolong_patches,
        out_shape=(field, jax.ShapeDtypeStruct((owned, fine_rows, 2 * BR), F32)),
        in_specs=in_smem(1) + in_vmem(4),
        out_specs=(pl.BlockSpec(memory_space=pltpu.HBM),) * 2,
        scratch_shapes=[
            pltpu.VMEM((owned, fine_rows, 2 * BR), F32),
            pltpu.SemaphoreType.DMA((-(-owned // GROUP) + 1,)),
        ],
        compiler_params=PARAMS,
        name="prolong_patches",
    )(slots, evolved, arrived, radial_matrix, tile_matrix)
    return (evolved, patches.reshape(1, owned, 2 * BZ, 2 * BT, 2 * BR))


def solution(mesh):
    in_specs = (
        P("ax", "az", None),
        P("ax", "az", None),
        P("ax", "az", None),
        P("ax", "az", None),
        P("ax", "az", None),
        P("az", "ax", None),
        P("az", "ax"),
    )
    out_specs = (P("ax", "az", None), P("az", "ax", None, None, None))
    return jax.shard_map(local, mesh=mesh, in_specs=in_specs, out_specs=out_specs, check_vma=False)
```

```python
import functools

import jax
import jax.numpy as jnp
import numpy as np
from jax import lax
from jax.experimental import pallas as pl
from jax.experimental.pallas import tpu as pltpu
from jax.sharding import PartitionSpec as P

BZ = 4
BT = 8
BR = 128
CAP = 2
HEAD_R = 2
GROUP = 4
F32 = jnp.float32
BF16 = jnp.bfloat16
DIFFUSION = 0.05
VMEM_LIMIT = 24 * 1024 * 1024

BLOCK_ROWS = BZ * BT


def pack_sector(values, courant_t, out_ref):
    rows_z, cells_t, cells_r = values.shape
    row = lax.broadcasted_iota(jnp.int32, (8, cells_r), 0)
    lane = lax.broadcasted_iota(jnp.int32, (cells_t, 128), 1)
    inner = jnp.zeros((cells_t, 128), F32)
    ends = []
    for k in range(rows_z):
        ends.append(jnp.where(row < 2, values[k, 0:8, :], values[k, cells_t - 8 :, :]))
        inner = jnp.where(lane == k, values[k, :, 0:1], inner)
    outer = (row < 2) | (row > 5)
    tiles = [
        jnp.where(outer, ends[k], pltpu.roll(ends[k + 1], 4, 0)) for k in range(0, rows_z, 2)
    ]
    faces = jnp.zeros((8, cells_r), F32)
    if courant_t is not None:
        for k in range(rows_z):
            face = courant_t[k].astype(F32)[cells_t - 8 :, :]
            faces = jnp.where(row == k, pltpu.roll(face, (k + 1) % 8, 0), faces)
    tiles.append(faces)
    rounded = inner.astype(BF16).astype(F32)
    rest = inner - rounded
    tiles.append(jnp.concatenate([rounded[:8], rounded[8:], rest[:8], rest[8:]], axis=1))
    for pair in range(len(tiles) // 2):
        out_ref[pair] = jnp.concatenate(tiles[2 * pair : 2 * pair + 2], axis=0).astype(BF16)


def tile_of(msg, index):
    return msg[index // 2].astype(F32)[(index % 2) * 8 : (index % 2) * 8 + 8, :]


def pack_slab(values, courant_z, even_ref, odd_ref):
    rows_z = values.shape[0]
    parity = lax.rem(lax.axis_index("ax"), 2)
    first_even = jnp.where(parity == 0, rows_z - 2, 0)
    first_odd = jnp.where(parity == 0, 0, rows_z - 2)
    for out_ref, first in ((even_ref, first_even), (odd_ref, first_odd)):
        for r in range(2):
            out_ref[r] = values[first + r].astype(BF16)
        if courant_z is not None:
            out_ref[2] = courant_z[rows_z - 1]


def first_messages(count, *refs):
    given, held = refs[:count], refs[count : 2 * count]
    sector_out, even_out, odd_out, sems = refs[2 * count :]
    copies = [pltpu.make_async_copy(given[i], held[i], sems.at[i]) for i in range(count)]
    for copy in copies:
        copy.start()
    density, courant_t, courant_z = held[:3]
    for copy in copies[:3]:
        copy.wait()
    pack_slab(density, courant_z, even_out, odd_out)
    pack_sector(density, courant_t, sector_out)
    for copy in copies[3:]:
        copy.wait()


def stretched(x):
    square = x * x
    return jnp.where(x < 0.0, -square * square, square * square)


def unstretched(y):
    root = jnp.sqrt(jnp.sqrt(jnp.abs(y)))
    return jnp.where(y < 0.0, -root, root)


def axial_flux(courant, back, here, up, up_two):
    low = here + 0.25 * (up - back)
    high = up - 0.25 * (up_two - here)
    return courant * jnp.where(courant > 0.0, low, high)


def inner_rates(values, courant_r, courant_z, ionization):
    rows_z, cells_t, cells_r = values.shape
    zero = jnp.zeros((cells_t, cells_r), F32)

    def row_at(k):
        return values[k] if 0 <= k < rows_z else zero

    lane = lax.broadcasted_iota(jnp.int32, (cells_t, cells_r), 1)
    index = lane.astype(F32)
    area = jnp.where(lane < cells_r - 1, index + 1.0, 0.0)
    inverse_radius = 1.0 / (index + 0.5)
    flux_z = zero
    for k in range(rows_z):
        here, back, up = row_at(k), row_at(k - 1), row_at(k + 1)
        next_flux = zero
        if k < rows_z - 1:
            next_flux = axial_flux(courant_z[k].astype(F32), back, here, up, row_at(k + 2))
        rate = (
            DIFFUSION * (up - 2.0 * here + back)
            + ionization[k].astype(F32) * here
            - (next_flux - flux_z)
        )
        flux_z = next_flux
        inward = jnp.where(lane == 0, 0.0, pltpu.roll(here, 1, 1))
        outward = jnp.where(lane == cells_r - 1, 0.0, pltpu.roll(here, cells_r - 1, 1))
        quarter = 0.25 * (outward - inward)
        courant = courant_r[k].astype(F32)
        flux = courant * jnp.where(
            courant > 0.0, here + quarter, pltpu.roll(here - quarter, cells_r - 1, 1)
        )
        carried = area * (DIFFUSION * (outward - here) - flux)
        yield rate + (carried - pltpu.roll(carried, 1, 1)) * inverse_radius


def outer_rates(values, sector, slab, faces_below, courants):
    rows_z, cells_t, cells_r = values.shape
    left, right, across = sector
    even_msg, odd_msg = slab
    left_faces, even_faces, odd_faces = faces_below
    courant_r, courant_t, courant_z = courants
    me = lax.axis_index("ax")
    is_even = lax.rem(me, 2) == 0
    has_below = me > 0
    has_above = me < lax.axis_size("ax") - 1
    zero = jnp.zeros((cells_t, cells_r), F32)

    def below(even, odd):
        return jnp.where(has_below, jnp.where(is_even, odd, even).astype(F32), zero)

    def above(even, odd):
        return jnp.where(has_above, jnp.where(is_even, even, odd).astype(F32), zero)

    top = rows_z - 1
    below_one, below_two = below(even_msg[1], odd_msg[1]), below(even_msg[0], odd_msg[0])
    above_one, above_two = above(even_msg[0], odd_msg[0]), above(even_msg[1], odd_msg[1])
    first_flux = axial_flux(
        below(even_faces[2], odd_faces[2]), below_two, below_one, values[0], values[1]
    )
    last_flux = axial_flux(
        courant_z[top].astype(F32), values[top - 1], values[top], above_one, above_two
    )
    low_change = -0.25 * jnp.maximum(courant_z[0].astype(F32), 0.0) * below_one
    high_change = -0.25 * jnp.minimum(courant_z[top - 1].astype(F32), 0.0) * above_one
    axial = {
        0: first_flux - low_change + DIFFUSION * below_one,
        1: low_change,
        top - 1: -high_change,
        top: high_change - last_flux + DIFFUSION * above_one,
    }
    halo_row = lax.broadcasted_iota(jnp.int32, (8, cells_r), 0)
    lane = lax.broadcasted_iota(jnp.int32, (cells_t, 128), 1)
    packed = tile_of(across, rows_z // 2 + 1)
    packed = packed[:, 0:256] + packed[:, 256:512]
    inner = jnp.concatenate([packed[:, 0:128], packed[:, 128:256]], axis=0)
    faces = tile_of(left_faces, rows_z // 2)
    rows = cells_t + 8
    for k in range(rows_z):
        here = values[k]
        halo = tile_of(left, k // 2)
        if right is not left:
            beyond = (halo_row < 2) | (halo_row == 4) | (halo_row == 5)
            halo = jnp.where(beyond, tile_of(right, k // 2), halo)
        if k % 2:
            halo = pltpu.roll(halo, 4, 0)
        ring = jnp.concatenate([halo, here], axis=0)
        face_halo = pltpu.roll(faces, 7 - k, 0)
        courant = jnp.concatenate([face_halo, courant_t[k].astype(F32)], axis=0)
        quarter = 0.25 * (pltpu.roll(ring, rows - 1, 0) - pltpu.roll(ring, 1, 0))
        flux = courant * jnp.where(courant > 0.0, ring + quarter, pltpu.roll(ring - quarter, rows - 1, 0))
        rate = (pltpu.roll(flux, 1, 0) - flux)[8:, :]
        if k in axial:
            rate = rate + axial[k]
        change = 0.25 * jnp.maximum(courant_r[k, :, 0:128].astype(F32), 0.0)
        change = change * (pltpu.roll(inner, 128 - k, 1) if k else inner)
        change = jnp.where(lane == 0, change, 0.0)
        change = 2.0 * change - (1.0 / 1.5) * pltpu.roll(change, 1, 1)
        yield jnp.concatenate([rate[:, 0:128] + change, rate[:, 128:]], axis=1)


def first_inner(density, courant_r, courant_z, ionization, partial):
    for k, rate in enumerate(inner_rates(density, courant_r, courant_z, ionization)):
        partial[k] = density[k] + rate


def second_inner(density, section, courant_r, courant_z, ionization, partial):
    for k, rate in enumerate(inner_rates(section, courant_r, courant_z, ionization)):
        partial[k] = 0.5 * (density[k] + section[k] + rate)


def first_stage(count, *refs):
    odd, sector, refs = refs[0], refs[1 : 1 + count], refs[1:]
    even, partial, density, courant_r, courant_t, courant_z = refs[count : count + 6]
    section, sector_out, even_out, odd_out = refs[count + 6 :]
    left, right, across = sector if count == 3 else sector * 3
    steps = outer_rates(
        density, (left, right, across), (even, odd), (left, even, odd), (courant_r, courant_t, courant_z)
    )
    for k, rate in enumerate(steps):
        section[k] = partial[k] + rate
    pack_sector(section, None, sector_out)
    pack_slab(section, None, even_out, odd_out)


def second_stage(count, *refs):
    wanted, odd, sector, refs = refs[0], refs[1], refs[2 : 2 + count], refs[2:]
    even, partial, section, courant_r, courant_t, courant_z = refs[count : count + 6]
    left_faces, even_faces, odd_faces = refs[count + 6 : count + 9]
    evolved, outgoing, table = refs[count + 9 :]
    left, right, across = sector if count == 3 else sector * 3
    steps = outer_rates(
        section,
        (left, right, across),
        (even, odd),
        (left_faces, even_faces, odd_faces),
        (courant_r, courant_t, courant_z),
    )
    for k, rate in enumerate(steps):
        evolved[k] = partial[k] + 0.5 * rate
    rows_z, cells_t, cells_r = evolved.shape
    blocks_t, blocks_r = cells_t // BT, cells_r // BR
    total = rows_z // BZ * blocks_t * blocks_r
    for block in range(total):
        z = block // (blocks_t * blocks_r) * BZ
        t = block // blocks_r % blocks_t * BT
        r = block % blocks_r * BR
        if r >= HEAD_R * BR:
            continue
        tiles = [stretched(evolved[z + i, t : t + BT, r : r + BR]) for i in range(BZ)]
        table[block] = jnp.concatenate(tiles, axis=0).astype(BF16)
    table[total] = jnp.zeros((BLOCK_ROWS, BR), BF16)
    for owner in range(outgoing.shape[0]):
        for slot in range(CAP):
            outgoing[owner, slot * BLOCK_ROWS : (slot + 1) * BLOCK_ROWS, :] = table[wanted[0, slot, owner]]


def halves(x):
    high = x.astype(BF16)
    return jnp.concatenate([high, (x - high.astype(F32)).astype(BF16)], axis=0)


def prolong_patches(slots, evolved, arrived, radial_matrix, tile_matrix, evolved_out, patches, fine, sems):
    copies = [pltpu.make_async_copy(evolved, evolved_out, sems.at[0])]
    copies[0].start()
    owned = fine.shape[0]

    def radial(group):
        blocks = []
        for p in group:
            source = lax.shift_right_logical(slots[0, p], 1)
            row = pl.multiple_of(lax.bitwise_and(slots[0, p], 1) * BLOCK_ROWS, BLOCK_ROWS)
            blocks.append(halves(unstretched(arrived[source, pl.ds(row, BLOCK_ROWS), :].astype(F32))))
        spread = jnp.dot(jnp.concatenate(blocks, axis=0), radial_matrix[...], preferred_element_type=F32)
        firsts = [2 * BLOCK_ROWS * i for i in range(len(blocks))]
        return [halves(spread[f : f + BLOCK_ROWS] + spread[f + BLOCK_ROWS : f + 2 * BLOCK_ROWS]) for f in firsts]

    groups = [range(p, min(p + GROUP, owned)) for p in range(0, owned, GROUP)]
    following = radial(groups[0])
    for g, group in enumerate(groups):
        pairs = following
        if g + 1 < len(groups):
            following = radial(groups[g + 1])
        for p, pair in zip(group, pairs):
            fine[p] = jnp.dot(tile_matrix[...], pair, preferred_element_type=F32)
        part = pl.ds(group[0], len(group))
        copies.append(pltpu.make_async_copy(fine.at[part], patches.at[part], sems.at[g + 1]))
        copies[-1].start()
    for copy in copies:
        copy.wait()


def interp_matrix(coarse_count):
    matrix = np.zeros((2 * coarse_count, coarse_count), np.float32)
    for m in range(coarse_count):
        matrix[2 * m, m] += 0.75
        matrix[2 * m, max(m - 1, 0)] += 0.25
        matrix[2 * m + 1, m] += 0.75
        matrix[2 * m + 1, min(m + 1, coarse_count - 1)] += 0.25
    return matrix


def in_vmem(count):
    return [pl.BlockSpec(memory_space=pltpu.VMEM)] * count


def in_smem(count):
    return [pl.BlockSpec(memory_space=pltpu.SMEM)] * count


PARAMS = pltpu.CompilerParams(vmem_limit_bytes=VMEM_LIMIT)


def local(density, courant_r, courant_t, courant_z, ionization, send_block, recv_slot):
    rows_z, cells_t, cells_r = density.shape
    ax_count = lax.axis_size("ax")
    az_count = lax.axis_size("az")
    owned = recv_slot.shape[1]

    def flat(a, i):
        return a * ax_count + i

    even_pairs = [(i, i ^ 1) for i in range(ax_count)]
    odd_pairs = []
    for a in range(az_count):
        odd_pairs += [(flat(a, i), flat(a, ((i - 1) ^ 1) + 1)) for i in range(1, ax_count - 1)]
        odd_pairs += [(flat(a, i), flat(a ^ 1, i)) for i in (0, ax_count - 1)]

    def by(steps):
        return [(a, (a + steps) % az_count) for a in range(az_count)]

    def exchange(sector, even, odd):
        if az_count == 2:
            sectors = [lax.ppermute(sector, "az", by(1))]
        else:
            sectors = [lax.ppermute(sector, "az", by(s)) for s in (1, az_count - 1, az_count // 2)]
        return sectors, lax.ppermute(even, "ax", even_pairs), lax.ppermute(odd, ("az", "ax"), odd_pairs)

    sector_shape = jax.ShapeDtypeStruct((rows_z // 4 + 1, cells_t, cells_r), BF16)
    slab_three = jax.ShapeDtypeStruct((3, cells_t, cells_r), BF16)
    slab_two = jax.ShapeDtypeStruct((3, cells_t, cells_r), BF16)
    field = jax.ShapeDtypeStruct(density.shape, F32)

    given = (
        density, courant_t, courant_z, courant_r, ionization, jnp.transpose(send_block, (0, 2, 1)), recv_slot
    )
    given = tuple(pltpu.with_memory_space_constraint(x, pltpu.HBM) for x in given)
    *held, sector, even, odd = pl.pallas_call(
        functools.partial(first_messages, len(given)),
        out_shape=tuple(
            pltpu.SMEM(x.shape, x.dtype) if x.dtype == jnp.int32 else jax.ShapeDtypeStruct(x.shape, x.dtype)
            for x in given
        )
        + (sector_shape, slab_three, slab_three),
        in_specs=[pl.BlockSpec(memory_space=pltpu.HBM)] * len(given),
        out_specs=tuple(in_vmem(len(given) - 2) + in_smem(2) + in_vmem(3)),
        scratch_shapes=[pltpu.SemaphoreType.DMA((len(given),))],
        compiler_params=PARAMS,
        name="first_messages",
    )(*given)
    density, courant_t, courant_z, courant_r, ionization, wanted, slots = held
    sectors, even, odd = exchange(sector, even, odd)
    count = len(sectors)

    inner_cost = pl.CostEstimate(flops=40 * density.size, bytes_accessed=16 * density.size, transcendentals=0)
    partial = pl.pallas_call(
        first_inner,
        out_shape=field,
        in_specs=in_vmem(4),
        out_specs=in_vmem(1)[0],
        compiler_params=PARAMS,
        cost_estimate=inner_cost,
        name="first_inner",
    )(density, courant_r, courant_z, ionization)
    section, sector, even_two, odd_two = pl.pallas_call(
        functools.partial(first_stage, count),
        out_shape=(field, sector_shape, slab_two, slab_two),
        in_specs=in_vmem(7 + count),
        out_specs=tuple(in_vmem(4)),
        compiler_params=PARAMS,
        name="first_stage",
    )(odd, *sectors, even, partial, density, courant_r, courant_t, courant_z)
    sectors_two, even_two, odd_two = exchange(sector, even_two, odd_two)

    partial = pl.pallas_call(
        second_inner,
        out_shape=field,
        in_specs=in_vmem(5),
        out_specs=in_vmem(1)[0],
        compiler_params=PARAMS,
        cost_estimate=inner_cost,
        name="second_inner",
    )(density, section, courant_r, courant_z, ionization)
    blocks = rows_z // BZ * (cells_t // BT) * (cells_r // BR)
    evolved, outgoing = pl.pallas_call(
        functools.partial(second_stage, count),
        out_shape=(field, jax.ShapeDtypeStruct((ax_count, CAP * BLOCK_ROWS, BR), BF16)),
        in_specs=in_smem(1) + in_vmem(10 + count),
        out_specs=tuple(in_vmem(2)),
        scratch_shapes=[
            pltpu.VMEM((blocks + 1, BLOCK_ROWS, BR), BF16),
        ],
        compiler_params=PARAMS,
        name="second_stage",
    )(
        wanted, odd_two, *sectors_two, even_two, partial, section, courant_r, courant_t, courant_z,
        sectors[0], even, odd,
    )

    arrived = lax.all_to_all(outgoing, "ax", split_axis=0, concat_axis=0, tiled=True)

    tile_matrix = np.kron(interp_matrix(BZ), interp_matrix(BT))
    tile_matrix = jnp.asarray(np.concatenate([tile_matrix, tile_matrix], axis=1), BF16)
    radial_matrix = jnp.asarray(interp_matrix(BR).T, BF16)
    fine_rows = 4 * BZ * BT
    evolved, patches = pl.pallas_call(
        prolong_patches,
        out_shape=(field, jax.ShapeDtypeStruct((owned, fine_rows, 2 * BR), F32)),
        in_specs=in_smem(1) + in_vmem(4),
        out_specs=(pl.BlockSpec(memory_space=pltpu.HBM),) * 2,
        scratch_shapes=[
            pltpu.VMEM((owned, fine_rows, 2 * BR), F32),
            pltpu.SemaphoreType.DMA((-(-owned // GROUP) + 1,)),
        ],
        compiler_params=PARAMS,
        name="prolong_patches",
    )(slots, evolved, arrived, radial_matrix, tile_matrix)
    return (evolved, patches.reshape(1, owned, 2 * BZ, 2 * BT, 2 * BR))


def solution(mesh):
    in_specs = (
        P("ax", "az", None),
        P("ax", "az", None),
        P("ax", "az", None),
        P("ax", "az", None),
        P("ax", "az", None),
        P("az", "ax", None),
        P("az", "ax"),
    )
    out_specs = (P("ax", "az", None), P("az", "ax", None, None, None))
    return jax.shard_map(local, mesh=mesh, in_specs=in_specs, out_specs=out_specs, check_vma=False)
```

```python
import functools

import jax
import jax.numpy as jnp
import numpy as np
from jax import lax
from jax.experimental import pallas as pl
from jax.experimental.pallas import tpu as pltpu
from jax.sharding import PartitionSpec as P

BZ = 4
BT = 8
BR = 128
CAP = 2
HEAD_R = 2
GROUP = 4
F32 = jnp.float32
BF16 = jnp.bfloat16
DIFFUSION = 0.05
VMEM_LIMIT = 24 * 1024 * 1024

BLOCK_ROWS = BZ * BT


def pack_sector(values, courant_t, out_ref):
    rows_z, cells_t, cells_r = values.shape
    row = lax.broadcasted_iota(jnp.int32, (8, cells_r), 0)
    lane = lax.broadcasted_iota(jnp.int32, (cells_t, 128), 1)
    inner = jnp.zeros((cells_t, 128), F32)
    ends = []
    for k in range(rows_z):
        ends.append(jnp.where(row < 2, values[k, 0:8, :], values[k, cells_t - 8 :, :]))
        inner = jnp.where(lane == k, values[k, :, 0:1], inner)
    outer = (row < 2) | (row > 5)
    tiles = [
        jnp.where(outer, ends[k], pltpu.roll(ends[k + 1], 4, 0)) for k in range(0, rows_z, 2)
    ]
    if courant_t is not None:
        faces = jnp.zeros((8, cells_r), F32)
        for k in range(rows_z):
            face = courant_t[k].astype(F32)[cells_t - 8 :, :]
            faces = jnp.where(row == k, pltpu.roll(face, (k + 1) % 8, 0), faces)
        tiles.append(faces)
    rounded = inner.astype(BF16).astype(F32)
    rest = inner - rounded
    tiles.append(jnp.concatenate([rounded[:8], rounded[8:], rest[:8], rest[8:]], axis=1))
    write_tiles(out_ref, 0, tiles)


def unpack_inner(msg, index):
    parts = tile_of(msg, index, (0, 512))
    parts = parts[:, 0:256] + parts[:, 256:512]
    return jnp.concatenate([parts[:, 0:128], parts[:, 128:256]], axis=0)


def write_tiles(out_ref, first, tiles):
    if out_ref.shape[1] == 8:
        for index, tile in enumerate(tiles):
            out_ref[first + index] = tile.astype(BF16)
    else:
        for index in range(0, len(tiles), 2):
            out_ref[(first + index) // 2] = jnp.concatenate(tiles[index : index + 2], axis=0).astype(BF16)


def tile_of(msg, index, lanes):
    if msg.shape[1] == 8:
        return msg[index, :, lanes[0] : lanes[1]].astype(F32)
    return msg[index // 2, :, lanes[0] : lanes[1]].astype(F32)[(index % 2) * 8 : (index % 2) * 8 + 8, :]


def row_of(msg, r, rows, lanes):
    if msg.shape[1] == 8:
        parts = rows // 8
        return jnp.concatenate([tile_of(msg, parts * r + part, lanes) for part in range(parts)], axis=0)
    return msg[r, :, lanes[0] : lanes[1]].astype(F32)


def pack_slab(values, courant_z, even_ref, odd_ref):
    rows_z, cells_t, _ = values.shape
    parity = lax.rem(lax.axis_index("ax"), 2)
    first_even = jnp.where(parity == 0, rows_z - 2, 0)
    first_odd = jnp.where(parity == 0, 0, rows_z - 2)
    parts = cells_t // 8
    for out_ref, first in ((even_ref, first_even), (odd_ref, first_odd)):
        rows = [values[first + r] for r in range(2)]
        if courant_z is not None:
            rows.append(courant_z[rows_z - 1].astype(F32))
        for r, row in enumerate(rows):
            write_tiles(out_ref, parts * r, [row[8 * part : 8 * part + 8, :] for part in range(parts)])


def first_messages(count, *refs):
    given, held = refs[:count], refs[count : 2 * count]
    sector_out, even_out, odd_out, sems = refs[2 * count :]
    copies = [pltpu.make_async_copy(given[i], held[i], sems.at[i]) for i in range(count)]
    for copy in copies:
        copy.start()
    density, courant_t, courant_z = held[:3]
    for copy in copies[:3]:
        copy.wait()
    pack_slab(density, courant_z, even_out, odd_out)
    pack_sector(density, courant_t, sector_out)
    for copy in copies[3:]:
        copy.wait()


def stretched(x):
    square = x * x
    return jnp.where(x < 0.0, -square * square, square * square)


def unstretched(y):
    root = jnp.sqrt(jnp.sqrt(jnp.abs(y)))
    return jnp.where(y < 0.0, -root, root)


def axial_flux(courant, back, here, up, up_two):
    low = here + 0.25 * (up - back)
    high = up - 0.25 * (up_two - here)
    return courant * jnp.where(courant > 0.0, low, high)


def inner_rates(values, courant_r, courant_z, ionization):
    rows_z, cells_t, cells_r = values.shape
    zero = jnp.zeros((cells_t, cells_r), F32)

    def row_at(k):
        return values[k] if 0 <= k < rows_z else zero

    lane = lax.broadcasted_iota(jnp.int32, (cells_t, cells_r), 1)
    index = lane.astype(F32)
    area = jnp.where(lane < cells_r - 1, index + 1.0, 0.0)
    inverse_radius = 1.0 / (index + 0.5)
    flux_z = zero
    for k in range(rows_z):
        here, back, up = row_at(k), row_at(k - 1), row_at(k + 1)
        next_flux = zero
        if k < rows_z - 1:
            next_flux = axial_flux(courant_z[k].astype(F32), back, here, up, row_at(k + 2))
        rate = (
            DIFFUSION * (up - 2.0 * here + back)
            + ionization[k].astype(F32) * here
            - (next_flux - flux_z)
        )
        flux_z = next_flux
        inward = jnp.where(lane == 0, 0.0, pltpu.roll(here, 1, 1))
        outward = jnp.where(lane == cells_r - 1, 0.0, pltpu.roll(here, cells_r - 1, 1))
        quarter = 0.25 * (outward - inward)
        courant = courant_r[k].astype(F32)
        flux = courant * jnp.where(
            courant > 0.0, here + quarter, pltpu.roll(here - quarter, cells_r - 1, 1)
        )
        carried = area * (DIFFUSION * (outward - here) - flux)
        yield rate + (carried - pltpu.roll(carried, 1, 1)) * inverse_radius


def outer_rates(values, lanes, sector, inner, slab, faces_below, courants):
    rows_z, cells_t = values.shape[:2]
    low, high = lanes
    width = high - low
    left, right = sector
    even_msg, odd_msg = slab
    left_faces, even_faces, odd_faces = faces_below
    courant_r, courant_t, courant_z = courants
    me = lax.axis_index("ax")
    is_even = lax.rem(me, 2) == 0
    has_below = me > 0
    has_above = me < lax.axis_size("ax") - 1
    zero = jnp.zeros((cells_t, width), F32)

    def below(even, odd, r):
        even, odd = row_of(even, r, cells_t, lanes), row_of(odd, r, cells_t, lanes)
        return jnp.where(has_below, jnp.where(is_even, odd, even), zero)

    def above(even, odd, r):
        even, odd = row_of(even, r, cells_t, lanes), row_of(odd, r, cells_t, lanes)
        return jnp.where(has_above, jnp.where(is_even, even, odd), zero)

    def axial_courant(k):
        return courant_z[k, :, low:high].astype(F32)

    def at(k):
        return values[k, :, low:high]

    top = rows_z - 1
    below_one, below_two = below(even_msg, odd_msg, 1), below(even_msg, odd_msg, 0)
    above_one, above_two = above(even_msg, odd_msg, 0), above(even_msg, odd_msg, 1)
    below_courant = below(even_faces, odd_faces, 2)
    first_flux = axial_flux(below_courant, below_two, below_one, at(0), at(1))
    last_flux = axial_flux(axial_courant(top), at(top - 1), at(top), above_one, above_two)
    low_change = -0.25 * jnp.maximum(axial_courant(0), 0.0) * below_one
    high_change = -0.25 * jnp.minimum(axial_courant(top - 1), 0.0) * above_one
    axial = {
        0: first_flux - low_change + DIFFUSION * below_one,
        1: low_change,
        top - 1: -high_change,
        top: high_change - last_flux + DIFFUSION * above_one,
    }
    halo_row = lax.broadcasted_iota(jnp.int32, (8, width), 0)
    lane = lax.broadcasted_iota(jnp.int32, (cells_t, 128), 1)
    faces = tile_of(left_faces, rows_z // 2, lanes)
    rows = cells_t + 8
    for k in range(rows_z):
        here = at(k)
        halo = tile_of(left, k // 2, lanes)
        if right is not left:
            beyond = (halo_row < 2) | (halo_row == 4) | (halo_row == 5)
            halo = jnp.where(beyond, tile_of(right, k // 2, lanes), halo)
        if k % 2:
            halo = pltpu.roll(halo, 4, 0)
        ring = jnp.concatenate([halo, here], axis=0)
        face_halo = pltpu.roll(faces, 7 - k, 0)
        courant = jnp.concatenate([face_halo, courant_t[k, :, low:high].astype(F32)], axis=0)
        quarter = 0.25 * (pltpu.roll(ring, rows - 1, 0) - pltpu.roll(ring, 1, 0))
        flux = courant * jnp.where(courant > 0.0, ring + quarter, pltpu.roll(ring - quarter, rows - 1, 0))
        rate = (pltpu.roll(flux, 1, 0) - flux)[8:, :]
        if k in axial:
            rate = rate + axial[k]
        if inner is None:
            yield rate
            continue
        change = 0.25 * jnp.maximum(courant_r[k, :, 0:128].astype(F32), 0.0)
        change = change * (pltpu.roll(inner, 128 - k, 1) if k else inner)
        change = jnp.where(lane == 0, change, 0.0)
        change = 2.0 * change - (1.0 / 1.5) * pltpu.roll(change, 1, 1)
        yield jnp.concatenate([rate[:, 0:128] + change, rate[:, 128:]], axis=1)


def first_inner(density, courant_r, courant_z, ionization, partial):
    for k, rate in enumerate(inner_rates(density, courant_r, courant_z, ionization)):
        partial[k] = density[k] + rate


def second_inner(density, section, courant_r, courant_z, ionization, partial):
    for k, rate in enumerate(inner_rates(section, courant_r, courant_z, ionization)):
        partial[k] = 0.5 * (density[k] + section[k] + rate)


def first_stage(count, *refs):
    odd, sector, refs = refs[0], refs[1 : 1 + count], refs[1:]
    even, partial, density, courant_r, courant_t, courant_z = refs[count : count + 6]
    section, sector_out, even_out, odd_out = refs[count + 6 :]
    left, right, across = sector if count == 3 else sector * 3
    inner = unpack_inner(across, density.shape[0] // 2 + 1)
    steps = outer_rates(
        density,
        (0, density.shape[2]),
        (left, right),
        inner,
        (even, odd),
        (left, even, odd),
        (courant_r, courant_t, courant_z),
    )
    for k, rate in enumerate(steps):
        section[k] = partial[k] + rate
    pack_sector(section, None, sector_out)
    pack_slab(section, None, even_out, odd_out)


def second_head(count, *refs):
    wanted, odd, sector, refs = refs[0], refs[1], refs[2 : 2 + count], refs[2:]
    even, partial, section, courant_r, courant_t, courant_z = refs[count : count + 6]
    left_faces, even_faces, odd_faces = refs[count + 6 : count + 9]
    evolved, outgoing, table = refs[count + 9 :]
    rows_z, cells_t, lanes = evolved.shape
    left, right, across = sector if count == 3 else sector * 3
    steps = outer_rates(
        section,
        (0, lanes),
        (left, right),
        unpack_inner(across, rows_z // 2),
        (even, odd),
        (left_faces, even_faces, odd_faces),
        (courant_r, courant_t, courant_z),
    )
    for k, rate in enumerate(steps):
        evolved[k] = partial[k, :, 0:lanes] + 0.5 * rate
    blocks_t, blocks_r = cells_t // BT, section.shape[2] // BR
    total = rows_z // BZ * blocks_t * blocks_r
    for block in range(total):
        z = block // (blocks_t * blocks_r) * BZ
        t = block // blocks_r % blocks_t * BT
        r = block % blocks_r * BR
        if r >= lanes:
            continue
        tiles = [stretched(evolved[z + i, t : t + BT, r : r + BR]) for i in range(BZ)]
        table[block] = jnp.concatenate(tiles, axis=0).astype(BF16)
    table[total] = jnp.zeros((BLOCK_ROWS, BR), BF16)
    for owner in range(outgoing.shape[0]):
        for slot in range(CAP):
            outgoing[owner, slot * BLOCK_ROWS : (slot + 1) * BLOCK_ROWS, :] = table[wanted[0, slot, owner]]


def second_tail(count, refs, evolved):
    odd, sector, refs = refs[0], refs[1 : 1 + count], refs[1:]
    even, partial, section, courant_t, courant_z, left_faces, even_faces, odd_faces = refs[count:]
    left, right, _ = sector if count == 3 else sector * 3
    low, high = section.shape[2] - evolved.shape[2], section.shape[2]
    steps = outer_rates(
        section,
        (low, high),
        (left, right),
        None,
        (even, odd),
        (left_faces, even_faces, odd_faces),
        (None, courant_t, courant_z),
    )
    for k, rate in enumerate(steps):
        evolved[k] = partial[k, :, low:high] + 0.5 * rate


def halves(x):
    high = x.astype(BF16)
    return jnp.concatenate([high, (x - high.astype(F32)).astype(BF16)], axis=0)


def prolong_patches(count, slots, head, arrived, radial_matrix, tile_matrix, *refs):
    for_tail, (evolved, patches, tail, fine, sems) = refs[: count + 9], refs[count + 9 :]
    lanes = head.shape[2]
    copies = [pltpu.make_async_copy(head, evolved.at[:, :, pl.ds(0, lanes)], sems.at[0])]
    copies[0].start()
    owned = fine.shape[0]

    def radial(group):
        blocks = []
        for p in group:
            source = lax.shift_right_logical(slots[0, p], 1)
            row = pl.multiple_of(lax.bitwise_and(slots[0, p], 1) * BLOCK_ROWS, BLOCK_ROWS)
            blocks.append(halves(unstretched(arrived[source, pl.ds(row, BLOCK_ROWS), :].astype(F32))))
        spread = jnp.dot(jnp.concatenate(blocks, axis=0), radial_matrix[...], preferred_element_type=F32)
        firsts = [2 * BLOCK_ROWS * i for i in range(len(blocks))]
        return [halves(spread[f : f + BLOCK_ROWS] + spread[f + BLOCK_ROWS : f + 2 * BLOCK_ROWS]) for f in firsts]

    groups = [range(p, min(p + GROUP, owned)) for p in range(0, owned, GROUP)]
    following = radial(groups[0])
    for g, group in enumerate(groups):
        pairs = following
        if g + 1 < len(groups):
            following = radial(groups[g + 1])
        for p, pair in zip(group, pairs):
            fine[p] = jnp.dot(tile_matrix[...], pair, preferred_element_type=F32)
        part = pl.ds(group[0], len(group))
        copies.append(pltpu.make_async_copy(fine.at[part], patches.at[part], sems.at[g + 1]))
        copies[-1].start()
        if g == min(1, len(groups) - 1):
            second_tail(count, for_tail, tail)
            copies.append(
                pltpu.make_async_copy(tail, evolved.at[:, :, pl.ds(lanes, tail.shape[2])], sems.at[len(groups) + 1])
            )
            copies[-1].start()
    for copy in copies:
        copy.wait()


def interp_matrix(coarse_count):
    matrix = np.zeros((2 * coarse_count, coarse_count), np.float32)
    for m in range(coarse_count):
        matrix[2 * m, m] += 0.75
        matrix[2 * m, max(m - 1, 0)] += 0.25
        matrix[2 * m + 1, m] += 0.75
        matrix[2 * m + 1, min(m + 1, coarse_count - 1)] += 0.25
    return matrix


def in_vmem(count):
    return [pl.BlockSpec(memory_space=pltpu.VMEM)] * count


def in_smem(count):
    return [pl.BlockSpec(memory_space=pltpu.SMEM)] * count


PARAMS = pltpu.CompilerParams(vmem_limit_bytes=VMEM_LIMIT)


def local(density, courant_r, courant_t, courant_z, ionization, send_block, recv_slot):
    rows_z, cells_t, cells_r = density.shape
    ax_count = lax.axis_size("ax")
    az_count = lax.axis_size("az")
    owned = recv_slot.shape[1]

    def flat(a, i):
        return a * ax_count + i

    even_pairs = [(i, i ^ 1) for i in range(ax_count)]
    odd_pairs = []
    for a in range(az_count):
        odd_pairs += [(flat(a, i), flat(a, ((i - 1) ^ 1) + 1)) for i in range(1, ax_count - 1)]
        odd_pairs += [(flat(a, i), flat(a ^ 1, i)) for i in (0, ax_count - 1)]

    def by(steps):
        return [(a, (a + steps) % az_count) for a in range(az_count)]

    beside = (1,) if az_count == 2 else (1, az_count - 1)
    all_steps = beside if az_count == 2 else beside + (az_count // 2,)

    def exchange(sector, even, odd, steps):
        sectors = [lax.ppermute(sector, "az", by(s)) for s in steps]
        return sectors, lax.ppermute(even, "ax", even_pairs), lax.ppermute(odd, ("az", "ax"), odd_pairs)

    lanes = HEAD_R * BR
    message = jax.ShapeDtypeStruct((rows_z // 4 + 1, cells_t, cells_r), BF16)
    second_message = jax.ShapeDtypeStruct((rows_z // 2 + 1, 8, cells_r), BF16)
    field = jax.ShapeDtypeStruct(density.shape, F32)

    given = (
        density, courant_t, courant_z, courant_r, ionization, jnp.transpose(send_block, (0, 2, 1)), recv_slot
    )
    given = tuple(pltpu.with_memory_space_constraint(x, pltpu.HBM) for x in given)
    *held, sector, even, odd = pl.pallas_call(
        functools.partial(first_messages, len(given)),
        out_shape=tuple(
            pltpu.SMEM(x.shape, x.dtype) if x.dtype == jnp.int32 else jax.ShapeDtypeStruct(x.shape, x.dtype)
            for x in given
        )
        + (message,) * 3,
        in_specs=[pl.BlockSpec(memory_space=pltpu.HBM)] * len(given),
        out_specs=tuple(in_vmem(len(given) - 2) + in_smem(2) + in_vmem(3)),
        scratch_shapes=[pltpu.SemaphoreType.DMA((len(given),))],
        compiler_params=PARAMS,
        name="first_messages",
    )(*given)
    density, courant_t, courant_z, courant_r, ionization, wanted, slots = held
    sectors, even, odd = exchange(sector, even, odd, all_steps)
    count = len(sectors)

    inner_cost = pl.CostEstimate(flops=40 * density.size, bytes_accessed=16 * density.size, transcendentals=0)
    partial = pl.pallas_call(
        first_inner,
        out_shape=field,
        in_specs=in_vmem(4),
        out_specs=in_vmem(1)[0],
        compiler_params=PARAMS,
        cost_estimate=inner_cost,
        name="first_inner",
    )(density, courant_r, courant_z, ionization)
    section, sector, even_two, odd_two = pl.pallas_call(
        functools.partial(first_stage, count),
        out_shape=(field,) + (second_message,) * 3,
        in_specs=in_vmem(7 + count),
        out_specs=tuple(in_vmem(4)),
        compiler_params=PARAMS,
        name="first_stage",
    )(odd, *sectors, even, partial, density, courant_r, courant_t, courant_z)
    sectors_two, even_two, odd_two = exchange(sector, even_two, odd_two, all_steps)

    partial = pl.pallas_call(
        second_inner,
        out_shape=field,
        in_specs=in_vmem(5),
        out_specs=in_vmem(1)[0],
        compiler_params=PARAMS,
        cost_estimate=inner_cost,
        name="second_inner",
    )(density, section, courant_r, courant_z, ionization)
    blocks = rows_z // BZ * (cells_t // BT) * (cells_r // BR)
    head, outgoing = pl.pallas_call(
        functools.partial(second_head, count),
        out_shape=(
            jax.ShapeDtypeStruct((rows_z, cells_t, lanes), F32),
            jax.ShapeDtypeStruct((ax_count, CAP * BLOCK_ROWS, BR), BF16),
        ),
        in_specs=in_smem(1) + in_vmem(10 + count),
        out_specs=tuple(in_vmem(2)),
        scratch_shapes=[pltpu.VMEM((blocks + 1, BLOCK_ROWS, BR), BF16)],
        compiler_params=PARAMS,
        name="second_head",
    )(
        wanted, odd_two, *sectors_two, even_two, partial, section, courant_r, courant_t, courant_z,
        sectors[0], even, odd,
    )

    arrived = lax.all_to_all(outgoing, "ax", split_axis=0, concat_axis=0, tiled=True)

    tile_matrix = np.kron(interp_matrix(BZ), interp_matrix(BT))
    tile_matrix = jnp.asarray(np.concatenate([tile_matrix, tile_matrix], axis=1), BF16)
    radial_matrix = jnp.asarray(interp_matrix(BR).T, BF16)
    fine_rows = 4 * BZ * BT
    evolved, patches = pl.pallas_call(
        functools.partial(prolong_patches, count),
        out_shape=(field, jax.ShapeDtypeStruct((owned, fine_rows, 2 * BR), F32)),
        in_specs=in_smem(1) + in_vmem(13 + count),
        out_specs=(pl.BlockSpec(memory_space=pltpu.HBM),) * 2,
        scratch_shapes=[
            pltpu.VMEM((rows_z, cells_t, cells_r - lanes), F32),
            pltpu.VMEM((owned, fine_rows, 2 * BR), F32),
            pltpu.SemaphoreType.DMA((-(-owned // GROUP) + 2,)),
        ],
        compiler_params=PARAMS,
        name="prolong_patches",
    )(
        slots, head, arrived, radial_matrix, tile_matrix,
        odd_two, *sectors_two, even_two, partial, section, courant_t, courant_z, sectors[0], even, odd,
    )
    return (evolved, patches.reshape(1, owned, 2 * BZ, 2 * BT, 2 * BR))


def solution(mesh):
    in_specs = (
        P("ax", "az", None),
        P("ax", "az", None),
        P("ax", "az", None),
        P("ax", "az", None),
        P("ax", "az", None),
        P("az", "ax", None),
        P("az", "ax"),
    )
    out_specs = (P("ax", "az", None), P("az", "ax", None, None, None))
    return jax.shard_map(local, mesh=mesh, in_specs=in_specs, out_specs=out_specs, check_vma=False)
```

```python
import functools

import jax
import jax.numpy as jnp
import numpy as np
from jax import lax
from jax.experimental import pallas as pl
from jax.experimental.pallas import tpu as pltpu
from jax.sharding import PartitionSpec as P

BZ = 4
BT = 8
BR = 128
CAP = 2
HEAD_R = 2
GROUP = 4
F32 = jnp.float32
BF16 = jnp.bfloat16
DIFFUSION = 0.05
VMEM_LIMIT = 24 * 1024 * 1024

BLOCK_ROWS = BZ * BT


def gathered(values, j):
    rows_z, _, cells_r = values.shape
    row = lax.broadcasted_iota(jnp.int32, (8, cells_r), 0)
    tile = jnp.zeros((8, cells_r), F32)
    for k in range(rows_z):
        part = values[k].astype(F32)[j // 8 * 8 : j // 8 * 8 + 8, :]
        tile = jnp.where(row == k, pltpu.roll(part, (k - j) % 8, 0), tile)
    return tile


def pack_sector(tiles, values, out_ref):
    rows_z, cells_t, _ = values.shape
    lane = lax.broadcasted_iota(jnp.int32, (cells_t, 128), 1)
    inner = jnp.zeros((cells_t, 128), F32)
    for k in range(rows_z):
        inner = jnp.where(lane == k, values[k, :, 0:1], inner)
    rounded = inner.astype(BF16).astype(F32)
    rest = inner - rounded
    write_tiles(out_ref, 0, tiles + [jnp.concatenate([rounded[:8], rounded[8:], rest[:8], rest[8:]], axis=1)])


def unpack_inner(msg, index):
    parts = tile_of(msg, index, (0, 512))
    parts = parts[:, 0:256] + parts[:, 256:512]
    return jnp.concatenate([parts[:, 0:128], parts[:, 128:256]], axis=0)


def write_tiles(out_ref, first, tiles):
    if out_ref.shape[1] == 8:
        for index, tile in enumerate(tiles):
            out_ref[first + index] = tile.astype(BF16)
    else:
        for index in range(0, len(tiles), 2):
            out_ref[(first + index) // 2] = jnp.concatenate(tiles[index : index + 2], axis=0).astype(BF16)


def tile_of(msg, index, lanes):
    if msg.shape[1] == 8:
        return msg[index, :, lanes[0] : lanes[1]].astype(F32)
    return msg[index // 2, :, lanes[0] : lanes[1]].astype(F32)[(index % 2) * 8 : (index % 2) * 8 + 8, :]


def row_of(msg, r, rows, lanes):
    if msg.shape[1] == 8:
        parts = rows // 8
        return jnp.concatenate([tile_of(msg, parts * r + part, lanes) for part in range(parts)], axis=0)
    return msg[r, :, lanes[0] : lanes[1]].astype(F32)


def pack_slab(values, courant_z, even_ref, odd_ref):
    rows_z, cells_t, _ = values.shape
    parity = lax.rem(lax.axis_index("ax"), 2)
    first_even = jnp.where(parity == 0, rows_z - 2, 0)
    first_odd = jnp.where(parity == 0, 0, rows_z - 2)
    parts = cells_t // 8
    for out_ref, first in ((even_ref, first_even), (odd_ref, first_odd)):
        rows = [values[first + r] for r in range(2)]
        if courant_z is not None:
            rows.append(courant_z[rows_z - 1].astype(F32))
        for r, row in enumerate(rows):
            write_tiles(out_ref, parts * r, [row[8 * part : 8 * part + 8, :] for part in range(parts)])


def first_messages(count, *refs):
    given, held = refs[:count], refs[count : 2 * count]
    edges, sector_out, even_out, odd_out, sems = refs[2 * count :]
    copies = [pltpu.make_async_copy(given[i], held[i], sems.at[i]) for i in range(count)]
    for copy in copies:
        copy.start()
    density, courant_t, courant_z = held[:3]
    for copy in copies[:3]:
        copy.wait()
    pack_slab(density, courant_z, even_out, odd_out)
    cells_t = density.shape[1]
    tiles = [gathered(density, j) for j in (0, 1, cells_t - 2, cells_t - 1)]
    for index, tile in enumerate(tiles):
        edges[index] = tile
    pack_sector(tiles + [gathered(courant_t, cells_t - 1)], density, sector_out)
    for copy in copies[3:]:
        copy.wait()


def stretched(x):
    square = x * x
    return jnp.where(x < 0.0, -square * square, square * square)


def unstretched(y):
    root = jnp.sqrt(jnp.sqrt(jnp.abs(y)))
    return jnp.where(y < 0.0, -root, root)


def axial_flux(courant, back, here, up, up_two):
    low = here + 0.25 * (up - back)
    high = up - 0.25 * (up_two - here)
    return courant * jnp.where(courant > 0.0, low, high)


def inner_rates(values, courant_r, courant_t, courant_z, ionization):
    rows_z, cells_t, cells_r = values.shape
    zero = jnp.zeros((cells_t, cells_r), F32)

    def row_at(k):
        return values[k] if 0 <= k < rows_z else zero

    lane = lax.broadcasted_iota(jnp.int32, (cells_t, cells_r), 1)
    index = lane.astype(F32)
    area = jnp.where(lane < cells_r - 1, index + 1.0, 0.0)
    inverse_radius = 1.0 / (index + 0.5)
    last_row = lax.broadcasted_iota(jnp.int32, (cells_t, cells_r), 0) == cells_t - 1
    flux_z = zero
    for k in range(rows_z):
        here, back, up = row_at(k), row_at(k - 1), row_at(k + 1)
        next_flux = zero
        if k < rows_z - 1:
            next_flux = axial_flux(courant_z[k].astype(F32), back, here, up, row_at(k + 2))
        rate = (
            DIFFUSION * (up - 2.0 * here + back)
            + ionization[k].astype(F32) * here
            - (next_flux - flux_z)
        )
        flux_z = next_flux
        courant = jnp.where(last_row, 0.0, courant_t[k].astype(F32))
        quarter = 0.25 * (pltpu.roll(here, cells_t - 1, 0) - pltpu.roll(here, 1, 0))
        flux = courant * jnp.where(
            courant > 0.0, here + quarter, pltpu.roll(here - quarter, cells_t - 1, 0)
        )
        rate = rate + (pltpu.roll(flux, 1, 0) - flux)
        inward = jnp.where(lane == 0, 0.0, pltpu.roll(here, 1, 1))
        outward = jnp.where(lane == cells_r - 1, 0.0, pltpu.roll(here, cells_r - 1, 1))
        quarter = 0.25 * (outward - inward)
        courant = courant_r[k].astype(F32)
        flux = courant * jnp.where(
            courant > 0.0, here + quarter, pltpu.roll(here - quarter, cells_r - 1, 1)
        )
        carried = area * (DIFFUSION * (outward - here) - flux)
        yield rate + (carried - pltpu.roll(carried, 1, 1)) * inverse_radius


def finish(out, partial, scale, values, edges, lanes, sector, inner, slab, faces_below, faces, courants):
    rows_z, cells_t = values.shape[:2]
    low, high = lanes
    width = high - low
    left, right = sector
    even_msg, odd_msg = slab
    left_faces, even_faces, odd_faces = faces_below
    courant_r, courant_z = courants
    me = lax.axis_index("ax")
    is_even = lax.rem(me, 2) == 0
    has_below = me > 0
    has_above = me < lax.axis_size("ax") - 1
    zero = jnp.zeros((cells_t, width), F32)

    def below(even, odd, r):
        even, odd = row_of(even, r, cells_t, lanes), row_of(odd, r, cells_t, lanes)
        return jnp.where(has_below, jnp.where(is_even, odd, even), zero)

    def above(even, odd, r):
        even, odd = row_of(even, r, cells_t, lanes), row_of(odd, r, cells_t, lanes)
        return jnp.where(has_above, jnp.where(is_even, even, odd), zero)

    def axial_courant(k):
        return courant_z[k, :, low:high].astype(F32)

    def at(k):
        return values[k, :, low:high]

    top = rows_z - 1
    below_one, below_two = below(even_msg, odd_msg, 1), below(even_msg, odd_msg, 0)
    above_one, above_two = above(even_msg, odd_msg, 0), above(even_msg, odd_msg, 1)
    below_courant = below(even_faces, odd_faces, 2)
    first_flux = axial_flux(below_courant, below_two, below_one, at(0), at(1))
    last_flux = axial_flux(axial_courant(top), at(top - 1), at(top), above_one, above_two)
    low_change = -0.25 * jnp.maximum(axial_courant(0), 0.0) * below_one
    high_change = -0.25 * jnp.minimum(axial_courant(top - 1), 0.0) * above_one
    axial = {
        0: first_flux - low_change + DIFFUSION * below_one,
        1: low_change,
        top - 1: -high_change,
        top: high_change - last_flux + DIFFUSION * above_one,
    }
    lane = lax.broadcasted_iota(jnp.int32, (cells_t, 128), 1)
    for k in range(rows_z):
        row = partial[k, :, low:high]
        if k in axial:
            row = row + scale * axial[k]
        if inner is not None:
            change = 0.25 * scale * jnp.maximum(courant_r[k, :, 0:128].astype(F32), 0.0)
            change = change * (pltpu.roll(inner, 128 - k, 1) if k else inner)
            change = jnp.where(lane == 0, change, 0.0)
            change = 2.0 * change - (1.0 / 1.5) * pltpu.roll(change, 1, 1)
            row = jnp.concatenate([row[:, 0:128] + change, row[:, 128:]], axis=1)
        out[k] = row
    first, second, last_but_one, last = [edges[index, :, low:high] for index in range(4)]
    first_face, next_face, last_face = [faces[index, :, low:high] for index in range(3)]
    before_two, before_one = tile_of(left, 2, lanes), tile_of(left, 3, lanes)
    after_one, after_two = tile_of(right, 0, lanes), tile_of(right, 1, lanes)
    low_flux = axial_flux(tile_of(left_faces, 4, lanes), before_two, before_one, first, second)
    high_flux = axial_flux(last_face, last_but_one, last, after_one, after_two)
    low_change = -0.25 * jnp.maximum(first_face, 0.0) * (before_one - last)
    high_change = -0.25 * jnp.minimum(next_face, 0.0) * (after_one - first)
    changes = {
        0: low_flux - low_change,
        1: low_change,
        cells_t - 2: -high_change,
        cells_t - 1: high_change - high_flux,
    }
    tiles = []
    for j, change in changes.items():
        tiles.append(out[:, j, :] + scale * change)
        out[:, j, :] = tiles[-1]
    return tiles


def first_inner(density, courant_r, courant_t, courant_z, ionization, partial, faces):
    for k, rate in enumerate(inner_rates(density, courant_r, courant_t, courant_z, ionization)):
        partial[k] = density[k] + rate
    cells_t = density.shape[1]
    for index, j in enumerate((0, cells_t - 2, cells_t - 1)):
        faces[index] = gathered(courant_t, j)


def second_inner(density, section, courant_r, courant_t, courant_z, ionization, partial):
    for k, rate in enumerate(inner_rates(section, courant_r, courant_t, courant_z, ionization)):
        partial[k] = 0.5 * (density[k] + section[k] + rate)


def first_stage(count, *refs):
    odd, sector, refs = refs[0], refs[1 : 1 + count], refs[1:]
    even, partial, density, edges, faces, courant_r, courant_z = refs[count : count + 7]
    section, section_edges, sector_out, even_out, odd_out = refs[count + 7 :]
    left, right, across = sector if count == 3 else sector * 3
    tiles = finish(
        section,
        partial,
        1.0,
        density,
        edges,
        (0, density.shape[2]),
        (left, right),
        unpack_inner(across, 5),
        (even, odd),
        (left, even, odd),
        faces,
        (courant_r, courant_z),
    )
    for index, tile in enumerate(tiles):
        section_edges[index] = tile
    pack_sector(tiles, section, sector_out)
    pack_slab(section, None, even_out, odd_out)


def second_head(count, *refs):
    wanted, odd, sector, refs = refs[0], refs[1], refs[2 : 2 + count], refs[2:]
    even, partial, section, edges, faces, courant_r, courant_z = refs[count : count + 7]
    left_faces, even_faces, odd_faces = refs[count + 7 : count + 10]
    evolved, outgoing, table = refs[count + 10 :]
    rows_z, cells_t, lanes = evolved.shape
    left, right, across = sector if count == 3 else sector * 3
    finish(
        evolved,
        partial,
        0.5,
        section,
        edges,
        (0, lanes),
        (left, right),
        unpack_inner(across, 4),
        (even, odd),
        (left_faces, even_faces, odd_faces),
        faces,
        (courant_r, courant_z),
    )
    blocks_t, blocks_r = cells_t // BT, section.shape[2] // BR
    total = rows_z // BZ * blocks_t * blocks_r
    for block in range(total):
        z = block // (blocks_t * blocks_r) * BZ
        t = block // blocks_r % blocks_t * BT
        r = block % blocks_r * BR
        if r >= lanes:
            continue
        tiles = [stretched(evolved[z + i, t : t + BT, r : r + BR]) for i in range(BZ)]
        table[block] = jnp.concatenate(tiles, axis=0).astype(BF16)
    table[total] = jnp.zeros((BLOCK_ROWS, BR), BF16)
    for owner in range(outgoing.shape[0]):
        for slot in range(CAP):
            outgoing[owner, slot * BLOCK_ROWS : (slot + 1) * BLOCK_ROWS, :] = table[wanted[0, slot, owner]]


def second_tail(count, refs, evolved):
    odd, sector, refs = refs[0], refs[1 : 1 + count], refs[1:]
    even, partial, section, edges, faces, courant_z, left_faces, even_faces, odd_faces = refs[count:]
    left, right, _ = sector if count == 3 else sector * 3
    finish(
        evolved,
        partial,
        0.5,
        section,
        edges,
        (section.shape[2] - evolved.shape[2], section.shape[2]),
        (left, right),
        None,
        (even, odd),
        (left_faces, even_faces, odd_faces),
        faces,
        (None, courant_z),
    )


def halves(x):
    high = x.astype(BF16)
    return jnp.concatenate([high, (x - high.astype(F32)).astype(BF16)], axis=0)


def prolong_patches(count, slots, head, arrived, radial_matrix, tile_matrix, *refs):
    for_tail, (evolved, patches, tail, fine, sems) = refs[: count + 10], refs[count + 10 :]
    lanes = head.shape[2]
    copies = [pltpu.make_async_copy(head, evolved.at[:, :, pl.ds(0, lanes)], sems.at[0])]
    copies[0].start()
    owned = fine.shape[0]

    def radial(group):
        blocks = []
        for p in group:
            source = lax.shift_right_logical(slots[0, p], 1)
            row = pl.multiple_of(lax.bitwise_and(slots[0, p], 1) * BLOCK_ROWS, BLOCK_ROWS)
            blocks.append(halves(unstretched(arrived[source, pl.ds(row, BLOCK_ROWS), :].astype(F32))))
        spread = jnp.dot(jnp.concatenate(blocks, axis=0), radial_matrix[...], preferred_element_type=F32)
        firsts = [2 * BLOCK_ROWS * i for i in range(len(blocks))]
        return [halves(spread[f : f + BLOCK_ROWS] + spread[f + BLOCK_ROWS : f + 2 * BLOCK_ROWS]) for f in firsts]

    groups = [range(p, min(p + GROUP, owned)) for p in range(0, owned, GROUP)]
    following = radial(groups[0])
    for g, group in enumerate(groups):
        pairs = following
        if g + 1 < len(groups):
            following = radial(groups[g + 1])
        for p, pair in zip(group, pairs):
            fine[p] = jnp.dot(tile_matrix[...], pair, preferred_element_type=F32)
        part = pl.ds(group[0], len(group))
        copies.append(pltpu.make_async_copy(fine.at[part], patches.at[part], sems.at[g + 1]))
        copies[-1].start()
        if g == min(1, len(groups) - 1):
            second_tail(count, for_tail, tail)
            copies.append(
                pltpu.make_async_copy(tail, evolved.at[:, :, pl.ds(lanes, tail.shape[2])], sems.at[len(groups) + 1])
            )
            copies[-1].start()
    for copy in copies:
        copy.wait()


def interp_matrix(coarse_count):
    matrix = np.zeros((2 * coarse_count, coarse_count), np.float32)
    for m in range(coarse_count):
        matrix[2 * m, m] += 0.75
        matrix[2 * m, max(m - 1, 0)] += 0.25
        matrix[2 * m + 1, m] += 0.75
        matrix[2 * m + 1, min(m + 1, coarse_count - 1)] += 0.25
    return matrix


def in_vmem(count):
    return [pl.BlockSpec(memory_space=pltpu.VMEM)] * count


def in_smem(count):
    return [pl.BlockSpec(memory_space=pltpu.SMEM)] * count


PARAMS = pltpu.CompilerParams(vmem_limit_bytes=VMEM_LIMIT)


def local(density, courant_r, courant_t, courant_z, ionization, send_block, recv_slot):
    rows_z, cells_t, cells_r = density.shape
    ax_count = lax.axis_size("ax")
    az_count = lax.axis_size("az")
    owned = recv_slot.shape[1]

    def flat(a, i):
        return a * ax_count + i

    even_pairs = [(i, i ^ 1) for i in range(ax_count)]
    odd_pairs = []
    for a in range(az_count):
        odd_pairs += [(flat(a, i), flat(a, ((i - 1) ^ 1) + 1)) for i in range(1, ax_count - 1)]
        odd_pairs += [(flat(a, i), flat(a ^ 1, i)) for i in (0, ax_count - 1)]

    def by(steps):
        return [(a, (a + steps) % az_count) for a in range(az_count)]

    beside = (1,) if az_count == 2 else (1, az_count - 1)
    all_steps = beside if az_count == 2 else beside + (az_count // 2,)

    def exchange(sector, even, odd, steps):
        sectors = [lax.ppermute(sector, "az", by(s)) for s in steps]
        return sectors, lax.ppermute(even, "ax", even_pairs), lax.ppermute(odd, ("az", "ax"), odd_pairs)

    lanes = HEAD_R * BR
    message = jax.ShapeDtypeStruct((rows_z // 4 + 1, cells_t, cells_r), BF16)
    edge_tiles = jax.ShapeDtypeStruct((4, rows_z, cells_r), F32)
    second_message = jax.ShapeDtypeStruct((rows_z // 2 + 1, 8, cells_r), BF16)
    field = jax.ShapeDtypeStruct(density.shape, F32)

    given = (
        density, courant_t, courant_z, courant_r, ionization, jnp.transpose(send_block, (0, 2, 1)), recv_slot
    )
    given = tuple(pltpu.with_memory_space_constraint(x, pltpu.HBM) for x in given)
    *held, edges, sector, even, odd = pl.pallas_call(
        functools.partial(first_messages, len(given)),
        out_shape=tuple(
            pltpu.SMEM(x.shape, x.dtype) if x.dtype == jnp.int32 else jax.ShapeDtypeStruct(x.shape, x.dtype)
            for x in given
        )
        + (edge_tiles,) + (message,) * 3,
        in_specs=[pl.BlockSpec(memory_space=pltpu.HBM)] * len(given),
        out_specs=tuple(in_vmem(len(given) - 2) + in_smem(2) + in_vmem(4)),
        scratch_shapes=[pltpu.SemaphoreType.DMA((len(given),))],
        compiler_params=PARAMS,
        name="first_messages",
    )(*given)
    density, courant_t, courant_z, courant_r, ionization, wanted, slots = held
    sectors, even, odd = exchange(sector, even, odd, all_steps)
    count = len(sectors)

    inner_cost = pl.CostEstimate(flops=40 * density.size, bytes_accessed=16 * density.size, transcendentals=0)
    partial, faces = pl.pallas_call(
        first_inner,
        out_shape=(field, jax.ShapeDtypeStruct((3, rows_z, cells_r), F32)),
        in_specs=in_vmem(5),
        out_specs=tuple(in_vmem(2)),
        compiler_params=PARAMS,
        cost_estimate=inner_cost,
        name="first_inner",
    )(density, courant_r, courant_t, courant_z, ionization)
    section, section_edges, sector, even_two, odd_two = pl.pallas_call(
        functools.partial(first_stage, count),
        out_shape=(field, edge_tiles) + (second_message,) * 3,
        in_specs=in_vmem(8 + count),
        out_specs=tuple(in_vmem(5)),
        compiler_params=PARAMS,
        name="first_stage",
    )(odd, *sectors, even, partial, density, edges, faces, courant_r, courant_z)
    sectors_two, even_two, odd_two = exchange(sector, even_two, odd_two, all_steps)

    partial = pl.pallas_call(
        second_inner,
        out_shape=field,
        in_specs=in_vmem(6),
        out_specs=in_vmem(1)[0],
        compiler_params=PARAMS,
        cost_estimate=inner_cost,
        name="second_inner",
    )(density, section, courant_r, courant_t, courant_z, ionization)
    blocks = rows_z // BZ * (cells_t // BT) * (cells_r // BR)
    head, outgoing = pl.pallas_call(
        functools.partial(second_head, count),
        out_shape=(
            jax.ShapeDtypeStruct((rows_z, cells_t, lanes), F32),
            jax.ShapeDtypeStruct((ax_count, CAP * BLOCK_ROWS, BR), BF16),
        ),
        in_specs=in_smem(1) + in_vmem(11 + count),
        out_specs=tuple(in_vmem(2)),
        scratch_shapes=[pltpu.VMEM((blocks + 1, BLOCK_ROWS, BR), BF16)],
        compiler_params=PARAMS,
        name="second_head",
    )(
        wanted, odd_two, *sectors_two, even_two, partial, section, section_edges, faces, courant_r, courant_z,
        sectors[0], even, odd,
    )

    arrived = lax.all_to_all(outgoing, "ax", split_axis=0, concat_axis=0, tiled=True)

    tile_matrix = np.kron(interp_matrix(BZ), interp_matrix(BT))
    tile_matrix = jnp.asarray(np.concatenate([tile_matrix, tile_matrix], axis=1), BF16)
    radial_matrix = jnp.asarray(interp_matrix(BR).T, BF16)
    fine_rows = 4 * BZ * BT
    evolved, patches = pl.pallas_call(
        functools.partial(prolong_patches, count),
        out_shape=(field, jax.ShapeDtypeStruct((owned, fine_rows, 2 * BR), F32)),
        in_specs=in_smem(1) + in_vmem(14 + count),
        out_specs=(pl.BlockSpec(memory_space=pltpu.HBM),) * 2,
        scratch_shapes=[
            pltpu.VMEM((rows_z, cells_t, cells_r - lanes), F32),
            pltpu.VMEM((owned, fine_rows, 2 * BR), F32),
            pltpu.SemaphoreType.DMA((-(-owned // GROUP) + 2,)),
        ],
        compiler_params=PARAMS,
        name="prolong_patches",
    )(
        slots, head, arrived, radial_matrix, tile_matrix,
        odd_two, *sectors_two, even_two, partial, section, section_edges, faces, courant_z, sectors[0], even, odd,
    )
    return (evolved, patches.reshape(1, owned, 2 * BZ, 2 * BT, 2 * BR))


def solution(mesh):
    in_specs = (
        P("ax", "az", None),
        P("ax", "az", None),
        P("ax", "az", None),
        P("ax", "az", None),
        P("ax", "az", None),
        P("az", "ax", None),
        P("az", "ax"),
    )
    out_specs = (P("ax", "az", None), P("az", "ax", None, None, None))
    return jax.shard_map(local, mesh=mesh, in_specs=in_specs, out_specs=out_specs, check_vma=False)
```

```python
import functools

import jax
import jax.numpy as jnp
import numpy as np
from jax import lax
from jax.experimental import pallas as pl
from jax.experimental.pallas import tpu as pltpu
from jax.sharding import PartitionSpec as P

BZ = 4
BT = 8
BR = 128
CAP = 2
HEAD_R = 2
GROUP = 4
F32 = jnp.float32
BF16 = jnp.bfloat16
DIFFUSION = 0.05
VMEM_LIMIT = 24 * 1024 * 1024

BLOCK_ROWS = BZ * BT


def gathered(values, j):
    rows_z, _, cells_r = values.shape
    row = lax.broadcasted_iota(jnp.int32, (8, cells_r), 0)
    tile = jnp.zeros((8, cells_r), F32)
    for k in range(rows_z):
        part = values[k].astype(F32)[j // 8 * 8 : j // 8 * 8 + 8, :]
        tile = jnp.where(row == k, pltpu.roll(part, (k - j) % 8, 0), tile)
    return tile


def pack_sector(tiles, values, out_ref):
    rows_z, cells_t, _ = values.shape
    lane = lax.broadcasted_iota(jnp.int32, (cells_t, 128), 1)
    inner = jnp.zeros((cells_t, 128), F32)
    for k in range(rows_z):
        inner = jnp.where(lane == k, values[k, :, 0:1], inner)
    rounded = inner.astype(BF16).astype(F32)
    rest = inner - rounded
    write_tiles(out_ref, 0, tiles + [jnp.concatenate([rounded[:8], rounded[8:], rest[:8], rest[8:]], axis=1)])


def unpack_inner(msg, index):
    parts = tile_of(msg, index, (0, 512))
    parts = parts[:, 0:256] + parts[:, 256:512]
    return jnp.concatenate([parts[:, 0:128], parts[:, 128:256]], axis=0)


class Either:
    def __init__(self, chosen, one, other):
        self.chosen, self.one, self.other, self.shape = chosen, one, other, one.shape

    def __getitem__(self, index):
        return jnp.where(self.chosen, self.one[index], self.other[index])


def crosses():
    me = lax.axis_index("ax")
    inside = (me > 0) & (me < lax.axis_size("ax") - 1)
    return inside & ((lax.rem(me, 4) == 3) | (lax.rem(me, 4) == 0))


def parted(count, odd, sector):
    if count == 3:
        return odd, *sector
    one = Either(crosses(), sector[0], odd)
    return Either(crosses(), odd, sector[0]), one, one, one


def write_tiles(out_ref, first, tiles):
    if out_ref.shape[1] == 8:
        for index, tile in enumerate(tiles):
            out_ref[first + index] = tile.astype(BF16)
    else:
        for index in range(0, len(tiles), 2):
            out_ref[(first + index) // 2] = jnp.concatenate(tiles[index : index + 2], axis=0).astype(BF16)


def tile_of(msg, index, lanes):
    if msg.shape[1] == 8:
        return msg[index, :, lanes[0] : lanes[1]].astype(F32)
    return msg[index // 2, :, lanes[0] : lanes[1]].astype(F32)[(index % 2) * 8 : (index % 2) * 8 + 8, :]


def row_of(msg, r, rows, lanes):
    if msg.shape[1] == 8:
        parts = rows // 8
        return jnp.concatenate([tile_of(msg, parts * r + part, lanes) for part in range(parts)], axis=0)
    return msg[r, :, lanes[0] : lanes[1]].astype(F32)


def pack_slab(values, courant_z, even_ref, odd_ref):
    rows_z, cells_t, _ = values.shape
    parity = lax.rem(lax.axis_index("ax"), 2)
    first_even = jnp.where(parity == 0, rows_z - 2, 0)
    first_odd = jnp.where(parity == 0, 0, rows_z - 2)
    parts = cells_t // 8
    for out_ref, first in ((even_ref, first_even), (odd_ref, first_odd)):
        rows = [values[first + r] for r in range(2)]
        if courant_z is not None:
            rows.append(courant_z[rows_z - 1].astype(F32))
        for r, row in enumerate(rows):
            write_tiles(out_ref, parts * r, [row[8 * part : 8 * part + 8, :] for part in range(parts)])


def pack(count, tiles, values, courant_z, sector_out, even_out, odd_out):
    def write(sector_out, odd_out):
        pack_slab(values, courant_z, even_out, odd_out)
        pack_sector(tiles, values, sector_out)

    if count == 3:
        write(sector_out, odd_out)
        return

    @pl.when(crosses())
    def _():
        write(sector_out, odd_out)

    @pl.when(jnp.logical_not(crosses()))
    def _():
        write(odd_out, sector_out)


def first_messages(sectors, count, *refs):
    given, held = refs[:count], refs[count : 2 * count]
    edges, sector_out, even_out, odd_out, sems = refs[2 * count :]
    copies = [pltpu.make_async_copy(given[i], held[i], sems.at[i]) for i in range(count)]
    for copy in copies:
        copy.start()
    density, courant_t, courant_z = held[:3]
    for copy in copies[:3]:
        copy.wait()
    cells_t = density.shape[1]
    tiles = [gathered(density, j) for j in (0, 1, cells_t - 2, cells_t - 1)]
    for index, tile in enumerate(tiles):
        edges[index] = tile
    tiles.append(gathered(courant_t, cells_t - 1))

    pack(sectors, tiles, density, courant_z, sector_out, even_out, odd_out)
    for copy in copies[3:]:
        copy.wait()


def stretched(x):
    square = x * x
    return jnp.where(x < 0.0, -square * square, square * square)


def unstretched(y):
    root = jnp.sqrt(jnp.sqrt(jnp.abs(y)))
    return jnp.where(y < 0.0, -root, root)


def axial_flux(courant, back, here, up, up_two):
    low = here + 0.25 * (up - back)
    high = up - 0.25 * (up_two - here)
    return courant * jnp.where(courant > 0.0, low, high)


def inner_rates(values, courant_r, courant_t, courant_z, ionization):
    rows_z, cells_t, cells_r = values.shape
    zero = jnp.zeros((cells_t, cells_r), F32)

    def row_at(k):
        return values[k] if 0 <= k < rows_z else zero

    lane = lax.broadcasted_iota(jnp.int32, (cells_t, cells_r), 1)
    index = lane.astype(F32)
    area = jnp.where(lane < cells_r - 1, index + 1.0, 0.0)
    inverse_radius = 1.0 / (index + 0.5)
    last_row = lax.broadcasted_iota(jnp.int32, (cells_t, cells_r), 0) == cells_t - 1
    flux_z = zero
    for k in range(rows_z):
        here, back, up = row_at(k), row_at(k - 1), row_at(k + 1)
        next_flux = zero
        if k < rows_z - 1:
            next_flux = axial_flux(courant_z[k].astype(F32), back, here, up, row_at(k + 2))
        rate = (
            DIFFUSION * (up - 2.0 * here + back)
            + ionization[k].astype(F32) * here
            - (next_flux - flux_z)
        )
        flux_z = next_flux
        courant = jnp.where(last_row, 0.0, courant_t[k].astype(F32))
        quarter = 0.25 * (pltpu.roll(here, cells_t - 1, 0) - pltpu.roll(here, 1, 0))
        flux = courant * jnp.where(
            courant > 0.0, here + quarter, pltpu.roll(here - quarter, cells_t - 1, 0)
        )
        rate = rate + (pltpu.roll(flux, 1, 0) - flux)
        inward = jnp.where(lane == 0, 0.0, pltpu.roll(here, 1, 1))
        outward = jnp.where(lane == cells_r - 1, 0.0, pltpu.roll(here, cells_r - 1, 1))
        quarter = 0.25 * (outward - inward)
        courant = courant_r[k].astype(F32)
        flux = courant * jnp.where(
            courant > 0.0, here + quarter, pltpu.roll(here - quarter, cells_r - 1, 1)
        )
        carried = area * (DIFFUSION * (outward - here) - flux)
        yield rate + (carried - pltpu.roll(carried, 1, 1)) * inverse_radius


def finish(out, partial, scale, values, edges, lanes, sector, inner, slab, faces_below, faces, courants):
    rows_z, cells_t = values.shape[:2]
    low, high = lanes
    width = high - low
    left, right = sector
    even_msg, odd_msg = slab
    left_faces, even_faces, odd_faces = faces_below
    courant_r, courant_z = courants
    me = lax.axis_index("ax")
    is_even = lax.rem(me, 2) == 0
    has_below = me > 0
    has_above = me < lax.axis_size("ax") - 1
    zero = jnp.zeros((cells_t, width), F32)

    def below(even, odd, r):
        even, odd = row_of(even, r, cells_t, lanes), row_of(odd, r, cells_t, lanes)
        return jnp.where(has_below, jnp.where(is_even, odd, even), zero)

    def above(even, odd, r):
        even, odd = row_of(even, r, cells_t, lanes), row_of(odd, r, cells_t, lanes)
        return jnp.where(has_above, jnp.where(is_even, even, odd), zero)

    def axial_courant(k):
        return courant_z[k, :, low:high].astype(F32)

    def at(k):
        return values[k, :, low:high]

    top = rows_z - 1
    below_one, below_two = below(even_msg, odd_msg, 1), below(even_msg, odd_msg, 0)
    above_one, above_two = above(even_msg, odd_msg, 0), above(even_msg, odd_msg, 1)
    below_courant = below(even_faces, odd_faces, 2)
    first_flux = axial_flux(below_courant, below_two, below_one, at(0), at(1))
    last_flux = axial_flux(axial_courant(top), at(top - 1), at(top), above_one, above_two)
    low_change = -0.25 * jnp.maximum(axial_courant(0), 0.0) * below_one
    high_change = -0.25 * jnp.minimum(axial_courant(top - 1), 0.0) * above_one
    axial = {
        0: first_flux - low_change + DIFFUSION * below_one,
        1: low_change,
        top - 1: -high_change,
        top: high_change - last_flux + DIFFUSION * above_one,
    }
    lane = lax.broadcasted_iota(jnp.int32, (cells_t, 128), 1)
    for k in range(rows_z):
        row = partial[k, :, low:high]
        if k in axial:
            row = row + scale * axial[k]
        if inner is not None:
            change = 0.25 * scale * jnp.maximum(courant_r[k, :, 0:128].astype(F32), 0.0)
            change = change * (pltpu.roll(inner, 128 - k, 1) if k else inner)
            change = jnp.where(lane == 0, change, 0.0)
            change = 2.0 * change - (1.0 / 1.5) * pltpu.roll(change, 1, 1)
            row = jnp.concatenate([row[:, 0:128] + change, row[:, 128:]], axis=1)
        out[k] = row
    first, second, last_but_one, last = [edges[index, :, low:high] for index in range(4)]
    first_face, next_face, last_face = [faces[index, :, low:high] for index in range(3)]
    before_two, before_one = tile_of(left, 2, lanes), tile_of(left, 3, lanes)
    after_one, after_two = tile_of(right, 0, lanes), tile_of(right, 1, lanes)
    low_flux = axial_flux(tile_of(left_faces, 4, lanes), before_two, before_one, first, second)
    high_flux = axial_flux(last_face, last_but_one, last, after_one, after_two)
    low_change = -0.25 * jnp.maximum(first_face, 0.0) * (before_one - last)
    high_change = -0.25 * jnp.minimum(next_face, 0.0) * (after_one - first)
    changes = {
        0: low_flux - low_change,
        1: low_change,
        cells_t - 2: -high_change,
        cells_t - 1: high_change - high_flux,
    }
    tiles = []
    for j, change in changes.items():
        tiles.append(out[:, j, :] + scale * change)
        out[:, j, :] = tiles[-1]
    return tiles


def first_inner(density, courant_r, courant_t, courant_z, ionization, partial, faces):
    for k, rate in enumerate(inner_rates(density, courant_r, courant_t, courant_z, ionization)):
        partial[k] = density[k] + rate
    cells_t = density.shape[1]
    for index, j in enumerate((0, cells_t - 2, cells_t - 1)):
        faces[index] = gathered(courant_t, j)


def second_inner(density, section, courant_r, courant_t, courant_z, ionization, partial):
    for k, rate in enumerate(inner_rates(section, courant_r, courant_t, courant_z, ionization)):
        partial[k] = 0.5 * (density[k] + section[k] + rate)


def first_stage(count, *refs):
    odd, sector, refs = refs[0], refs[1 : 1 + count], refs[1:]
    even, partial, density, edges, faces, courant_r, courant_z = refs[count : count + 7]
    section, section_edges, sector_out, even_out, odd_out = refs[count + 7 :]
    odd, left, right, across = parted(count, odd, sector)
    tiles = finish(
        section,
        partial,
        1.0,
        density,
        edges,
        (0, density.shape[2]),
        (left, right),
        unpack_inner(across, 5),
        (even, odd),
        (left, even, odd),
        faces,
        (courant_r, courant_z),
    )
    for index, tile in enumerate(tiles):
        section_edges[index] = tile
    pack(count, tiles, section, None, sector_out, even_out, odd_out)


def second_head(count, *refs):
    wanted, odd, sector, refs = refs[0], refs[1], refs[2 : 2 + count], refs[2:]
    even, partial, section, edges, faces, courant_r, courant_z = refs[count : count + 7]
    left_faces, even_faces, odd_faces = refs[count + 7 : count + 10]
    evolved, outgoing, table = refs[count + 10 :]
    rows_z, cells_t, lanes = evolved.shape
    odd, left, right, across = parted(count, odd, sector)
    odd_faces, left_faces = parted(count, odd_faces, [left_faces] * count)[:2]
    finish(
        evolved,
        partial,
        0.5,
        section,
        edges,
        (0, lanes),
        (left, right),
        unpack_inner(across, 4),
        (even, odd),
        (left_faces, even_faces, odd_faces),
        faces,
        (courant_r, courant_z),
    )
    blocks_t, blocks_r = cells_t // BT, section.shape[2] // BR
    total = rows_z // BZ * blocks_t * blocks_r
    for block in range(total):
        z = block // (blocks_t * blocks_r) * BZ
        t = block // blocks_r % blocks_t * BT
        r = block % blocks_r * BR
        if r >= lanes:
            continue
        tiles = [stretched(evolved[z + i, t : t + BT, r : r + BR]) for i in range(BZ)]
        table[block] = jnp.concatenate(tiles, axis=0).astype(BF16)
    table[total] = jnp.zeros((BLOCK_ROWS, BR), BF16)
    for owner in range(outgoing.shape[0]):
        for slot in range(CAP):
            outgoing[owner, slot * BLOCK_ROWS : (slot + 1) * BLOCK_ROWS, :] = table[wanted[0, slot, owner]]


def second_tail(count, refs, evolved):
    odd, sector, refs = refs[0], refs[1 : 1 + count], refs[1:]
    even, partial, section, edges, faces, courant_z, left_faces, even_faces, odd_faces = refs[count:]
    odd, left, right, _ = parted(count, odd, sector)
    odd_faces, left_faces = parted(count, odd_faces, [left_faces] * count)[:2]
    finish(
        evolved,
        partial,
        0.5,
        section,
        edges,
        (section.shape[2] - evolved.shape[2], section.shape[2]),
        (left, right),
        None,
        (even, odd),
        (left_faces, even_faces, odd_faces),
        faces,
        (None, courant_z),
    )


def halves(x):
    high = x.astype(BF16)
    return jnp.concatenate([high, (x - high.astype(F32)).astype(BF16)], axis=0)


def prolong_patches(count, slots, head, arrived, radial_matrix, tile_matrix, *refs):
    for_tail, (evolved, patches, tail, fine, sems) = refs[: count + 10], refs[count + 10 :]
    lanes = head.shape[2]
    copies = [pltpu.make_async_copy(head, evolved.at[:, :, pl.ds(0, lanes)], sems.at[0])]
    copies[0].start()
    owned = fine.shape[0]

    def radial(group):
        blocks = []
        for p in group:
            source = lax.shift_right_logical(slots[0, p], 1)
            row = pl.multiple_of(lax.bitwise_and(slots[0, p], 1) * BLOCK_ROWS, BLOCK_ROWS)
            blocks.append(halves(unstretched(arrived[source, pl.ds(row, BLOCK_ROWS), :].astype(F32))))
        spread = jnp.dot(jnp.concatenate(blocks, axis=0), radial_matrix[...], preferred_element_type=F32)
        firsts = [2 * BLOCK_ROWS * i for i in range(len(blocks))]
        return [halves(spread[f : f + BLOCK_ROWS] + spread[f + BLOCK_ROWS : f + 2 * BLOCK_ROWS]) for f in firsts]

    groups = [range(p, min(p + GROUP, owned)) for p in range(0, owned, GROUP)]
    following = radial(groups[0])
    for g, group in enumerate(groups):
        pairs = following
        if g + 1 < len(groups):
            following = radial(groups[g + 1])
        for p, pair in zip(group, pairs):
            fine[p] = jnp.dot(tile_matrix[...], pair, preferred_element_type=F32)
        part = pl.ds(group[0], len(group))
        copies.append(pltpu.make_async_copy(fine.at[part], patches.at[part], sems.at[g + 1]))
        copies[-1].start()
        if g == min(1, len(groups) - 1):
            second_tail(count, for_tail, tail)
            copies.append(
                pltpu.make_async_copy(tail, evolved.at[:, :, pl.ds(lanes, tail.shape[2])], sems.at[len(groups) + 1])
            )
            copies[-1].start()
    for copy in copies:
        copy.wait()


def interp_matrix(coarse_count):
    matrix = np.zeros((2 * coarse_count, coarse_count), np.float32)
    for m in range(coarse_count):
        matrix[2 * m, m] += 0.75
        matrix[2 * m, max(m - 1, 0)] += 0.25
        matrix[2 * m + 1, m] += 0.75
        matrix[2 * m + 1, min(m + 1, coarse_count - 1)] += 0.25
    return matrix


def in_vmem(count):
    return [pl.BlockSpec(memory_space=pltpu.VMEM)] * count


def in_smem(count):
    return [pl.BlockSpec(memory_space=pltpu.SMEM)] * count


PARAMS = pltpu.CompilerParams(vmem_limit_bytes=VMEM_LIMIT)


def local(density, courant_r, courant_t, courant_z, ionization, send_block, recv_slot):
    rows_z, cells_t, cells_r = density.shape
    ax_count = lax.axis_size("ax")
    az_count = lax.axis_size("az")
    owned = recv_slot.shape[1]

    def flat(a, i):
        return a * ax_count + i

    even_pairs = [(i, i ^ 1) for i in range(ax_count)]
    odd_pairs = []
    for a in range(az_count):
        odd_pairs += [(flat(a, i), flat(a, ((i - 1) ^ 1) + 1)) for i in range(1, ax_count - 1)]
        odd_pairs += [(flat(a, i), flat(a ^ 1, i)) for i in (0, ax_count - 1)]

    def by(steps):
        return [(a, (a + steps) % az_count) for a in range(az_count)]

    beside = (1,) if az_count == 2 else (1, az_count - 1)
    all_steps = beside if az_count == 2 else beside + (az_count // 2,)

    pairs_one, pairs_two = [], []
    for a in range(az_count):
        for i in range(ax_count):
            end = i in (0, ax_count - 1)
            far = i % 4 in (0, 3) and not end
            beside_me = flat(a, ((i - 1) ^ 1) + 1)
            opposite = flat(a ^ 1, i)
            pairs_one.append((flat(a, i), beside_me if far else opposite))
            pairs_two.append((flat(a, i), opposite if far or end else beside_me))

    def exchange(sector, even, odd, steps):
        if len(steps) == 1:
            sectors = [lax.ppermute(sector, ("az", "ax"), pairs_two)]
        else:
            sectors = [lax.ppermute(sector, "az", by(s)) for s in steps]
        odd = lax.ppermute(odd, ("az", "ax"), pairs_one if len(steps) == 1 else odd_pairs)
        return sectors, lax.ppermute(even, "ax", even_pairs), odd

    lanes = HEAD_R * BR
    message = jax.ShapeDtypeStruct((rows_z // 4 + 1, cells_t, cells_r), BF16)
    edge_tiles = jax.ShapeDtypeStruct((4, rows_z, cells_r), F32)
    second_message = jax.ShapeDtypeStruct((rows_z // 2 + 1, 8, cells_r), BF16)
    field = jax.ShapeDtypeStruct(density.shape, F32)

    given = (
        density, courant_t, courant_z, courant_r, ionization, jnp.transpose(send_block, (0, 2, 1)), recv_slot
    )
    given = tuple(pltpu.with_memory_space_constraint(x, pltpu.HBM) for x in given)
    *held, edges, sector, even, odd = pl.pallas_call(
        functools.partial(first_messages, len(all_steps), len(given)),
        out_shape=tuple(
            pltpu.SMEM(x.shape, x.dtype) if x.dtype == jnp.int32 else jax.ShapeDtypeStruct(x.shape, x.dtype)
            for x in given
        )
        + (edge_tiles,) + (message,) * 3,
        in_specs=[pl.BlockSpec(memory_space=pltpu.HBM)] * len(given),
        out_specs=tuple(in_vmem(len(given) - 2) + in_smem(2) + in_vmem(4)),
        scratch_shapes=[pltpu.SemaphoreType.DMA((len(given),))],
        compiler_params=PARAMS,
        name="first_messages",
    )(*given)
    density, courant_t, courant_z, courant_r, ionization, wanted, slots = held
    sectors, even, odd = exchange(sector, even, odd, all_steps)
    count = len(sectors)

    inner_cost = pl.CostEstimate(flops=40 * density.size, bytes_accessed=16 * density.size, transcendentals=0)
    partial, faces = pl.pallas_call(
        first_inner,
        out_shape=(field, jax.ShapeDtypeStruct((3, rows_z, cells_r), F32)),
        in_specs=in_vmem(5),
        out_specs=tuple(in_vmem(2)),
        compiler_params=PARAMS,
        cost_estimate=inner_cost,
        name="first_inner",
    )(density, courant_r, courant_t, courant_z, ionization)
    section, section_edges, sector, even_two, odd_two = pl.pallas_call(
        functools.partial(first_stage, count),
        out_shape=(field, edge_tiles) + (second_message,) * 3,
        in_specs=in_vmem(8 + count),
        out_specs=tuple(in_vmem(5)),
        compiler_params=PARAMS,
        name="first_stage",
    )(odd, *sectors, even, partial, density, edges, faces, courant_r, courant_z)
    sectors_two, even_two, odd_two = exchange(sector, even_two, odd_two, all_steps)

    partial = pl.pallas_call(
        second_inner,
        out_shape=field,
        in_specs=in_vmem(6),
        out_specs=in_vmem(1)[0],
        compiler_params=PARAMS,
        cost_estimate=inner_cost,
        name="second_inner",
    )(density, section, courant_r, courant_t, courant_z, ionization)
    blocks = rows_z // BZ * (cells_t // BT) * (cells_r // BR)
    head, outgoing = pl.pallas_call(
        functools.partial(second_head, count),
        out_shape=(
            jax.ShapeDtypeStruct((rows_z, cells_t, lanes), F32),
            jax.ShapeDtypeStruct((ax_count, CAP * BLOCK_ROWS, BR), BF16),
        ),
        in_specs=in_smem(1) + in_vmem(11 + count),
        out_specs=tuple(in_vmem(2)),
        scratch_shapes=[pltpu.VMEM((blocks + 1, BLOCK_ROWS, BR), BF16)],
        compiler_params=PARAMS,
        name="second_head",
    )(
        wanted, odd_two, *sectors_two, even_two, partial, section, section_edges, faces, courant_r, courant_z,
        sectors[0], even, odd,
    )

    arrived = lax.all_to_all(outgoing, "ax", split_axis=0, concat_axis=0, tiled=True)

    tile_matrix = np.kron(interp_matrix(BZ), interp_matrix(BT))
    tile_matrix = jnp.asarray(np.concatenate([tile_matrix, tile_matrix], axis=1), BF16)
    radial_matrix = jnp.asarray(interp_matrix(BR).T, BF16)
    fine_rows = 4 * BZ * BT
    evolved, patches = pl.pallas_call(
        functools.partial(prolong_patches, count),
        out_shape=(field, jax.ShapeDtypeStruct((owned, fine_rows, 2 * BR), F32)),
        in_specs=in_smem(1) + in_vmem(14 + count),
        out_specs=(pl.BlockSpec(memory_space=pltpu.HBM),) * 2,
        scratch_shapes=[
            pltpu.VMEM((rows_z, cells_t, cells_r - lanes), F32),
            pltpu.VMEM((owned, fine_rows, 2 * BR), F32),
            pltpu.SemaphoreType.DMA((-(-owned // GROUP) + 2,)),
        ],
        compiler_params=PARAMS,
        name="prolong_patches",
    )(
        slots, head, arrived, radial_matrix, tile_matrix,
        odd_two, *sectors_two, even_two, partial, section, section_edges, faces, courant_z, sectors[0], even, odd,
    )
    return (evolved, patches.reshape(1, owned, 2 * BZ, 2 * BT, 2 * BR))


def solution(mesh):
    in_specs = (
        P("ax", "az", None),
        P("ax", "az", None),
        P("ax", "az", None),
        P("ax", "az", None),
        P("ax", "az", None),
        P("az", "ax", None),
        P("az", "ax"),
    )
    out_specs = (P("ax", "az", None), P("az", "ax", None, None, None))
    return jax.shard_map(local, mesh=mesh, in_specs=in_specs, out_specs=out_specs, check_vma=False)
```

```python
import functools

import jax
import jax.numpy as jnp
import numpy as np
from jax import lax
from jax.experimental import pallas as pl
from jax.experimental.pallas import tpu as pltpu
from jax.sharding import PartitionSpec as P

BZ = 4
BT = 8
BR = 128
CAP = 2
HEAD_R = 2
GROUP = 4
F32 = jnp.float32
BF16 = jnp.bfloat16
DIFFUSION = 0.05
VMEM_LIMIT = 24 * 1024 * 1024

BLOCK_ROWS = BZ * BT


def gathered(values, j):
    rows_z, _, cells_r = values.shape
    row = lax.broadcasted_iota(jnp.int32, (8, cells_r), 0)
    tile = jnp.zeros((8, cells_r), F32)
    for k in range(rows_z):
        part = values[k].astype(F32)[j // 8 * 8 : j // 8 * 8 + 8, :]
        tile = jnp.where(row == k, pltpu.roll(part, (k - j) % 8, 0), tile)
    return tile


def pack_sector(tiles, values, out_ref):
    rows_z, cells_t, _ = values.shape
    lane = lax.broadcasted_iota(jnp.int32, (cells_t, 128), 1)
    inner = jnp.zeros((cells_t, 128), F32)
    for k in range(rows_z):
        inner = jnp.where(lane == k, values[k, :, 0:1], inner)
    rounded = inner.astype(BF16).astype(F32)
    rest = inner - rounded
    write_tiles(out_ref, 0, tiles + [jnp.concatenate([rounded[:8], rounded[8:], rest[:8], rest[8:]], axis=1)])


def unpack_inner(msg, index):
    parts = tile_of(msg, index, (0, 512))
    parts = parts[:, 0:256] + parts[:, 256:512]
    return jnp.concatenate([parts[:, 0:128], parts[:, 128:256]], axis=0)


class Either:
    def __init__(self, chosen, one, other):
        self.chosen, self.one, self.other, self.shape = chosen, one, other, one.shape

    def __getitem__(self, index):
        return jnp.where(self.chosen, self.one[index], self.other[index])


def crosses():
    me = lax.axis_index("ax")
    inside = (me > 0) & (me < lax.axis_size("ax") - 1)
    return inside & ((lax.rem(me, 4) == 3) | (lax.rem(me, 4) == 0))


def parted(count, odd, sector):
    if count == 3:
        return odd, *sector
    one = Either(crosses(), sector[0], odd)
    return Either(crosses(), odd, sector[0]), one, one, one


def write_tiles(out_ref, first, tiles):
    if out_ref.shape[1] == 8:
        for index, tile in enumerate(tiles):
            out_ref[first + index] = tile.astype(BF16)
    else:
        for index in range(0, len(tiles), 2):
            out_ref[(first + index) // 2] = jnp.concatenate(tiles[index : index + 2], axis=0).astype(BF16)


def tile_of(msg, index, lanes):
    if msg.shape[1] == 8:
        return msg[index, :, lanes[0] : lanes[1]].astype(F32)
    return msg[index // 2, :, lanes[0] : lanes[1]].astype(F32)[(index % 2) * 8 : (index % 2) * 8 + 8, :]


def row_of(msg, r, rows, lanes):
    if msg.shape[1] == 8:
        parts = rows // 8
        return jnp.concatenate([tile_of(msg, parts * r + part, lanes) for part in range(parts)], axis=0)
    return msg[r, :, lanes[0] : lanes[1]].astype(F32)


def pack_slab(values, courant_z, even_ref, odd_ref):
    rows_z, cells_t, _ = values.shape
    parity = lax.rem(lax.axis_index("ax"), 2)
    first_even = jnp.where(parity == 0, rows_z - 2, 0)
    first_odd = jnp.where(parity == 0, 0, rows_z - 2)
    parts = cells_t // 8
    for out_ref, first in ((even_ref, first_even), (odd_ref, first_odd)):
        rows = [values[first + r] for r in range(2)]
        if courant_z is not None:
            rows.append(courant_z[rows_z - 1].astype(F32))
        for r, row in enumerate(rows):
            write_tiles(out_ref, parts * r, [row[8 * part : 8 * part + 8, :] for part in range(parts)])


def pack(count, tiles, values, courant_z, sector_out, even_out, odd_out):
    def write(sector_out, odd_out):
        pack_slab(values, courant_z, even_out, odd_out)
        pack_sector(tiles, values, sector_out)

    if count == 3:
        write(sector_out, odd_out)
        return

    @pl.when(crosses())
    def _():
        write(sector_out, odd_out)

    @pl.when(jnp.logical_not(crosses()))
    def _():
        write(odd_out, sector_out)


def first_messages(sectors, count, *refs):
    given, held = refs[:count], refs[count : 2 * count]
    edges, sector_out, even_out, odd_out, sems = refs[2 * count :]
    copies = [pltpu.make_async_copy(given[i], held[i], sems.at[i]) for i in range(count)]
    for copy in copies:
        copy.start()
    density, courant_t, courant_z = held[:3]
    for copy in copies[:3]:
        copy.wait()
    cells_t = density.shape[1]
    tiles = [gathered(density, j) for j in (0, 1, cells_t - 2, cells_t - 1)]
    for index, tile in enumerate(tiles):
        edges[index] = tile
    tiles.append(gathered(courant_t, cells_t - 1))

    pack(sectors, tiles, density, courant_z, sector_out, even_out, odd_out)
    for copy in copies[3:]:
        copy.wait()


def stretched(x):
    square = x * x
    return jnp.where(x < 0.0, -square * square, square * square)


def unstretched(y):
    root = jnp.sqrt(jnp.sqrt(jnp.abs(y)))
    return jnp.where(y < 0.0, -root, root)


def axial_flux(courant, back, here, up, up_two):
    low = here + 0.25 * (up - back)
    high = up - 0.25 * (up_two - here)
    return courant * jnp.where(courant > 0.0, low, high)


def inner_rates(values, courant_r, courant_t, courant_z, ionization):
    rows_z, cells_t, cells_r = values.shape
    zero = jnp.zeros((cells_t, cells_r), F32)

    def row_at(k):
        return values[k] if 0 <= k < rows_z else zero

    lane = lax.broadcasted_iota(jnp.int32, (cells_t, cells_r), 1)
    index = lane.astype(F32)
    area = jnp.where(lane < cells_r - 1, index + 1.0, 0.0)
    inverse_radius = 1.0 / (index + 0.5)
    last_row = lax.broadcasted_iota(jnp.int32, (cells_t, cells_r), 0) == cells_t - 1
    flux_z = zero
    for k in range(rows_z):
        here, back, up = row_at(k), row_at(k - 1), row_at(k + 1)
        next_flux = zero
        if k < rows_z - 1:
            next_flux = axial_flux(courant_z[k].astype(F32), back, here, up, row_at(k + 2))
        rate = (
            DIFFUSION * (up - 2.0 * here + back)
            + ionization[k].astype(F32) * here
            - (next_flux - flux_z)
        )
        flux_z = next_flux
        courant = jnp.where(last_row, 0.0, courant_t[k].astype(F32))
        quarter = 0.25 * (pltpu.roll(here, cells_t - 1, 0) - pltpu.roll(here, 1, 0))
        flux = courant * jnp.where(
            courant > 0.0, here + quarter, pltpu.roll(here - quarter, cells_t - 1, 0)
        )
        rate = rate + (pltpu.roll(flux, 1, 0) - flux)
        inward = jnp.where(lane == 0, 0.0, pltpu.roll(here, 1, 1))
        outward = jnp.where(lane == cells_r - 1, 0.0, pltpu.roll(here, cells_r - 1, 1))
        quarter = 0.25 * (outward - inward)
        courant = courant_r[k].astype(F32)
        flux = courant * jnp.where(
            courant > 0.0, here + quarter, pltpu.roll(here - quarter, cells_r - 1, 1)
        )
        carried = area * (DIFFUSION * (outward - here) - flux)
        yield rate + (carried - pltpu.roll(carried, 1, 1)) * inverse_radius


def finish(out, partial, scale, values, edges, lanes, sector, inner, slab, faces_below, faces, courants):
    rows_z, cells_t = values.shape[:2]
    low, high = lanes
    width = high - low
    left, right = sector
    even_msg, odd_msg = slab
    left_faces, even_faces, odd_faces = faces_below
    courant_r, courant_z = courants
    me = lax.axis_index("ax")
    is_even = lax.rem(me, 2) == 0
    has_below = me > 0
    has_above = me < lax.axis_size("ax") - 1
    zero = jnp.zeros((cells_t, width), F32)

    def below(even, odd, r):
        even, odd = row_of(even, r, cells_t, lanes), row_of(odd, r, cells_t, lanes)
        return jnp.where(has_below, jnp.where(is_even, odd, even), zero)

    def above(even, odd, r):
        even, odd = row_of(even, r, cells_t, lanes), row_of(odd, r, cells_t, lanes)
        return jnp.where(has_above, jnp.where(is_even, even, odd), zero)

    def axial_courant(k):
        return courant_z[k, :, low:high].astype(F32)

    def at(k):
        return values[k, :, low:high]

    top = rows_z - 1
    below_one, below_two = below(even_msg, odd_msg, 1), below(even_msg, odd_msg, 0)
    above_one, above_two = above(even_msg, odd_msg, 0), above(even_msg, odd_msg, 1)
    below_courant = below(even_faces, odd_faces, 2)
    first_flux = axial_flux(below_courant, below_two, below_one, at(0), at(1))
    last_flux = axial_flux(axial_courant(top), at(top - 1), at(top), above_one, above_two)
    low_change = -0.25 * jnp.maximum(axial_courant(0), 0.0) * below_one
    high_change = -0.25 * jnp.minimum(axial_courant(top - 1), 0.0) * above_one
    axial = {
        0: first_flux - low_change + DIFFUSION * below_one,
        1: low_change,
        top - 1: -high_change,
        top: high_change - last_flux + DIFFUSION * above_one,
    }
    lane = lax.broadcasted_iota(jnp.int32, (cells_t, 128), 1)
    for k in range(rows_z):
        row = partial[k, :, low:high]
        if k in axial:
            row = row + scale * axial[k]
        if inner is not None:
            change = 0.25 * scale * jnp.maximum(courant_r[k, :, 0:128].astype(F32), 0.0)
            change = change * (pltpu.roll(inner, 128 - k, 1) if k else inner)
            change = jnp.where(lane == 0, change, 0.0)
            change = 2.0 * change - (1.0 / 1.5) * pltpu.roll(change, 1, 1)
            row = jnp.concatenate([row[:, 0:128] + change, row[:, 128:]], axis=1)
        out[k] = row
    first, second, last_but_one, last = [edges[index, :, low:high] for index in range(4)]
    first_face, next_face, last_face = [faces[index, :, low:high] for index in range(3)]
    before_two, before_one = tile_of(left, 2, lanes), tile_of(left, 3, lanes)
    after_one, after_two = tile_of(right, 0, lanes), tile_of(right, 1, lanes)
    low_flux = axial_flux(tile_of(left_faces, 4, lanes), before_two, before_one, first, second)
    high_flux = axial_flux(last_face, last_but_one, last, after_one, after_two)
    low_change = -0.25 * jnp.maximum(first_face, 0.0) * (before_one - last)
    high_change = -0.25 * jnp.minimum(next_face, 0.0) * (after_one - first)
    changes = {
        0: low_flux - low_change,
        1: low_change,
        cells_t - 2: -high_change,
        cells_t - 1: high_change - high_flux,
    }
    tiles = []
    for j, change in changes.items():
        tiles.append(out[:, j, :] + scale * change)
        out[:, j, :] = tiles[-1]
    return tiles


def first_inner(density, courant_r, courant_t, courant_z, ionization, partial, faces):
    for k, rate in enumerate(inner_rates(density, courant_r, courant_t, courant_z, ionization)):
        partial[k] = density[k] + rate
    cells_t = density.shape[1]
    for index, j in enumerate((0, cells_t - 2, cells_t - 1)):
        faces[index] = gathered(courant_t, j)


def second_inner(density, section, courant_r, courant_t, courant_z, ionization, partial):
    for k, rate in enumerate(inner_rates(section, courant_r, courant_t, courant_z, ionization)):
        partial[k] = 0.5 * (density[k] + section[k] + rate)


def first_stage(count, *refs):
    odd, sector, refs = refs[0], refs[1 : 1 + count], refs[1:]
    even, partial, density, edges, faces, courant_r, courant_z = refs[count : count + 7]
    section, section_edges, sector_out, even_out, odd_out = refs[count + 7 :]
    odd, left, right, across = parted(count, odd, sector)
    tiles = finish(
        section,
        partial,
        1.0,
        density,
        edges,
        (0, density.shape[2]),
        (left, right),
        unpack_inner(across, 5),
        (even, odd),
        (left, even, odd),
        faces,
        (courant_r, courant_z),
    )
    for index, tile in enumerate(tiles):
        section_edges[index] = tile
    pack(count, tiles, section, None, sector_out, even_out, odd_out)


def second_head(count, *refs):
    wanted, odd, sector, refs = refs[0], refs[1], refs[2 : 2 + count], refs[2:]
    even, partial, section, edges, faces, courant_r, courant_z = refs[count : count + 7]
    left_faces, even_faces, odd_faces = refs[count + 7 : count + 10]
    evolved, outgoing, table = refs[count + 10 :]
    rows_z, cells_t, lanes = evolved.shape
    odd, left, right, across = parted(count, odd, sector)
    odd_faces, left_faces = parted(count, odd_faces, [left_faces] * count)[:2]
    finish(
        evolved,
        partial,
        0.5,
        section,
        edges,
        (0, lanes),
        (left, right),
        unpack_inner(across, 4),
        (even, odd),
        (left_faces, even_faces, odd_faces),
        faces,
        (courant_r, courant_z),
    )
    blocks_t, blocks_r = cells_t // BT, section.shape[2] // BR
    total = rows_z // BZ * blocks_t * blocks_r
    for block in range(total):
        z = block // (blocks_t * blocks_r) * BZ
        t = block // blocks_r % blocks_t * BT
        r = block % blocks_r * BR
        if r >= lanes:
            continue
        tiles = [stretched(evolved[z + i, t : t + BT, r : r + BR]) for i in range(BZ)]
        table[block] = jnp.concatenate(tiles, axis=0).astype(BF16)
    table[total] = jnp.zeros((BLOCK_ROWS, BR), BF16)
    for owner in range(outgoing.shape[0]):
        for slot in range(CAP):
            outgoing[owner, slot * BLOCK_ROWS : (slot + 1) * BLOCK_ROWS, :] = table[wanted[0, slot, owner]]


def second_tail(count, refs, evolved):
    odd, sector, refs = refs[0], refs[1 : 1 + count], refs[1:]
    even, partial, section, edges, faces, courant_z, left_faces, even_faces, odd_faces = refs[count:]
    odd, left, right, _ = parted(count, odd, sector)
    odd_faces, left_faces = parted(count, odd_faces, [left_faces] * count)[:2]
    finish(
        evolved,
        partial,
        0.5,
        section,
        edges,
        (section.shape[2] - evolved.shape[2], section.shape[2]),
        (left, right),
        None,
        (even, odd),
        (left_faces, even_faces, odd_faces),
        faces,
        (None, courant_z),
    )


def halves(x):
    high = x.astype(BF16)
    return jnp.concatenate([high, (x - high.astype(F32)).astype(BF16)], axis=0)


def prolong_patches(count, slots, head, arrived, radial_matrix, tile_matrix, *refs):
    for_tail, (evolved, patches, tail, fine, sems) = refs[: count + 10], refs[count + 10 :]
    lanes = head.shape[2]
    copies = [pltpu.make_async_copy(head, evolved.at[:, :, pl.ds(0, lanes)], sems.at[0])]
    copies[0].start()
    owned = fine.shape[0]

    def radial(group):
        blocks = []
        for p in group:
            source = lax.shift_right_logical(slots[0, p], 1)
            row = pl.multiple_of(lax.bitwise_and(slots[0, p], 1) * BLOCK_ROWS, BLOCK_ROWS)
            blocks.append(halves(unstretched(arrived[source, pl.ds(row, BLOCK_ROWS), :].astype(F32))))
        spread = jnp.dot(jnp.concatenate(blocks, axis=0), radial_matrix[...], preferred_element_type=F32)
        firsts = [2 * BLOCK_ROWS * i for i in range(len(blocks))]
        return [halves(spread[f : f + BLOCK_ROWS] + spread[f + BLOCK_ROWS : f + 2 * BLOCK_ROWS]) for f in firsts]

    starts = [0, *range(GROUP // 2, owned, GROUP), owned]
    groups = [range(p, q) for p, q in zip(starts, starts[1:])]
    following = radial(groups[0])
    for g, group in enumerate(groups):
        pairs = following
        if g + 1 < len(groups):
            following = radial(groups[g + 1])
        for p, pair in zip(group, pairs):
            fine[p] = jnp.dot(tile_matrix[...], pair, preferred_element_type=F32)
        part = pl.ds(group[0], len(group))
        copies.append(pltpu.make_async_copy(fine.at[part], patches.at[part], sems.at[g + 1]))
        copies[-1].start()
        if g == min(1, len(groups) - 1):
            second_tail(count, for_tail, tail)
            copies.append(
                pltpu.make_async_copy(tail, evolved.at[:, :, pl.ds(lanes, tail.shape[2])], sems.at[len(groups) + 1])
            )
            copies[-1].start()
    for copy in copies:
        copy.wait()


def interp_matrix(coarse_count):
    matrix = np.zeros((2 * coarse_count, coarse_count), np.float32)
    for m in range(coarse_count):
        matrix[2 * m, m] += 0.75
        matrix[2 * m, max(m - 1, 0)] += 0.25
        matrix[2 * m + 1, m] += 0.75
        matrix[2 * m + 1, min(m + 1, coarse_count - 1)] += 0.25
    return matrix


def in_vmem(count):
    return [pl.BlockSpec(memory_space=pltpu.VMEM)] * count


def in_smem(count):
    return [pl.BlockSpec(memory_space=pltpu.SMEM)] * count


PARAMS = pltpu.CompilerParams(vmem_limit_bytes=VMEM_LIMIT)


def local(density, courant_r, courant_t, courant_z, ionization, send_block, recv_slot):
    rows_z, cells_t, cells_r = density.shape
    ax_count = lax.axis_size("ax")
    az_count = lax.axis_size("az")
    owned = recv_slot.shape[1]

    def flat(a, i):
        return a * ax_count + i

    even_pairs = [(i, i ^ 1) for i in range(ax_count)]
    odd_pairs = []
    for a in range(az_count):
        odd_pairs += [(flat(a, i), flat(a, ((i - 1) ^ 1) + 1)) for i in range(1, ax_count - 1)]
        odd_pairs += [(flat(a, i), flat(a ^ 1, i)) for i in (0, ax_count - 1)]

    def by(steps):
        return [(a, (a + steps) % az_count) for a in range(az_count)]

    beside = (1,) if az_count == 2 else (1, az_count - 1)
    all_steps = beside if az_count == 2 else beside + (az_count // 2,)

    pairs_one, pairs_two = [], []
    for a in range(az_count):
        for i in range(ax_count):
            end = i in (0, ax_count - 1)
            far = i % 4 in (0, 3) and not end
            beside_me = flat(a, ((i - 1) ^ 1) + 1)
            opposite = flat(a ^ 1, i)
            pairs_one.append((flat(a, i), beside_me if far else opposite))
            pairs_two.append((flat(a, i), opposite if far or end else beside_me))

    def exchange(sector, even, odd, steps):
        if len(steps) == 1:
            sectors = [lax.ppermute(sector, ("az", "ax"), pairs_two)]
        else:
            sectors = [lax.ppermute(sector, "az", by(s)) for s in steps]
        odd = lax.ppermute(odd, ("az", "ax"), pairs_one if len(steps) == 1 else odd_pairs)
        return sectors, lax.ppermute(even, "ax", even_pairs), odd

    lanes = HEAD_R * BR
    message = jax.ShapeDtypeStruct((rows_z // 4 + 1, cells_t, cells_r), BF16)
    edge_tiles = jax.ShapeDtypeStruct((4, rows_z, cells_r), F32)
    second_message = jax.ShapeDtypeStruct((rows_z // 2 + 1, 8, cells_r), BF16)
    field = jax.ShapeDtypeStruct(density.shape, F32)

    given = (
        density, courant_t, courant_z, courant_r, ionization, jnp.transpose(send_block, (0, 2, 1)), recv_slot
    )
    given = tuple(pltpu.with_memory_space_constraint(x, pltpu.HBM) for x in given)
    *held, edges, sector, even, odd = pl.pallas_call(
        functools.partial(first_messages, len(all_steps), len(given)),
        out_shape=tuple(
            pltpu.SMEM(x.shape, x.dtype) if x.dtype == jnp.int32 else jax.ShapeDtypeStruct(x.shape, x.dtype)
            for x in given
        )
        + (edge_tiles,) + (message,) * 3,
        in_specs=[pl.BlockSpec(memory_space=pltpu.HBM)] * len(given),
        out_specs=tuple(in_vmem(len(given) - 2) + in_smem(2) + in_vmem(4)),
        scratch_shapes=[pltpu.SemaphoreType.DMA((len(given),))],
        compiler_params=PARAMS,
        name="first_messages",
    )(*given)
    density, courant_t, courant_z, courant_r, ionization, wanted, slots = held
    sectors, even, odd = exchange(sector, even, odd, all_steps)
    count = len(sectors)

    inner_cost = pl.CostEstimate(flops=40 * density.size, bytes_accessed=16 * density.size, transcendentals=0)
    partial, faces = pl.pallas_call(
        first_inner,
        out_shape=(field, jax.ShapeDtypeStruct((3, rows_z, cells_r), F32)),
        in_specs=in_vmem(5),
        out_specs=tuple(in_vmem(2)),
        compiler_params=PARAMS,
        cost_estimate=inner_cost,
        name="first_inner",
    )(density, courant_r, courant_t, courant_z, ionization)
    section, section_edges, sector, even_two, odd_two = pl.pallas_call(
        functools.partial(first_stage, count),
        out_shape=(field, edge_tiles) + (second_message,) * 3,
        in_specs=in_vmem(8 + count),
        out_specs=tuple(in_vmem(5)),
        compiler_params=PARAMS,
        name="first_stage",
    )(odd, *sectors, even, partial, density, edges, faces, courant_r, courant_z)
    sectors_two, even_two, odd_two = exchange(sector, even_two, odd_two, all_steps)

    partial = pl.pallas_call(
        second_inner,
        out_shape=field,
        in_specs=in_vmem(6),
        out_specs=in_vmem(1)[0],
        compiler_params=PARAMS,
        cost_estimate=inner_cost,
        name="second_inner",
    )(density, section, courant_r, courant_t, courant_z, ionization)
    blocks = rows_z // BZ * (cells_t // BT) * (cells_r // BR)
    head, outgoing = pl.pallas_call(
        functools.partial(second_head, count),
        out_shape=(
            jax.ShapeDtypeStruct((rows_z, cells_t, lanes), F32),
            jax.ShapeDtypeStruct((ax_count, CAP * BLOCK_ROWS, BR), BF16),
        ),
        in_specs=in_smem(1) + in_vmem(11 + count),
        out_specs=tuple(in_vmem(2)),
        scratch_shapes=[pltpu.VMEM((blocks + 1, BLOCK_ROWS, BR), BF16)],
        compiler_params=PARAMS,
        name="second_head",
    )(
        wanted, odd_two, *sectors_two, even_two, partial, section, section_edges, faces, courant_r, courant_z,
        sectors[0], even, odd,
    )

    arrived = lax.all_to_all(outgoing, "ax", split_axis=0, concat_axis=0, tiled=True)

    tile_matrix = np.kron(interp_matrix(BZ), interp_matrix(BT))
    tile_matrix = jnp.asarray(np.concatenate([tile_matrix, tile_matrix], axis=1), BF16)
    radial_matrix = jnp.asarray(interp_matrix(BR).T, BF16)
    fine_rows = 4 * BZ * BT
    evolved, patches = pl.pallas_call(
        functools.partial(prolong_patches, count),
        out_shape=(field, jax.ShapeDtypeStruct((owned, fine_rows, 2 * BR), F32)),
        in_specs=in_smem(1) + in_vmem(14 + count),
        out_specs=(pl.BlockSpec(memory_space=pltpu.HBM),) * 2,
        scratch_shapes=[
            pltpu.VMEM((rows_z, cells_t, cells_r - lanes), F32),
            pltpu.VMEM((owned, fine_rows, 2 * BR), F32),
            pltpu.SemaphoreType.DMA((-(-owned // GROUP) + 3,)),
        ],
        compiler_params=PARAMS,
        name="prolong_patches",
    )(
        slots, head, arrived, radial_matrix, tile_matrix,
        odd_two, *sectors_two, even_two, partial, section, section_edges, faces, courant_z, sectors[0], even, odd,
    )
    return (evolved, patches.reshape(1, owned, 2 * BZ, 2 * BT, 2 * BR))


def solution(mesh):
    in_specs = (
        P("ax", "az", None),
        P("ax", "az", None),
        P("ax", "az", None),
        P("ax", "az", None),
        P("ax", "az", None),
        P("az", "ax", None),
        P("az", "ax"),
    )
    out_specs = (P("ax", "az", None), P("az", "ax", None, None, None))
    return jax.shard_map(local, mesh=mesh, in_specs=in_specs, out_specs=out_specs, check_vma=False)
```

```python
import functools

import jax
import jax.numpy as jnp
import numpy as np
from jax import lax
from jax.experimental import pallas as pl
from jax.experimental.pallas import tpu as pltpu
from jax.sharding import PartitionSpec as P

BZ = 4
BT = 8
BR = 128
CAP = 2
HEAD_R = 2
GROUP = 4
F32 = jnp.float32
BF16 = jnp.bfloat16
DIFFUSION = 0.05
VMEM_LIMIT = 24 * 1024 * 1024

BLOCK_ROWS = BZ * BT


def gathered(values, j):
    rows_z, _, cells_r = values.shape
    row = lax.broadcasted_iota(jnp.int32, (8, cells_r), 0)
    tile = jnp.zeros((8, cells_r), F32)
    for k in range(rows_z):
        part = values[k].astype(F32)[j // 8 * 8 : j // 8 * 8 + 8, :]
        tile = jnp.where(row == k, pltpu.roll(part, (k - j) % 8, 0), tile)
    return tile


def pack_sector(tiles, values, out_ref):
    rows_z, cells_t, _ = values.shape
    lane = lax.broadcasted_iota(jnp.int32, (cells_t, 128), 1)
    inner = jnp.zeros((cells_t, 128), F32)
    for k in range(rows_z):
        inner = jnp.where(lane == k, values[k, :, 0:1], inner)
    rounded = inner.astype(BF16).astype(F32)
    rest = inner - rounded
    write_tiles(out_ref, 0, tiles + [jnp.concatenate([rounded[:8], rounded[8:], rest[:8], rest[8:]], axis=1)])


def unpack_inner(msg, index):
    parts = tile_of(msg, index, (0, 512))
    parts = parts[:, 0:256] + parts[:, 256:512]
    return jnp.concatenate([parts[:, 0:128], parts[:, 128:256]], axis=0)


class Either:
    def __init__(self, chosen, one, other):
        self.chosen, self.one, self.other, self.shape = chosen, one, other, one.shape

    def __getitem__(self, index):
        return jnp.where(self.chosen, self.one[index], self.other[index])


def crosses():
    me = lax.axis_index("ax")
    inside = (me > 0) & (me < lax.axis_size("ax") - 1)
    return inside & ((lax.rem(me, 4) == 3) | (lax.rem(me, 4) == 0))


def parted(count, odd, sector):
    if count == 3:
        return odd, *sector
    one = Either(crosses(), sector[0], odd)
    return Either(crosses(), odd, sector[0]), one, one, one


def write_tiles(out_ref, first, tiles):
    if out_ref.shape[1] == 8:
        for index, tile in enumerate(tiles):
            out_ref[first + index] = tile.astype(BF16)
    else:
        for index in range(0, len(tiles), 2):
            out_ref[(first + index) // 2] = jnp.concatenate(tiles[index : index + 2], axis=0).astype(BF16)


def tile_of(msg, index, lanes):
    if msg.shape[1] == 8:
        return msg[index, :, lanes[0] : lanes[1]].astype(F32)
    return msg[index // 2, :, lanes[0] : lanes[1]].astype(F32)[(index % 2) * 8 : (index % 2) * 8 + 8, :]


def row_of(msg, r, rows, lanes):
    if msg.shape[1] == 8:
        parts = rows // 8
        return jnp.concatenate([tile_of(msg, parts * r + part, lanes) for part in range(parts)], axis=0)
    return msg[r, :, lanes[0] : lanes[1]].astype(F32)


def pack_slab(values, courant_z, even_ref, odd_ref):
    rows_z, cells_t, _ = values.shape
    parity = lax.rem(lax.axis_index("ax"), 2)
    first_even = jnp.where(parity == 0, rows_z - 2, 0)
    first_odd = jnp.where(parity == 0, 0, rows_z - 2)
    parts = cells_t // 8
    for out_ref, first in ((even_ref, first_even), (odd_ref, first_odd)):
        rows = [values[first + r] for r in range(2)]
        if courant_z is not None:
            rows.append(courant_z[rows_z - 1].astype(F32))
        for r, row in enumerate(rows):
            write_tiles(out_ref, parts * r, [row[8 * part : 8 * part + 8, :] for part in range(parts)])


def pack(count, tiles, values, courant_z, sector_out, even_out, odd_out):
    def write(sector_out, odd_out):
        pack_slab(values, courant_z, even_out, odd_out)
        pack_sector(tiles, values, sector_out)

    if count == 3:
        write(sector_out, odd_out)
        return

    @pl.when(crosses())
    def _():
        write(sector_out, odd_out)

    @pl.when(jnp.logical_not(crosses()))
    def _():
        write(odd_out, sector_out)


def first_messages(sectors, count, *refs):
    given, held = refs[:count], refs[count : 2 * count]
    edges, sector_out, even_out, odd_out, sems = refs[2 * count :]
    copies = [pltpu.make_async_copy(given[i], held[i], sems.at[i]) for i in range(count)]
    for copy in copies:
        copy.start()
    density, courant_t, courant_z = held[:3]
    for copy in copies[:3]:
        copy.wait()
    cells_t = density.shape[1]
    tiles = [gathered(density, j) for j in (0, 1, cells_t - 2, cells_t - 1)]
    for index, tile in enumerate(tiles):
        edges[index] = tile
    tiles.append(gathered(courant_t, cells_t - 1))

    pack(sectors, tiles, density, courant_z, sector_out, even_out, odd_out)
    for copy in copies[3:]:
        copy.wait()


def stretched(x):
    square = x * x
    return jnp.where(x < 0.0, -square * square, square * square)


def unstretched(y):
    root = jnp.sqrt(jnp.sqrt(jnp.abs(y)))
    return jnp.where(y < 0.0, -root, root)


def axial_flux(courant, back, here, up, up_two):
    low = here + 0.25 * (up - back)
    high = up - 0.25 * (up_two - here)
    return courant * jnp.where(courant > 0.0, low, high)


def inner_rates(values, courant_r, courant_t, courant_z, ionization):
    rows_z, cells_t, cells_r = values.shape
    zero = jnp.zeros((cells_t, cells_r), F32)

    def row_at(k):
        return values[k] if 0 <= k < rows_z else zero

    lane = lax.broadcasted_iota(jnp.int32, (cells_t, cells_r), 1)
    index = lane.astype(F32)
    area = jnp.where(lane < cells_r - 1, index + 1.0, 0.0)
    inverse_radius = 1.0 / (index + 0.5)
    last_row = lax.broadcasted_iota(jnp.int32, (cells_t, cells_r), 0) == cells_t - 1
    flux_z = zero
    for k in range(rows_z):
        here, back, up = row_at(k), row_at(k - 1), row_at(k + 1)
        next_flux = zero
        if k < rows_z - 1:
            next_flux = axial_flux(courant_z[k].astype(F32), back, here, up, row_at(k + 2))
        rate = (
            DIFFUSION * (up - 2.0 * here + back)
            + ionization[k].astype(F32) * here
            - (next_flux - flux_z)
        )
        flux_z = next_flux
        courant = jnp.where(last_row, 0.0, courant_t[k].astype(F32))
        quarter = 0.25 * (pltpu.roll(here, cells_t - 1, 0) - pltpu.roll(here, 1, 0))
        flux = courant * jnp.where(
            courant > 0.0, here + quarter, pltpu.roll(here - quarter, cells_t - 1, 0)
        )
        rate = rate + (pltpu.roll(flux, 1, 0) - flux)
        inward = jnp.where(lane == 0, 0.0, pltpu.roll(here, 1, 1))
        outward = jnp.where(lane == cells_r - 1, 0.0, pltpu.roll(here, cells_r - 1, 1))
        quarter = 0.25 * (outward - inward)
        courant = courant_r[k].astype(F32)
        flux = courant * jnp.where(
            courant > 0.0, here + quarter, pltpu.roll(here - quarter, cells_r - 1, 1)
        )
        carried = area * (DIFFUSION * (outward - here) - flux)
        yield rate + (carried - pltpu.roll(carried, 1, 1)) * inverse_radius


def finish(out, partial, scale, values, edges, lanes, sector, inner, slab, faces_below, faces, courants):
    rows_z, cells_t = values.shape[:2]
    low, high = lanes
    width = high - low
    left, right = sector
    even_msg, odd_msg = slab
    left_faces, even_faces, odd_faces = faces_below
    courant_r, courant_z = courants
    me = lax.axis_index("ax")
    is_even = lax.rem(me, 2) == 0
    has_below = me > 0
    has_above = me < lax.axis_size("ax") - 1
    zero = jnp.zeros((cells_t, width), F32)

    def below(even, odd, r):
        even, odd = row_of(even, r, cells_t, lanes), row_of(odd, r, cells_t, lanes)
        return jnp.where(has_below, jnp.where(is_even, odd, even), zero)

    def above(even, odd, r):
        even, odd = row_of(even, r, cells_t, lanes), row_of(odd, r, cells_t, lanes)
        return jnp.where(has_above, jnp.where(is_even, even, odd), zero)

    def axial_courant(k):
        return courant_z[k, :, low:high].astype(F32)

    def at(k):
        return values[k, :, low:high]

    top = rows_z - 1
    below_one, below_two = below(even_msg, odd_msg, 1), below(even_msg, odd_msg, 0)
    above_one, above_two = above(even_msg, odd_msg, 0), above(even_msg, odd_msg, 1)
    below_courant = below(even_faces, odd_faces, 2)
    first_flux = axial_flux(below_courant, below_two, below_one, at(0), at(1))
    last_flux = axial_flux(axial_courant(top), at(top - 1), at(top), above_one, above_two)
    low_change = -0.25 * jnp.maximum(axial_courant(0), 0.0) * below_one
    high_change = -0.25 * jnp.minimum(axial_courant(top - 1), 0.0) * above_one
    axial = {
        0: first_flux - low_change + DIFFUSION * below_one,
        1: low_change,
        top - 1: -high_change,
        top: high_change - last_flux + DIFFUSION * above_one,
    }
    lane = lax.broadcasted_iota(jnp.int32, (cells_t, 128), 1)
    for k in range(rows_z):
        row = partial[k, :, low:high]
        if k in axial:
            row = row + scale * axial[k]
        if inner is not None:
            change = 0.25 * scale * jnp.maximum(courant_r[k, :, 0:128].astype(F32), 0.0)
            change = change * (pltpu.roll(inner, 128 - k, 1) if k else inner)
            change = jnp.where(lane == 0, change, 0.0)
            change = 2.0 * change - (1.0 / 1.5) * pltpu.roll(change, 1, 1)
            row = jnp.concatenate([row[:, 0:128] + change, row[:, 128:]], axis=1)
        out[k] = row
    first, second, last_but_one, last = [edges[index, :, low:high] for index in range(4)]
    first_face, next_face, last_face = [faces[index, :, low:high] for index in range(3)]
    before_two, before_one = tile_of(left, 2, lanes), tile_of(left, 3, lanes)
    after_one, after_two = tile_of(right, 0, lanes), tile_of(right, 1, lanes)
    low_flux = axial_flux(tile_of(left_faces, 4, lanes), before_two, before_one, first, second)
    high_flux = axial_flux(last_face, last_but_one, last, after_one, after_two)
    low_change = -0.25 * jnp.maximum(first_face, 0.0) * (before_one - last)
    high_change = -0.25 * jnp.minimum(next_face, 0.0) * (after_one - first)
    changes = {
        0: low_flux - low_change,
        1: low_change,
        cells_t - 2: -high_change,
        cells_t - 1: high_change - high_flux,
    }
    tiles = []
    for j, change in changes.items():
        tiles.append(out[:, j, :] + scale * change)
        out[:, j, :] = tiles[-1]
    return tiles


def first_inner(density, courant_r, courant_t, courant_z, ionization, partial, faces):
    for k, rate in enumerate(inner_rates(density, courant_r, courant_t, courant_z, ionization)):
        partial[k] = density[k] + rate
    cells_t = density.shape[1]
    for index, j in enumerate((0, cells_t - 2, cells_t - 1)):
        faces[index] = gathered(courant_t, j)


def second_inner(density, section, courant_r, courant_t, courant_z, ionization, partial):
    for k, rate in enumerate(inner_rates(section, courant_r, courant_t, courant_z, ionization)):
        partial[k] = 0.5 * (density[k] + section[k] + rate)


def first_stage(count, *refs):
    odd, sector, refs = refs[0], refs[1 : 1 + count], refs[1:]
    even, partial, density, edges, faces, courant_r, courant_z = refs[count : count + 7]
    section, section_edges, sector_out, even_out, odd_out = refs[count + 7 :]
    odd, left, right, across = parted(count, odd, sector)
    tiles = finish(
        section,
        partial,
        1.0,
        density,
        edges,
        (0, density.shape[2]),
        (left, right),
        unpack_inner(across, 5),
        (even, odd),
        (left, even, odd),
        faces,
        (courant_r, courant_z),
    )
    for index, tile in enumerate(tiles):
        section_edges[index] = tile
    pack(count, tiles, section, None, sector_out, even_out, odd_out)


def second_head(count, *refs):
    wanted, odd, sector, refs = refs[0], refs[1], refs[2 : 2 + count], refs[2:]
    even, partial, section, edges, faces, courant_r, courant_z = refs[count : count + 7]
    left_faces, even_faces, odd_faces = refs[count + 7 : count + 10]
    evolved, outgoing, table = refs[count + 10 :]
    rows_z, cells_t, lanes = evolved.shape
    odd, left, right, across = parted(count, odd, sector)
    odd_faces, left_faces = parted(count, odd_faces, [left_faces] * count)[:2]
    finish(
        evolved,
        partial,
        0.5,
        section,
        edges,
        (0, lanes),
        (left, right),
        unpack_inner(across, 4),
        (even, odd),
        (left_faces, even_faces, odd_faces),
        faces,
        (courant_r, courant_z),
    )
    blocks_t, blocks_r = cells_t // BT, section.shape[2] // BR
    total = rows_z // BZ * blocks_t * blocks_r
    for block in range(total):
        z = block // (blocks_t * blocks_r) * BZ
        t = block // blocks_r % blocks_t * BT
        r = block % blocks_r * BR
        if r >= lanes:
            continue
        tiles = [stretched(evolved[z + i, t : t + BT, r : r + BR]) for i in range(BZ)]
        table[block] = jnp.concatenate(tiles, axis=0).astype(BF16)
    table[total] = jnp.zeros((BLOCK_ROWS, BR), BF16)
    for owner in range(outgoing.shape[0]):
        for slot in range(CAP):
            outgoing[owner, slot * BLOCK_ROWS : (slot + 1) * BLOCK_ROWS, :] = table[wanted[0, slot, owner]]


def second_tail(count, refs, evolved):
    odd, sector, refs = refs[0], refs[1 : 1 + count], refs[1:]
    even, partial, section, edges, faces, courant_z, left_faces, even_faces, odd_faces = refs[count:]
    odd, left, right, _ = parted(count, odd, sector)
    odd_faces, left_faces = parted(count, odd_faces, [left_faces] * count)[:2]
    finish(
        evolved,
        partial,
        0.5,
        section,
        edges,
        (section.shape[2] - evolved.shape[2], section.shape[2]),
        (left, right),
        None,
        (even, odd),
        (left_faces, even_faces, odd_faces),
        faces,
        (None, courant_z),
    )


def halves(x):
    high = x.astype(BF16)
    return jnp.concatenate([high, (x - high.astype(F32)).astype(BF16)], axis=0)


def prolong_patches(count, slots, head, arrived, radial_matrix, tile_matrix, *refs):
    for_tail, (evolved, patches, tail, fine, sems) = refs[: count + 10], refs[count + 10 :]
    lanes = head.shape[2]
    copies = [pltpu.make_async_copy(head, evolved.at[:, :, pl.ds(0, lanes)], sems.at[0])]
    copies[0].start()
    owned = fine.shape[0]

    def radial(group):
        blocks = []
        for p in group:
            source = lax.shift_right_logical(slots[0, p], 1)
            row = pl.multiple_of(lax.bitwise_and(slots[0, p], 1) * BLOCK_ROWS, BLOCK_ROWS)
            blocks.append(halves(unstretched(arrived[source, pl.ds(row, BLOCK_ROWS), :].astype(F32))))
        spread = jnp.dot(jnp.concatenate(blocks, axis=0), radial_matrix[...], preferred_element_type=F32)
        firsts = [2 * BLOCK_ROWS * i for i in range(len(blocks))]
        return [halves(spread[f : f + BLOCK_ROWS] + spread[f + BLOCK_ROWS : f + 2 * BLOCK_ROWS]) for f in firsts]

    starts = [0, 1, *range(GROUP, owned, GROUP), owned]
    groups = [range(p, q) for p, q in zip(starts, starts[1:])]
    following = radial(groups[0])
    for g, group in enumerate(groups):
        pairs = following
        if g + 1 < len(groups):
            following = radial(groups[g + 1])
        for p, pair in zip(group, pairs):
            fine[p] = jnp.dot(tile_matrix[...], pair, preferred_element_type=F32)
        part = pl.ds(group[0], len(group))
        copies.append(pltpu.make_async_copy(fine.at[part], patches.at[part], sems.at[g + 1]))
        copies[-1].start()
        if g == min(1, len(groups) - 1):
            second_tail(count, for_tail, tail)
            copies.append(
                pltpu.make_async_copy(tail, evolved.at[:, :, pl.ds(lanes, tail.shape[2])], sems.at[len(groups) + 1])
            )
            copies[-1].start()
    for copy in copies:
        copy.wait()


def interp_matrix(coarse_count):
    matrix = np.zeros((2 * coarse_count, coarse_count), np.float32)
    for m in range(coarse_count):
        matrix[2 * m, m] += 0.75
        matrix[2 * m, max(m - 1, 0)] += 0.25
        matrix[2 * m + 1, m] += 0.75
        matrix[2 * m + 1, min(m + 1, coarse_count - 1)] += 0.25
    return matrix


def in_vmem(count):
    return [pl.BlockSpec(memory_space=pltpu.VMEM)] * count


def in_smem(count):
    return [pl.BlockSpec(memory_space=pltpu.SMEM)] * count


PARAMS = pltpu.CompilerParams(vmem_limit_bytes=VMEM_LIMIT)


def local(density, courant_r, courant_t, courant_z, ionization, send_block, recv_slot):
    rows_z, cells_t, cells_r = density.shape
    ax_count = lax.axis_size("ax")
    az_count = lax.axis_size("az")
    owned = recv_slot.shape[1]

    def flat(a, i):
        return a * ax_count + i

    even_pairs = [(i, i ^ 1) for i in range(ax_count)]
    odd_pairs = []
    for a in range(az_count):
        odd_pairs += [(flat(a, i), flat(a, ((i - 1) ^ 1) + 1)) for i in range(1, ax_count - 1)]
        odd_pairs += [(flat(a, i), flat(a ^ 1, i)) for i in (0, ax_count - 1)]

    def by(steps):
        return [(a, (a + steps) % az_count) for a in range(az_count)]

    beside = (1,) if az_count == 2 else (1, az_count - 1)
    all_steps = beside if az_count == 2 else beside + (az_count // 2,)

    pairs_one, pairs_two = [], []
    for a in range(az_count):
        for i in range(ax_count):
            end = i in (0, ax_count - 1)
            far = i % 4 in (0, 3) and not end
            beside_me = flat(a, ((i - 1) ^ 1) + 1)
            opposite = flat(a ^ 1, i)
            pairs_one.append((flat(a, i), beside_me if far else opposite))
            pairs_two.append((flat(a, i), opposite if far or end else beside_me))

    def exchange(sector, even, odd, steps):
        if len(steps) == 1:
            sectors = [lax.ppermute(sector, ("az", "ax"), pairs_two)]
        else:
            sectors = [lax.ppermute(sector, "az", by(s)) for s in steps]
        odd = lax.ppermute(odd, ("az", "ax"), pairs_one if len(steps) == 1 else odd_pairs)
        return sectors, lax.ppermute(even, "ax", even_pairs), odd

    lanes = HEAD_R * BR
    message = jax.ShapeDtypeStruct((rows_z // 4 + 1, cells_t, cells_r), BF16)
    edge_tiles = jax.ShapeDtypeStruct((4, rows_z, cells_r), F32)
    second_message = jax.ShapeDtypeStruct((rows_z // 2 + 1, 8, cells_r), BF16)
    field = jax.ShapeDtypeStruct(density.shape, F32)

    given = (
        density, courant_t, courant_z, courant_r, ionization, jnp.transpose(send_block, (0, 2, 1)), recv_slot
    )
    given = tuple(pltpu.with_memory_space_constraint(x, pltpu.HBM) for x in given)
    *held, edges, sector, even, odd = pl.pallas_call(
        functools.partial(first_messages, len(all_steps), len(given)),
        out_shape=tuple(
            pltpu.SMEM(x.shape, x.dtype) if x.dtype == jnp.int32 else jax.ShapeDtypeStruct(x.shape, x.dtype)
            for x in given
        )
        + (edge_tiles,) + (message,) * 3,
        in_specs=[pl.BlockSpec(memory_space=pltpu.HBM)] * len(given),
        out_specs=tuple(in_vmem(len(given) - 2) + in_smem(2) + in_vmem(4)),
        scratch_shapes=[pltpu.SemaphoreType.DMA((len(given),))],
        compiler_params=PARAMS,
        name="first_messages",
    )(*given)
    density, courant_t, courant_z, courant_r, ionization, wanted, slots = held
    sectors, even, odd = exchange(sector, even, odd, all_steps)
    count = len(sectors)

    inner_cost = pl.CostEstimate(flops=40 * density.size, bytes_accessed=16 * density.size, transcendentals=0)
    partial, faces = pl.pallas_call(
        first_inner,
        out_shape=(field, jax.ShapeDtypeStruct((3, rows_z, cells_r), F32)),
        in_specs=in_vmem(5),
        out_specs=tuple(in_vmem(2)),
        compiler_params=PARAMS,
        cost_estimate=inner_cost,
        name="first_inner",
    )(density, courant_r, courant_t, courant_z, ionization)
    section, section_edges, sector, even_two, odd_two = pl.pallas_call(
        functools.partial(first_stage, count),
        out_shape=(field, edge_tiles) + (second_message,) * 3,
        in_specs=in_vmem(8 + count),
        out_specs=tuple(in_vmem(5)),
        compiler_params=PARAMS,
        name="first_stage",
    )(odd, *sectors, even, partial, density, edges, faces, courant_r, courant_z)
    sectors_two, even_two, odd_two = exchange(sector, even_two, odd_two, all_steps)

    partial = pl.pallas_call(
        second_inner,
        out_shape=field,
        in_specs=in_vmem(6),
        out_specs=in_vmem(1)[0],
        compiler_params=PARAMS,
        cost_estimate=inner_cost,
        name="second_inner",
    )(density, section, courant_r, courant_t, courant_z, ionization)
    blocks = rows_z // BZ * (cells_t // BT) * (cells_r // BR)
    head, outgoing = pl.pallas_call(
        functools.partial(second_head, count),
        out_shape=(
            jax.ShapeDtypeStruct((rows_z, cells_t, lanes), F32),
            jax.ShapeDtypeStruct((ax_count, CAP * BLOCK_ROWS, BR), BF16),
        ),
        in_specs=in_smem(1) + in_vmem(11 + count),
        out_specs=tuple(in_vmem(2)),
        scratch_shapes=[pltpu.VMEM((blocks + 1, BLOCK_ROWS, BR), BF16)],
        compiler_params=PARAMS,
        name="second_head",
    )(
        wanted, odd_two, *sectors_two, even_two, partial, section, section_edges, faces, courant_r, courant_z,
        sectors[0], even, odd,
    )

    arrived = lax.all_to_all(outgoing, "ax", split_axis=0, concat_axis=0, tiled=True)

    tile_matrix = np.kron(interp_matrix(BZ), interp_matrix(BT))
    tile_matrix = jnp.asarray(np.concatenate([tile_matrix, tile_matrix], axis=1), BF16)
    radial_matrix = jnp.asarray(interp_matrix(BR).T, BF16)
    fine_rows = 4 * BZ * BT
    evolved, patches = pl.pallas_call(
        functools.partial(prolong_patches, count),
        out_shape=(field, jax.ShapeDtypeStruct((owned, fine_rows, 2 * BR), F32)),
        in_specs=in_smem(1) + in_vmem(14 + count),
        out_specs=(pl.BlockSpec(memory_space=pltpu.HBM),) * 2,
        scratch_shapes=[
            pltpu.VMEM((rows_z, cells_t, cells_r - lanes), F32),
            pltpu.VMEM((owned, fine_rows, 2 * BR), F32),
            pltpu.SemaphoreType.DMA((-(-owned // GROUP) + 3,)),
        ],
        compiler_params=PARAMS,
        name="prolong_patches",
    )(
        slots, head, arrived, radial_matrix, tile_matrix,
        odd_two, *sectors_two, even_two, partial, section, section_edges, faces, courant_z, sectors[0], even, odd,
    )
    return (evolved, patches.reshape(1, owned, 2 * BZ, 2 * BT, 2 * BR))


def solution(mesh):
    in_specs = (
        P("ax", "az", None),
        P("ax", "az", None),
        P("ax", "az", None),
        P("ax", "az", None),
        P("ax", "az", None),
        P("az", "ax", None),
        P("az", "ax"),
    )
    out_specs = (P("ax", "az", None), P("az", "ax", None, None, None))
    return jax.shard_map(local, mesh=mesh, in_specs=in_specs, out_specs=out_specs, check_vma=False)
```
